32 devices in a mesh: fsdp: 4 (over z), sp: 8 (over y, x, core).
Axes of the slice: x: 2, y: 2, z: 4, core: 2. Of those that a mesh axis runs over, the one named last changes fastest.
Arguments:
- tokens: bfloat16 [4, 4096, 2048], P('fsdp', 'sp'), may hold values from -6 to 6
- cotangent: bfloat16 [4, 4096, 2048], P('fsdp', 'sp'), may hold values from -6 to 6
- first_gain: bfloat16 [2048], P(('fsdp', 'sp')), may hold values from 0.5 to 1.5
- first_shift: bfloat16 [2048], P(('fsdp', 'sp')), may hold values from -1.1953125 to 1.1953125
- joint_weight: bfloat16 [2048, 6144], P(('fsdp', 'sp')), may hold values from -0.125 to 0.125
- joint_bias: bfloat16 [6144], P(('fsdp', 'sp')), may hold values from -0.29882812 to 0.29882812
- out_weight: bfloat16 [2048, 2048], P(('fsdp', 'sp')), may hold values from -1 to 1
- second_gain: bfloat16 [2048], P(('fsdp', 'sp')), may hold values from 0.5 to 1.5
- second_shift: bfloat16 [2048], P(('fsdp', 'sp')), may hold values from -1.1953125 to 1.1953125
- gate_weight: bfloat16 [2048, 5632], P(('fsdp', 'sp')), may hold values from -0.125 to 0.125
- up_weight: bfloat16 [2048, 5632], P(('fsdp', 'sp')), may hold values from -0.125 to 0.125
- down_weight: bfloat16 [5632, 2048], P(('fsdp', 'sp')), may hold values from -0.15625 to 0.15625
Outputs:
- output: bfloat16 [4, 4096, 2048], P('fsdp', 'sp')
- tokens_grad: float32 [4, 4096, 2048], P('fsdp', 'sp')
- first_gain_grad: float32 [2048], P(('fsdp', 'sp'))
- first_shift_grad: float32 [2048], P(('fsdp', 'sp'))
- joint_weight_grad: float32 [2048, 6144], P(('fsdp', 'sp'))
- joint_bias_grad: float32 [6144], P(('fsdp', 'sp'))
- out_weight_grad: float32 [2048, 2048], P(('fsdp', 'sp'))
- second_gain_grad: float32 [2048], P(('fsdp', 'sp'))
- second_shift_grad: float32 [2048], P(('fsdp', 'sp'))
- gate_weight_grad: float32 [2048, 5632], P(('fsdp', 'sp'))
- up_weight_grad: float32 [2048, 5632], P(('fsdp', 'sp'))
- down_weight_grad: float32 [5632, 2048], P(('fsdp', 'sp'))
The draws below stay inside these ranges and needn't reach their ends.
All inputs are finite; a program needn't handle non-finite values.
Results may differ from the reference program's by a relative error of at most 0.013.
Values may be sent and summed in bfloat16 or wider, within the bound.
No kernel may reach another device: no remote copies, remote signals or barrier semaphores. Data moves between devices by JAX's collectives and lax.ppermute only.
A program may use at most 448 MiB of HBM per device.

```python
import math
import jax
import jax.numpy as jnp
from jax import lax

D = 2048
HEADS = 32
HEAD = 64
ROT = 16
FF = 5632
LENGTH = 4096
SEQS = 4


def steps_of(stream_key, shape, pieces, least, high):
    factor_of = 1.0
    for axis_at, shards_of in pieces:
        draws = jax.random.uniform(jax.random.fold_in(jax.random.fold_in(stream_key, 6), axis_at), (shards_of,), jnp.float32, least / len(pieces), high / len(pieces))
        factor_of = factor_of * jnp.repeat(jnp.exp(draws), shape[axis_at] // shards_of).reshape((-1,) + (1,) * (len(shape) - 1 - axis_at))
    return factor_of


def gaussian(stream_key, shape, scale, bound, pieces=(), kind=jnp.bfloat16):
    factor_of = steps_of(stream_key, shape, pieces, -0.22, 0.18) if pieces else 1.0
    entries = jax.random.normal(stream_key, shape, jnp.float32) * scale * factor_of
    return jnp.minimum(jnp.maximum(entries, -bound), bound).astype(kind)


def setup_inputs(seed: int = 0) -> dict:
    key_list = jax.random.split(jax.random.key(seed), 13)
    tokens = gaussian(key_list[0], (SEQS, LENGTH, D), 1.0, 6.0, ((0, 4), (1, 8)))
    cotangent = gaussian(key_list[1], (SEQS, LENGTH, D), 1.0, 6.0, ((0, 4), (1, 8)))
    first_gain = jnp.clip(1.0 + 0.1 * jax.random.normal(key_list[2], (D,), jnp.float32), 0.5, 1.5).astype(jnp.bfloat16)
    first_shift = gaussian(key_list[3], (D,), 0.2, 1.1953125, ((0, 32),))
    joint_weight = gaussian(key_list[4], (D, 3 * D), D ** -0.5, 0.125, ((0, 32),))
    joint_bias = gaussian(key_list[5], (3 * D,), 0.05, 0.29882812, ((0, 32),))
    out_weight = gaussian(key_list[6], (D, D), (D // 64) ** -0.5, 1.0, ((0, 32),))
    second_gain = jnp.clip(1.0 + 0.1 * jax.random.normal(key_list[7], (D,), jnp.float32), 0.5, 1.5).astype(jnp.bfloat16)
    second_shift = gaussian(key_list[8], (D,), 0.2, 1.1953125, ((0, 32),))
    gate_weight = gaussian(key_list[9], (D, FF), D ** -0.5, 0.125, ((0, 32),))
    up_weight = gaussian(key_list[10], (D, FF), D ** -0.5, 0.125, ((0, 32),))
    down_weight = gaussian(key_list[11], (FF, D), (FF // 4) ** -0.5, 0.15625, ((0, 32),))
    return {"tokens": tokens, "cotangent": cotangent, "first_gain": first_gain, "first_shift": first_shift, "joint_weight": joint_weight, "joint_bias": joint_bias, "out_weight": out_weight, "second_gain": second_gain, "second_shift": second_shift, "gate_weight": gate_weight, "up_weight": up_weight, "down_weight": down_weight}


@jax.custom_vjp
def low(v):
    return lax.optimization_barrier(v.astype(jnp.bfloat16)).astype(jnp.float32)

@jax.custom_vjp
def low_back(v):
    return v

def low_keep(v):
    return (low(v), None)

def low_pass(kept, grad):
    return (grad,)

def back_keep(v):
    return (v, None)

def back_low(kept, grad):
    return (low(grad),)
low.defvjp(low_keep, low_pass)
low_back.defvjp(back_keep, back_low)
epsilon = 1e-05
masked_value = -1e+30
highest = lax.Precision.HIGHEST

def layer_norm(values, gain_vec, shift_vec):
    center = values - lax.optimization_barrier(jnp.mean(values, axis=-1, keepdims=True))
    spread = lax.optimization_barrier(jnp.mean(center * center, axis=-1, keepdims=True))
    return center * lax.rsqrt(spread + epsilon) * gain_vec + shift_vec

def rotary_tables(positions):
    indices = jnp.arange(ROT // 2, dtype=jnp.float32)
    inverse = 1.0 / 10000.0 ** (indices * 2.0 / ROT)
    angles = positions[:, None] * inverse[None, :]
    angles = jnp.concatenate([angles, angles], axis=-1)
    return (jnp.cos(angles), jnp.sin(angles))

def rotate(vectors, cosine, sine_table):
    turned = vectors[..., :ROT]
    first_half = turned[..., :ROT // 2]
    second_half = turned[..., ROT // 2:]
    flipped = jnp.concatenate([-second_half, first_half], axis=-1)
    rotated = turned * cosine[:, None, :] + flipped * sine_table[:, None, :]
    return jnp.concatenate([rotated, vectors[..., ROT:]], axis=-1)

def softmax_rows(scores):
    largest = lax.optimization_barrier(jnp.max(scores, axis=-1, keepdims=True))
    raised = jnp.exp(scores - largest)
    return raised / lax.optimization_barrier(jnp.sum(raised, axis=-1, keepdims=True))

def attend_block(first_row, queries, all_keys, values):
    block_rows = queries.shape[1]
    length = all_keys.shape[1]
    scores = jnp.einsum('gqhe,gkhe->ghqk', queries, all_keys, precision=highest) * HEAD ** (-0.5)
    scores = low_back(scores)
    row_ids = first_row + jnp.arange(block_rows, dtype=jnp.int32)
    col_ids = jnp.arange(length, dtype=jnp.int32)
    allowed = col_ids[None, :] <= row_ids[:, None]
    scores = jnp.where(allowed, scores, masked_value)
    attn_probs = low(softmax_rows(scores))
    return jnp.einsum('ghqk,gkhe->gqhe', attn_probs, values, precision=highest)

def attention(queries, all_keys, values):
    groups, length = (queries.shape[0], queries.shape[1])
    block_rows = min(512, length)
    block_count = length // block_rows
    blocks = jnp.moveaxis(queries.reshape(groups, block_count, block_rows, HEADS, HEAD), 1, 0)
    starts = jnp.arange(block_count, dtype=jnp.int32) * block_rows
    checked = jax.checkpoint(attend_block)

    def one_block(entry):
        return checked(entry[0], entry[1], all_keys, values)
    results = lax.map(one_block, (starts, blocks))
    return jnp.moveaxis(results, 0, 1).reshape(groups, length, HEADS, HEAD)

def forward(params, inputs):
    gain_one, shift_one, joint_full, joint_bias_full, out_full, gain_two, shift_two, gate_full, up_full, down_full = params
    groups, length = (inputs.shape[0], inputs.shape[1])
    normed = low(layer_norm(inputs, gain_one, shift_one))
    projected = jnp.einsum('gld,de->gle', normed, joint_full, precision=highest) + joint_bias_full
    projected = low_back(projected).reshape(groups, length, 3, HEADS, HEAD)
    cosine, sine_table = rotary_tables(jnp.arange(length, dtype=jnp.float32))
    queries = low_back(low(rotate(projected[:, :, 0], cosine, sine_table)))
    all_keys = low_back(low(rotate(projected[:, :, 1], cosine, sine_table)))
    values = low_back(low(projected[:, :, 2]))
    attended = low_back(low(attention(queries, all_keys, values))).reshape(groups, length, D)
    branch = low_back(jnp.einsum('gld,de->gle', attended, out_full, precision=highest))
    middle = inputs + branch
    normed_two = low(layer_norm(middle, gain_two, shift_two))
    gate_value = low_back(jnp.einsum('gld,df->glf', normed_two, gate_full, precision=highest))
    up_value = low_back(jnp.einsum('gld,df->glf', normed_two, up_full, precision=highest))
    hidden = low(gate_value * jax.nn.sigmoid(gate_value) * up_value)
    return middle + jnp.einsum('glf,fd->gld', hidden, down_full, precision=highest)

def reference(tokens, cotangent, first_gain, first_shift, joint_weight, joint_bias, out_weight, second_gain, second_shift, gate_weight, up_weight, down_weight):
    params = tuple((weight.astype(jnp.float32) for weight in (first_gain, first_shift, joint_weight, joint_bias, out_weight, second_gain, second_shift, gate_weight, up_weight, down_weight)))
    seq_total = tokens.shape[0]
    group_size = math.gcd(seq_total, max(1, 4096 // LENGTH))
    stacked_tokens = tokens.astype(jnp.float32).reshape(seq_total // group_size, group_size, LENGTH, D)
    stacked_grads = cotangent.astype(jnp.float32).reshape(seq_total // group_size, group_size, LENGTH, D)
    initial = tuple((jnp.zeros_like(weight) for weight in params))

    def step(carry, entry):
        piece_tokens, piece_grads = entry
        results, pullback = jax.vjp(forward, params, piece_tokens)
        param_grads, input_grads = pullback(piece_grads)
        carry = tuple((total + added for total, added in zip(carry, param_grads)))
        return (carry, (results.astype(jnp.bfloat16), input_grads))
    sums, (outputs, input_grads) = lax.scan(step, initial, (stacked_tokens, stacked_grads))
    output = outputs.reshape(seq_total, LENGTH, D)
    tokens_grad = input_grads.reshape(seq_total, LENGTH, D)
    return (output, tokens_grad, sums[0], sums[1], sums[2], sums[3], sums[4], sums[5], sums[6], sums[7], sums[8], sums[9])
```

```python
import functools
import math

import jax
import jax.numpy as jnp
import numpy as np
from jax import lax
from jax.experimental import pallas as pl
from jax.experimental.pallas import tpu as pltpu
from jax.sharding import PartitionSpec as P

D = 2048
HEADS = 32
HEAD = 64
ROT = 16

epsilon = 1e-05
masked_value = -1e30
f32 = jnp.float32
bf16 = jnp.bfloat16
LOG2E_SCALE = math.log2(math.e) * HEAD**-0.5
NN = (((1,), (0,)), ((), ()))
NT = (((1,), (1,)), ((), ()))
TN = (((0,), (0,)), ((), ()))


def dot(a, b, dims):
    return lax.dot_general(a, b, dims, preferred_element_type=f32)


def params(mib=56):
    return pltpu.CompilerParams(vmem_limit_bytes=mib * 2**20)


class Plane:
    def __init__(self, count):
        outer = count // 4
        self.count = count
        self.outer = outer

        def spot(o, i, c):
            return ((o % outer) * 2 + i) * 2 + c

        def split(s):
            return s // 4, (s // 2) % 2, s % 2

        self.core = [(s, s ^ 1) for s in range(count)]
        first = []
        later = [[] for _ in range(outer - 1)]
        for s in range(count):
            o, i, c = split(s)
            swapped = outer == 2 and c == 1
            first.append((s, spot(o + 1, i, c) if swapped else spot(o, 1 - i, c)))
            for k in range(1, outer):
                later[k - 1].append((s, spot(o, 1 - i, c) if swapped else spot(o + k, i, c)))
        self.first = first
        self.later = later
        here = list(range(count))

        def moved(table, perm):
            out = [None] * count
            for a, b in perm:
                out[b] = table[a]
            return out

        blocks = [here, moved(here, first)]
        for perm in later:
            blocks += [moved(blocks[0], perm), moved(blocks[1], perm)]
        blocks += [moved(b, self.core) for b in blocks]
        self.table = np.array(blocks, np.int32).T
        self.half = 2 * outer

    @staticmethod
    def send(value, perm):
        return lax.ppermute(value, "sp", perm)

    @staticmethod
    def back(value, perm):
        return lax.ppermute(value, "sp", [(b, a) for a, b in perm])

    def gather(self, value):
        partner = self.send(value, self.core)
        one = self.send(value, self.first)
        blocks = [value, one]
        for perm in self.later:
            blocks += [self.send(value, perm), self.send(one, perm)]
        return blocks, [partner] + [self.send(b, self.core) for b in blocks[1:]]

    def reduce(self, part_of):
        half = self.half
        sums = [None] * half
        total = None
        for start in reversed(range(0, half, 2)):
            theirs = self.send(part_of(half + start, half + start + 2).astype(bf16), self.core)
            mine = part_of(start, start + 2) + theirs.astype(f32)
            if start:
                got = self.back(mine.astype(bf16), self.later[start // 2 - 1])
                total = got.astype(f32) if total is None else total + got.astype(f32)
            else:
                total = mine if total is None else mine + total
        return total[0] + self.back(total[1].astype(bf16), self.first).astype(f32)


def norm_kernel(x_ref, gain_ref, shift_ref, *rest):
    out_ref = rest[-1]
    values = x_ref[...].astype(f32)
    center = values - jnp.mean(values, axis=-1, keepdims=True)
    spread = jnp.mean(center * center, axis=-1, keepdims=True)
    out_ref[...] = (center * lax.rsqrt(spread + epsilon) * gain_ref[...] + shift_ref[...]).astype(bf16)


def norm_block(x, gain, shift, at, blocks, buffer):
    rows = x.shape[0]
    tile = min(256, rows)
    steps = rows // tile
    operands = [x, gain, shift]
    specs = [
        pl.BlockSpec((tile, D), lambda i: (i, 0)),
        pl.BlockSpec((1, D), lambda i: (0, 0)),
        pl.BlockSpec((1, D), lambda i: (0, 0)),
    ]
    aliases = {}
    if buffer is not None:
        operands.append(buffer)
        specs.append(pl.BlockSpec(memory_space=pl.ANY))
        aliases = {3: 0}
    return pl.pallas_call(
        norm_kernel,
        grid=(steps,),
        in_specs=specs,
        out_specs=pl.BlockSpec((tile, D), lambda i: (at * steps + i, 0)),
        out_shape=jax.ShapeDtypeStruct((blocks * rows, D), bf16),
        input_output_aliases=aliases,
        compiler_params=params(32),
        cost_estimate=pl.CostEstimate(flops=rows * D * 12, bytes_accessed=rows * D * 4, transcendentals=rows),
        name="first_norm",
    )(*operands)


def turn(values, cosine, sine_up, sine_down):
    width = values.shape[1]
    half = ROT // 2
    return (
        values * cosine
        + pltpu.roll(values, width - half, 1) * sine_up
        + pltpu.roll(values, half, 1) * sine_down
    )


def joint_kernel(width, table_ref, x_ref, w_ref, bias_ref, cos_ref, up_ref, down_ref, q_ref, k_ref, v_ref):
    projected = dot(x_ref[...], w_ref[...], NN) + bias_ref[...]
    tables = (cos_ref[...], up_ref[...], down_ref[...])
    q_ref[...] = turn(projected[:, :width], *tables).astype(bf16)
    k_ref[...] = turn(projected[:, width : 2 * width], *tables).astype(bf16)
    v_ref[...] = projected[:, 2 * width :].astype(bf16)


def joint_projection(table, normed, weight, bias, tables, span):
    length = normed.shape[0]
    width = weight.shape[1] // 3
    placed = pl.BlockSpec((span, width), lambda b, t: (t[b], 0))
    return pl.pallas_call(
        functools.partial(joint_kernel, width),
        grid_spec=pltpu.PrefetchScalarGridSpec(
            num_scalar_prefetch=1,
            grid=(length // span,),
            in_specs=[
                pl.BlockSpec((span, D), lambda b, t: (b, 0)),
                pl.BlockSpec((D, 3 * width), lambda b, t: (0, 0)),
                pl.BlockSpec((1, 3 * width), lambda b, t: (0, 0)),
                placed,
                placed,
                placed,
            ],
            out_specs=[placed] * 3,
        ),
        out_shape=[jax.ShapeDtypeStruct((length, width), bf16)] * 3,
        compiler_params=params(),
        cost_estimate=pl.CostEstimate(
            flops=2 * length * D * 3 * width, bytes_accessed=length * (D + 3 * width) * 2, transcendentals=0
        ),
        name="joint_projection",
    )(table, normed, weight, bias, *tables)


def attend_kernel(heads, bq, bk, q_ref, k_ref, v_ref, o_ref, lse_ref, qm, vt, acc, m_s, l_s):
    i = pl.program_id(0)
    length, width = k_ref.shape
    lane = lax.broadcasted_iota(jnp.int32, (1, width), 1) // HEAD

    @pl.when(i == 0)
    def _():
        def flip(b, carry):
            rows = pl.ds(pl.multiple_of(b * bk, bk), bk)
            vt[:, rows] = jnp.transpose(v_ref[rows, :])
            return carry

        lax.fori_loop(0, length // bk, flip, 0)

    q = q_ref[...]
    for h in range(heads):
        qm[h] = jnp.where(lane == h, q, jnp.zeros_like(q))
    acc[...] = jnp.zeros_like(acc)
    m_s[...] = jnp.full_like(m_s, masked_value)
    l_s[...] = jnp.zeros_like(l_s)

    def body(j, masked):
        rows = pl.ds(pl.multiple_of(j * bk, bk), bk)
        k = k_ref[rows, :]
        scores = [dot(k, qm[h], NT) for h in range(heads)]
        if masked:
            key_at = lax.broadcasted_iota(jnp.int32, scores[0].shape, 0) + j * bk
            query_at = lax.broadcasted_iota(jnp.int32, scores[0].shape, 1) + i * bq
            scores = [jnp.where(key_at <= query_at, s, masked_value) for s in scores]
        m0 = m_s[...]
        l0 = l_s[...]
        m1 = jnp.maximum(m0, jnp.concatenate([jnp.max(s, axis=0, keepdims=True) for s in scores] + [m0[heads:]], 0))
        m_s[...] = m1
        kept = jnp.exp2((m0 - m1) * LOG2E_SCALE)
        base = m1 * LOG2E_SCALE
        raised = [jnp.exp2(scores[h] * LOG2E_SCALE - base[h : h + 1]) for h in range(heads)]
        l_s[...] = l0 * kept + jnp.concatenate([jnp.sum(p, axis=0, keepdims=True) for p in raised] + [l0[heads:]], 0)
        for h in range(heads):
            part = slice(h * HEAD, (h + 1) * HEAD)
            acc[part, :] = acc[part, :] * kept[h : h + 1] + dot(vt[part, rows], raised[h].astype(bf16), NN)

    whole = (i * bq) // bk
    lax.fori_loop(0, whole, lambda j, c: (body(j, False), c)[1], 0)
    for d in range(max(1, bq // bk)):
        body(whole + d, True)
    for h in range(heads):
        part = slice(h * HEAD, (h + 1) * HEAD)
        acc[part, :] = acc[part, :] * (1.0 / l_s[h : h + 1])
    o_ref[...] = jnp.transpose(acc[...].astype(bf16))
    lse_ref[...] = m_s[...] * LOG2E_SCALE + jnp.log2(l_s[...])


def attend(q, k, v):
    length, width = q.shape
    heads = width // HEAD
    bq = bk = min(512, length)
    full = pl.BlockSpec((length, width), lambda i: (0, 0))
    return pl.pallas_call(
        functools.partial(attend_kernel, heads, bq, bk),
        grid=(length // bq,),
        in_specs=[pl.BlockSpec((bq, width), lambda i: (i, 0)), full, full],
        out_specs=[pl.BlockSpec((bq, width), lambda i: (i, 0)), pl.BlockSpec((8, bq), lambda i: (0, i))],
        out_shape=[jax.ShapeDtypeStruct((length, width), bf16), jax.ShapeDtypeStruct((8, length), f32)],
        scratch_shapes=[
            pltpu.VMEM((heads, bq, width), bf16),
            pltpu.VMEM((width, length), bf16),
            pltpu.VMEM((width, bq), f32),
            pltpu.VMEM((8, bq), f32),
            pltpu.VMEM((8, bq), f32),
        ],
        compiler_params=params(),
        cost_estimate=pl.CostEstimate(
            flops=8 * length * length * width,
            bytes_accessed=length * width * 8,
            transcendentals=length * length * heads // 2,
        ),
        name="attend",
    )(q, k, v)


def attend_back_kernel(
    heads, bq, bk, place_ref, q_ref, k_ref, v_ref, do_ref, o_ref, lse_ref, cos_ref, up_ref, down_ref, out_ref,
    dq_acc, dk_acc, dv_acc, delta,
):
    j = pl.program_id(0)
    length, width = q_ref.shape
    lane = lax.broadcasted_iota(jnp.int32, (1, width), 1) // HEAD

    @pl.when(j == 0)
    def _():
        dq_acc[...] = jnp.zeros_like(dq_acc)
        pick = (
            lax.broadcasted_iota(jnp.int32, (8, width), 0) == lax.broadcasted_iota(jnp.int32, (8, width), 1) // HEAD
        ).astype(f32)

        def sums(b, carry):
            rows = pl.ds(pl.multiple_of(b * bq, bq), bq)
            both = do_ref[rows, :].astype(f32) * o_ref[rows, :].astype(f32)
            delta[:, rows] = lax.dot_general(
                pick, both, NT, precision=lax.Precision.HIGHEST, preferred_element_type=f32
            )
            return carry

        lax.fori_loop(0, length // bq, sums, 0)

    key_rows = pl.ds(pl.multiple_of(j * bk, bk), bk)
    k = k_ref[key_rows, :]
    v = v_ref[key_rows, :]
    kt = jnp.transpose(k)
    dk_acc[...] = jnp.zeros_like(dk_acc)
    dv_acc[...] = jnp.zeros_like(dv_acc)

    def body(i, masked):
        rows = pl.ds(pl.multiple_of(i * bq, bq), bq)
        q = q_ref[rows, :]
        do = do_ref[rows, :]
        probs, grads, queries, results = [], [], [], []
        for h in range(heads):
            qh = jnp.where(lane == h, q, jnp.zeros_like(q))
            doh = jnp.where(lane == h, do, jnp.zeros_like(do))
            s = dot(k, qh, NT)
            p = jnp.exp2(s * LOG2E_SCALE - lse_ref[h : h + 1, rows])
            if masked:
                key_at = lax.broadcasted_iota(jnp.int32, s.shape, 0) + j * bk
                query_at = lax.broadcasted_iota(jnp.int32, s.shape, 1) + i * bq
                p = jnp.where(key_at <= query_at, p, 0.0)
            dp = dot(v, doh, NT)
            ds = p * (dp - delta[h : h + 1, rows])
            probs.append(p.astype(bf16))
            grads.append(ds.astype(bf16))
            queries.append(qh)
            results.append(doh)
        dv_acc[...] += dot(jnp.concatenate(probs, 1), jnp.concatenate(results, 0), NN)
        dk_acc[...] += dot(jnp.concatenate(grads, 1), jnp.concatenate(queries, 0), NN)
        for h in range(heads):
            part = slice(h * HEAD, (h + 1) * HEAD)
            dq_acc[part, rows] += dot(kt[part], grads[h], NN)

    first = (j * bk) // bq
    near = max(1, bk // bq)
    for d in range(near):
        body(first + d, True)
    lax.fori_loop(first + near, length // bq, lambda i, c: (body(i, False), c)[1], 0)
    scale = HEAD**-0.5
    tables = (cos_ref[...], -up_ref[...], -down_ref[...])
    dq = (jnp.transpose(dq_acc[:, key_rows]) * scale).astype(bf16).astype(f32)
    dk = (dk_acc[...] * scale).astype(bf16).astype(f32)
    out_ref[:, :width] = turn(dq, *tables).astype(bf16)
    out_ref[:, width : 2 * width] = turn(dk, *tables).astype(bf16)
    out_ref[:, 2 * width :] = dv_acc[...].astype(bf16)


def attend_back(place, q, k, v, do, o, lse, tables, span):
    length, width = q.shape
    heads = width // HEAD
    bq = min(512, length)
    bk = span
    full = pl.BlockSpec((length, width), lambda i, t: (0, 0))
    block = pl.BlockSpec((bk, width), lambda i, t: (i, 0))
    return pl.pallas_call(
        functools.partial(attend_back_kernel, heads, bq, bk),
        grid_spec=pltpu.PrefetchScalarGridSpec(
            num_scalar_prefetch=1,
            grid=(length // bk,),
            in_specs=[full] * 5 + [pl.BlockSpec((8, length), lambda i, t: (0, 0))] + [block] * 3,
            out_specs=pl.BlockSpec((bk, 3 * width), lambda i, t: (t[i], 0)),
            scratch_shapes=[
                pltpu.VMEM((width, length), f32),
                pltpu.VMEM((bk, width), f32),
                pltpu.VMEM((bk, width), f32),
                pltpu.VMEM((8, length), f32),
            ],
        ),
        out_shape=jax.ShapeDtypeStruct((length, 3 * width), bf16),
        compiler_params=params(60),
        cost_estimate=pl.CostEstimate(
            flops=12 * length * length * width,
            bytes_accessed=length * width * 16,
            transcendentals=length * length * heads // 2,
        ),
        name="attend_back",
    )(place, q, k, v, do, o, lse, *tables)


def feed_kernel(ff, x0, x1, c0, c1, wgu_ref, wd_ref, *rest):
    hidden_ref, grad_ref, x_ref, c_ref = rest[-4:]
    which = pl.program_id(0)

    @pl.when(which == 0)
    def _():
        x_ref[...] = x0[...]
        c_ref[...] = c0[...]

    @pl.when(which == 1)
    def _():
        x_ref[...] = x1[...]
        c_ref[...] = c1[...]

    both = dot(x_ref[...], wgu_ref[...], NN)
    hidden_grad = dot(c_ref[...], wd_ref[...], NT)
    gate = both[:, :ff]
    up = both[:, ff:]
    open_ = jax.nn.sigmoid(gate)
    swished = gate * open_
    hidden_ref[...] = (swished * up).astype(bf16)
    grad_ref[:, :ff] = (hidden_grad * up * open_ * (1.0 + gate * (1.0 - open_))).astype(bf16)
    grad_ref[:, ff:] = (hidden_grad * swished).astype(bf16)


def feed_block(pair, cot_pair, gate_up, down, at, half, buffers):
    rows = pair[0].shape[0]
    ff = down.shape[0]
    tile = min(256, rows)
    steps = rows // tile
    length = 2 * half * rows
    early = pl.BlockSpec((tile, D), lambda p, i: (jnp.where(p == 0, i, steps - 1), 0))
    late = pl.BlockSpec((tile, D), lambda p, i: (jnp.where(p == 0, 0, i), 0))
    operands = [pair[0], pair[1], cot_pair[0], cot_pair[1], gate_up, down]
    specs = [
        early,
        late,
        early,
        late,
        pl.BlockSpec((D, 2 * ff), lambda p, i: (0, 0)),
        pl.BlockSpec((ff, D), lambda p, i: (0, 0)),
    ]
    aliases = {}
    if buffers is not None:
        aliases = {len(operands) + n: n for n in range(4)}
        operands += list(buffers)
        specs += [pl.BlockSpec(memory_space=pl.ANY)] * 4

    def place(p, i):
        return ((p * half + at) * steps + i, 0)

    return pl.pallas_call(
        functools.partial(feed_kernel, ff),
        grid=(2, steps),
        in_specs=specs,
        out_specs=[
            pl.BlockSpec((tile, ff), place),
            pl.BlockSpec((tile, 2 * ff), place),
            pl.BlockSpec((tile, D), place),
            pl.BlockSpec((tile, D), place),
        ],
        out_shape=[
            jax.ShapeDtypeStruct((length, ff), bf16),
            jax.ShapeDtypeStruct((length, 2 * ff), bf16),
            jax.ShapeDtypeStruct((length, D), bf16),
            jax.ShapeDtypeStruct((length, D), bf16),
        ],
        input_output_aliases=aliases,
        compiler_params=params(),
        cost_estimate=pl.CostEstimate(
            flops=12 * rows * D * ff, bytes_accessed=6 * D * ff + rows * D * 16, transcendentals=2 * rows * ff
        ),
        name="feed_forward",
    )(*operands)


def rotary_columns(length, width):
    half = ROT // 2
    indices = jnp.arange(half, dtype=f32)
    inverse = 1.0 / 10000.0 ** (indices * 2.0 / ROT)
    angles = jnp.arange(length, dtype=jnp.int32).astype(f32)[:, None] * inverse[None, :]
    cosine, sine = jnp.cos(angles), jnp.sin(angles)
    rest = jnp.zeros((length, HEAD - ROT), f32)
    none = jnp.zeros((length, half), f32)
    one_head = (
        jnp.concatenate([cosine, cosine, rest + 1.0], -1),
        jnp.concatenate([-sine, none, rest], -1),
        jnp.concatenate([none, sine, rest], -1),
    )
    return tuple(jnp.tile(t, (1, width // HEAD)) for t in one_head)


def norm_parts(values):
    center = values - jnp.mean(values, axis=-1, keepdims=True)
    spread = jnp.mean(center * center, axis=-1, keepdims=True)
    inverse = lax.rsqrt(spread + epsilon)
    return center * inverse, inverse


def norm_back(grad, xhat, inverse, gain):
    scaled = grad * gain
    middle = jnp.mean(scaled, axis=-1, keepdims=True)
    along = jnp.mean(scaled * xhat, axis=-1, keepdims=True)
    return (
        inverse * (scaled - middle - xhat * along),
        jnp.sum(grad * xhat, axis=0),
        jnp.sum(grad, axis=0),
    )


def swap_sp(value):
    return lax.all_to_all(value, "sp", split_axis=0, concat_axis=0, tiled=True)


def per_device(
    tokens, cotangent, first_gain, first_shift, joint_weight, joint_bias, out_weight, second_gain, second_shift,
    gate_weight, up_weight, down_weight,
):
    n_sp = lax.axis_size("sp")
    n_z = lax.axis_size("fsdp")
    n_all = n_sp * n_z
    plane = Plane(n_sp)
    half = plane.half
    me = lax.axis_index("sp")
    span = tokens.shape[1]
    length = n_sp * span
    width = D // n_sp
    depth = joint_weight.shape[0]
    ff_rows = down_weight.shape[0]
    unit = max(16, 128 // n_z)
    ff_pad = -(-ff_rows // unit) * unit
    ff = n_z * ff_pad

    order = jnp.asarray(plane.table)[me]
    place = jnp.asarray(np.argsort(plane.table, axis=1).astype(np.int32))[me]

    small = jnp.concatenate([first_gain, first_shift, second_gain, second_shift, joint_bias])
    small = jnp.broadcast_to(small[None], (n_all, small.shape[0]))
    small = lax.all_to_all(small, ("fsdp", "sp"), split_axis=0, concat_axis=0, tiled=True).astype(f32)
    n_gain = first_gain.shape[0]
    gain_one, shift_one, gain_two, shift_two = (
        small[:, i * n_gain : (i + 1) * n_gain].reshape(1, D) for i in range(4)
    )
    bias_all = small[:, 4 * n_gain :].reshape(3, n_sp, width)
    bias = lax.dynamic_index_in_dim(bias_all, me, axis=1, keepdims=False).reshape(1, 3 * width)

    x = tokens.reshape(span, D)
    blocks, partners = plane.gather(x)
    joint_cols = joint_weight.reshape(depth, 3, n_sp, width).transpose(2, 0, 1, 3).reshape(n_sp * depth, 3 * width)
    joint_mine = lax.all_gather(swap_sp(joint_cols), "fsdp", axis=0, tiled=True)

    def by_columns(weight):
        cut = weight.reshape(depth, n_z, n_sp, ff_rows)
        cut = jnp.pad(cut, ((0, 0), (0, 0), (0, 0), (0, ff_pad - ff_rows)))
        return cut.transpose(2, 0, 1, 3).reshape(n_sp * depth, ff)

    gate_up_cols = jnp.concatenate([by_columns(gate_weight), by_columns(up_weight)], axis=1)
    down_rows = jnp.pad(down_weight, ((0, ff_pad - ff_rows), (0, 0)))

    out_full = lax.all_gather(out_weight, ("fsdp", "sp"), axis=0, tiled=True)
    gate_up = lax.all_gather(swap_sp(gate_up_cols), "fsdp", axis=0, tiled=True)
    down = lax.all_gather(down_rows, "fsdp", axis=0, tiled=True)

    normed = None
    for t, block in enumerate(blocks + partners):
        normed = norm_block(block, gain_one, shift_one, t, n_sp, normed)
    tables = rotary_columns(length, width)
    q, k, v = joint_projection(order, normed, joint_mine, bias, tables, span)
    cot_blocks, cot_partners = plane.gather(cotangent.reshape(span, D))
    o, lse = attend(q, k, v)

    attended = swap_sp(o).reshape(n_sp, span, width)
    out_groups = out_full.reshape(n_sp, width, D)
    inputs = x.astype(f32)
    middle = inputs + jnp.einsum("jrc,jce->re", attended, out_groups, preferred_element_type=f32)
    xhat_two, inverse_two = norm_parts(middle)
    normed_two = (xhat_two * gain_two + shift_two).astype(bf16)

    two_blocks, two_partners = plane.gather(normed_two)
    feed = None
    for t in range(half):
        feed = feed_block(
            (two_blocks[t], two_partners[t]), (cot_blocks[t], cot_partners[t]), gate_up, down, t, half, feed
        )
    hidden, gate_up_grad, two_all, cot_all = feed

    def two_part(start, stop):
        rows = gate_up_grad[start * span : stop * span]
        return dot(rows, gate_up, NT).reshape(stop - start, span, D)

    two_grad = plane.reduce(two_part)

    def out_part(start, stop):
        rows = hidden[start * span : stop * span]
        return dot(rows, down, NN).reshape(stop - start, span, D)

    output = (middle + plane.reduce(out_part)).astype(bf16)

    down_sum = dot(hidden, cot_all, TN).astype(bf16)
    gate_up_sum = dot(two_all, gate_up_grad, TN).astype(bf16)
    down_grad = lax.psum_scatter(down_sum, "fsdp", scatter_dimension=0, tiled=True)[:ff_rows].astype(f32)
    gate_up_own = swap_sp(lax.psum_scatter(gate_up_sum, "fsdp", scatter_dimension=0, tiled=True))
    gate_up_own = gate_up_own.reshape(n_sp, depth, 2, n_z, ff_pad)[..., :ff_rows].transpose(2, 1, 3, 0, 4)
    gate_up_own = gate_up_own.reshape(2, depth, n_z * n_sp * ff_rows).astype(f32)

    two_input_grad, gain_two_sum, shift_two_sum = norm_back(two_grad, xhat_two, inverse_two, gain_two)
    middle_grad = cotangent.reshape(span, D).astype(f32) + two_input_grad
    branch_grad = middle_grad.astype(bf16)
    attended_grad = jnp.einsum("re,jce->jrc", branch_grad, out_groups, preferred_element_type=f32).astype(bf16)
    do = swap_sp(attended_grad.reshape(n_sp * span, width))
    out_sum = jnp.einsum("jrc,re->jce", attended, branch_grad, preferred_element_type=f32).reshape(D, D)
    out_grad = lax.psum_scatter(out_sum.astype(bf16), ("fsdp", "sp"), scatter_dimension=0, tiled=True).astype(f32)

    joint_grad_rows = attend_back(place, q, k, v, do, o, lse, tables, span)

    def normed_part(start, stop):
        rows = joint_grad_rows[start * span : stop * span]
        return dot(rows, joint_mine, NT).reshape(stop - start, span, D)

    normed_grad = plane.reduce(normed_part)
    joint_sum = dot(normed, joint_grad_rows, TN).astype(bf16)
    joint_own = swap_sp(lax.psum_scatter(joint_sum, "fsdp", scatter_dimension=0, tiled=True))
    joint_grad = joint_own.reshape(n_sp, depth, 3, width).transpose(1, 2, 0, 3).reshape(depth, 3 * D).astype(f32)
    bias_sum = jnp.sum(joint_grad_rows.astype(f32), axis=0).reshape(3, 1, width)
    bias_sum = lax.dynamic_update_slice(jnp.zeros((3, n_sp, width), f32), bias_sum, (0, me, 0))

    xhat_one, inverse_one = norm_parts(inputs)
    input_grad, gain_one_sum, shift_one_sum = norm_back(normed_grad, xhat_one, inverse_one, gain_one)
    tokens_grad = (middle_grad + input_grad).reshape(tokens.shape)

    sums = [gain_one_sum, shift_one_sum, gain_two_sum, shift_two_sum]
    sums = jnp.concatenate([s.reshape(n_all, n_gain) for s in sums] + [bias_sum.reshape(n_all, -1)], axis=1)
    sums = jnp.sum(lax.all_to_all(sums, ("fsdp", "sp"), split_axis=0, concat_axis=0, tiled=True), axis=0)
    gain_one_grad, shift_one_grad, gain_two_grad, shift_two_grad = (
        sums[i * n_gain : (i + 1) * n_gain] for i in range(4)
    )
    return (
        output.reshape(tokens.shape),
        tokens_grad,
        gain_one_grad,
        shift_one_grad,
        joint_grad,
        sums[4 * n_gain :],
        out_grad,
        gain_two_grad,
        shift_two_grad,
        gate_up_own[0],
        gate_up_own[1],
        down_grad,
    )


def solution(mesh):
    rows = P("fsdp", "sp", None)
    vector = P(("fsdp", "sp"))
    matrix = P(("fsdp", "sp"), None)
    return jax.shard_map(
        per_device,
        mesh=mesh,
        in_specs=(rows, rows, vector, vector, matrix, vector, matrix, vector, vector, matrix, matrix, matrix),
        out_specs=(rows, rows, vector, vector, matrix, vector, matrix, vector, vector, matrix, matrix, matrix),
        check_vma=False,
    )
```

```python
import functools
import math

import jax
import jax.numpy as jnp
import numpy as np
from jax import lax
from jax.experimental import pallas as pl
from jax.experimental.pallas import tpu as pltpu
from jax.sharding import PartitionSpec as P

D = 2048
HEADS = 32
HEAD = 64
ROT = 16

epsilon = 1e-05
masked_value = -1e30
f32 = jnp.float32
bf16 = jnp.bfloat16
LOG2E_SCALE = math.log2(math.e) * HEAD**-0.5
NN = (((1,), (0,)), ((), ()))
NT = (((1,), (1,)), ((), ()))
TN = (((0,), (0,)), ((), ()))


def dot(a, b, dims):
    return lax.dot_general(a, b, dims, preferred_element_type=f32)


def params(mib=56):
    return pltpu.CompilerParams(vmem_limit_bytes=mib * 2**20)


class Plane:
    def __init__(self, count):
        outer = count // 4
        self.count = count
        self.outer = outer

        def spot(o, i, c):
            return ((o % outer) * 2 + i) * 2 + c

        def split(s):
            return s // 4, (s // 2) % 2, s % 2

        self.core = [(s, s ^ 1) for s in range(count)]
        first = []
        later = [[] for _ in range(outer - 1)]
        for s in range(count):
            o, i, c = split(s)
            swapped = outer == 2 and c == 1
            first.append((s, spot(o + 1, i, c) if swapped else spot(o, 1 - i, c)))
            for k in range(1, outer):
                later[k - 1].append((s, spot(o, 1 - i, c) if swapped else spot(o + k, i, c)))
        self.first = first
        self.later = later
        here = list(range(count))

        def moved(table, perm):
            out = [None] * count
            for a, b in perm:
                out[b] = table[a]
            return out

        blocks = [here, moved(here, first)]
        for perm in later:
            blocks += [moved(blocks[0], perm), moved(blocks[1], perm)]
        blocks += [moved(b, self.core) for b in blocks]
        self.table = np.array(blocks, np.int32).T
        self.half = 2 * outer

    @staticmethod
    def send(value, perm):
        return lax.ppermute(value, "sp", perm)

    @staticmethod
    def back(value, perm):
        return lax.ppermute(value, "sp", [(b, a) for a, b in perm])

    def gather_first(self, value):
        return (
            self.send(value, self.core),
            self.send(value, self.first),
            [self.send(value, perm) for perm in self.later],
        )

    def gather_second(self, one, twos):
        return (
            self.send(one, self.core),
            [self.send(two, self.core) for two in twos],
            [self.send(one, perm) for perm in self.later],
        )

    def gather_third(self, threes):
        return [self.send(three, self.core) for three in threes]


    def reduce_far(self, product, deps=()):
        sent = []
        for start in reversed(range(2, self.half, 2)):
            theirs = self.send(product(self.half + start, self.half + start + 2, (), bf16, deps), self.core)
            mine = product(start, start + 2, ((theirs, 0),), bf16)
            sent.append(self.back(mine, self.later[start // 2 - 1]))
        return sent

    def reduce_near(self, product, deps=()):
        return self.send(product(self.half, self.half + 2, (), bf16, deps), self.core)

    def reduce_next(self, product, got, theirs, deps=()):
        one = product(1, 2, tuple((t, 1) for t in [theirs] + got), bf16, deps)
        return self.back(one, self.first)

    def reduce_own(self, product, got, theirs, last, dtype=bf16):
        return product(0, 1, tuple((t, 0) for t in [theirs] + got + [last]), dtype)[0]


def launch(
    kernel, operands, in_specs, outs, out_specs, *, grid, name, cost, scratch=(), deps=(), aliases=None, prefetch=0, mib=60
):
    deps = jax.tree.leaves(deps)
    count = len(operands)

    def body(*refs):
        kernel(*refs[:count], *refs[count + len(deps) :])

    flops, moved, transcendentals = cost
    return pl.pallas_call(
        body,
        grid_spec=pltpu.PrefetchScalarGridSpec(
            num_scalar_prefetch=prefetch,
            grid=grid,
            in_specs=list(in_specs) + [pl.BlockSpec(memory_space=pl.ANY)] * len(deps),
            out_specs=list(out_specs),
            scratch_shapes=list(scratch),
        ),
        out_shape=list(outs),
        input_output_aliases=aliases or {},
        compiler_params=pltpu.CompilerParams(vmem_limit_bytes=mib * 2**20),
        cost_estimate=pl.CostEstimate(flops=int(flops), bytes_accessed=int(moved), transcendentals=int(transcendentals)),
        name=name,
    )(*operands, *deps)


ANYWHERE = pl.BlockSpec(memory_space=pl.ANY)


def held(value, deps):
    return launch(
        lambda *refs: None, [value], [ANYWHERE], [shape_of(value.shape, value.dtype)], [ANYWHERE],
        grid=(1,), aliases={0: 0}, deps=deps, cost=(0, 0, 0), name="held",
    )[0]


def whole(shape):
    return pl.BlockSpec(shape, lambda *_: (0,) * len(shape))


def shape_of(shape, dtype):
    return jax.ShapeDtypeStruct(shape, dtype)


def product_kernel(terms, dims, *refs):
    out_ref = refs[-1]
    count, rows, width = out_ref.shape
    total = dot(refs[0][...], refs[terms][...], dims)
    for t in range(1, terms):
        total += dot(refs[t][...], refs[terms + t][...], dims)
    for ref in refs[2 * terms : -1]:
        total += ref[...].astype(f32).reshape(count * rows, width)
    out_ref[...] = total.astype(out_ref.dtype).reshape(count, rows, width)


def product_of(lefts, right, dims, span):
    tile = 512
    depth = sum(left.shape[1] for left in lefts)

    def right_at(at, left):
        if dims is NT:
            return pl.BlockSpec((tile, left.shape[1]), lambda i: (i, at))
        return pl.BlockSpec((left.shape[1], tile), lambda i: (at, i))

    def product(start, stop, addends, dtype, deps=()):
        count = stop - start
        assert start % count == 0 and all(at % count == 0 for _, at in addends)

        def columns(at):
            return pl.BlockSpec((count, span, tile), lambda i: (at // count, 0, i))

        return launch(
            functools.partial(product_kernel, len(lefts), dims),
            [*lefts, *[right] * len(lefts), *(value for value, _ in addends)],
            [pl.BlockSpec((count * span, a.shape[1]), lambda i: (start // count, 0)) for a in lefts]
            + [right_at(t, left) for t, left in enumerate(lefts)]
            + [columns(at) for _, at in addends],
            [shape_of((count, span, D), dtype)],
            [columns(0)],
            grid=(D // tile,),
            deps=deps,
            mib=60,
            cost=(2 * count * span * D * depth, 2 * depth * (D + count * span) + 4 * count * span * D, 0),
            name="block_product",
        )[0]

    return product


def norm_kernel(x_ref, gain_ref, shift_ref, *rest):
    out_ref = rest[-1]
    values = x_ref[...].astype(f32)
    center = values - jnp.mean(values, axis=-1, keepdims=True)
    spread = jnp.mean(center * center, axis=-1, keepdims=True)
    out_ref[...] = (center * lax.rsqrt(spread + epsilon) * gain_ref[...] + shift_ref[...]).astype(bf16)


def norm_block(x, gain, shift, at, blocks, buffer, deps=()):
    rows = x.shape[0]
    tile = min(256, rows)
    steps = rows // tile
    row = pl.BlockSpec((1, D), lambda i: (0, 0))
    held = [] if buffer is None else [buffer]
    return launch(
        norm_kernel,
        [x, gain, shift, *held],
        [pl.BlockSpec((tile, D), lambda i: (i, 0)), row, row, *[ANYWHERE] * len(held)],
        [shape_of((blocks * rows, D), bf16)],
        [pl.BlockSpec((tile, D), lambda i: (at * steps + i, 0))],
        grid=(steps,),
        aliases={3: 0} if held else {},
        deps=deps,
        mib=60,
        cost=(rows * D * 12, rows * D * 4, rows),
        name="first_norm",
    )[0]


def cut_joint_kernel(n_sp, groups, group, in_ref, out_ref):
    for j in range(n_sp):
        for g in range(groups):
            for m in range(3):
                to = (g * 3 + m) * group
                start = m * D + (j * groups + g) * group
                out_ref[j, :, to : to + group] = in_ref[:, start : start + group]


def cut_joint(weight, n_sp, groups):
    depth = weight.shape[0]
    width = D // n_sp
    return launch(
        functools.partial(cut_joint_kernel, n_sp, groups, width // groups),
        [weight], [whole(weight.shape)], [shape_of((n_sp, depth, 3 * width), bf16)], [whole((n_sp, depth, 3 * width))],
        grid=(1,), cost=(0, weight.size * 4, 0), name="cut_joint",
    )[0]


def join_joint_kernel(n_sp, groups, group, *refs):
    out_ref = refs[-1]
    for j in range(n_sp):
        for g in range(groups):
            for m in range(3):
                start = m * D + (j * groups + g) * group
                out_ref[:, start : start + group] = refs[g][j, :, m * group : (m + 1) * group].astype(f32)


def join_joint(parts, n_sp):
    groups = len(parts)
    depth = parts[0].shape[1]
    return launch(
        functools.partial(join_joint_kernel, n_sp, groups, parts[0].shape[2] // 3),
        parts, [whole(p.shape) for p in parts], [shape_of((depth, 3 * D), f32)], [whole((depth, 3 * D))],
        grid=(1,), cost=(0, depth * D * 18, 0), name="join_joint",
    )[0]


def cut_feed_kernel(n_sp, n_z, size, padded, gate_ref, up_ref, out_ref):
    out_ref[...] = jnp.zeros_like(out_ref)
    for j in range(n_sp):
        for p, ref in enumerate((gate_ref, up_ref)):
            for z in range(n_z):
                start = (z * n_sp + j) * size
                to = (p * n_z + z) * padded
                out_ref[j, :, to : to + size] = ref[:, start : start + size]


def cut_feed(gate_weight, up_weight, n_sp, n_z, padded, deps):
    depth, total = gate_weight.shape
    size = total // (n_sp * n_z)
    shape = (n_sp, depth, 2 * n_z * padded)
    return launch(
        functools.partial(cut_feed_kernel, n_sp, n_z, size, padded),
        [gate_weight, up_weight], [whole(gate_weight.shape)] * 2, [shape_of(shape, bf16)], [whole(shape)],
        grid=(1,), cost=(0, gate_weight.size * 8, 0), name="cut_feed", deps=deps,
    )[0]


def join_feed_kernel(n_sp, n_z, size, padded, in_ref, gate_ref, up_ref):
    for p, ref in enumerate((gate_ref, up_ref)):
        for z in range(n_z):
            for j in range(n_sp):
                start = (z * n_sp + j) * size
                to = (p * n_z + z) * padded
                ref[:, start : start + size] = in_ref[j, :, to : to + size].astype(f32)


def join_feed(value, n_z, size, padded):
    n_sp, depth, _ = value.shape
    shape = (depth, n_sp * n_z * size)
    return launch(
        functools.partial(join_feed_kernel, n_sp, n_z, size, padded),
        [value], [whole(value.shape)], [shape_of(shape, f32)] * 2, [whole(shape)] * 2,
        grid=(1,), cost=(0, value.size * 6, 0), name="join_feed",
    )


def norm_back_kernel(steps, n_parts, *refs):
    grad_ref, x_ref, gain_ref, beside_ref = refs[:4]
    weights = refs[4 : 4 + n_parts]
    outs = refs[4 + n_parts :]
    result_ref, sums_ref = outs[0], outs[1]
    values = x_ref[...].astype(f32)
    center = values - jnp.mean(values, axis=-1, keepdims=True)
    spread = jnp.mean(center * center, axis=-1, keepdims=True)
    inverse = lax.rsqrt(spread + epsilon)
    xhat = center * inverse
    grad = grad_ref[...].astype(f32)
    scaled = grad * gain_ref[...]
    level = jnp.mean(scaled, axis=-1, keepdims=True)
    along = jnp.mean(scaled * xhat, axis=-1, keepdims=True)
    result = beside_ref[...].astype(f32) + inverse * (scaled - level - xhat * along)
    result_ref[...] = result

    @pl.when(pl.program_id(0) == 0)
    def _():
        sums_ref[...] = jnp.zeros_like(sums_ref)

    sums_ref[0:1] += jnp.sum(grad * xhat, axis=0, keepdims=True)
    sums_ref[1:2] += jnp.sum(grad, axis=0, keepdims=True)
    if n_parts:
        branch = result.astype(bf16)
        outs[2][...] = branch
        parts = outs[3:]
        group = parts[0].shape[2]
        full = dot(branch, weights[0][...], NT).astype(bf16)
        for j in range(parts[0].shape[0]):
            for g, part in enumerate(parts):
                start = (j * len(parts) + g) * group
                part[j] = full[:, start : start + group]


def norm_back(grad, x, gain, beside, weight=None, n_sp=0, groups=0):
    rows = x.shape[0]
    tile = min(128, rows)
    row = pl.BlockSpec((1, D), lambda i: (0, 0))
    block = pl.BlockSpec((tile, D), lambda i: (i, 0))
    outs = [shape_of((rows, D), f32), shape_of((8, D), f32)]
    out_specs = [block, whole((8, D))]
    extra, specs = [], []
    if weight is not None:
        group = D // n_sp // groups
        extra, specs = [weight], [whole((D, D))]
        outs += [shape_of((rows, D), bf16)] + [shape_of((n_sp, rows, group), bf16)] * groups
        out_specs += [block] + [pl.BlockSpec((n_sp, tile, group), lambda i: (0, i, 0))] * groups
    return launch(
        functools.partial(norm_back_kernel, rows // tile, len(extra)),
        [grad, x, gain, beside, *extra],
        [block, block, row, block, *specs],
        outs,
        out_specs,
        grid=(rows // tile,),
        cost=(rows * D * (20 + 2 * D * len(extra)), rows * D * 16 + 2 * D * D * len(extra), rows),
        name="norm_back",
    )


def middle_kernel(groups, n_sp, *refs):
    parts, (out_w, x_ref, gain_ref, shift_ref) = refs[:groups], refs[groups : groups + 4]
    middle_ref, normed_ref, attended_ref = refs[groups + 4 :]
    group = parts[0].shape[2]
    for j in range(n_sp):
        for g in range(groups):
            start = (j * groups + g) * group
            attended_ref[:, start : start + group] = parts[g][j]
    values = x_ref[...].astype(f32) + dot(attended_ref[...], out_w[...], NN)
    middle_ref[...] = values
    center = values - jnp.mean(values, axis=-1, keepdims=True)
    spread = jnp.mean(center * center, axis=-1, keepdims=True)
    normed_ref[...] = (center * lax.rsqrt(spread + epsilon) * gain_ref[...] + shift_ref[...]).astype(bf16)


def middle_of(parts, out_w, x, gain, shift, deps=()):
    n_sp, rows, group = parts[0].shape
    tile = min(128, rows)
    row = pl.BlockSpec((1, D), lambda i: (0, 0))
    block = pl.BlockSpec((tile, D), lambda i: (i, 0))
    return launch(
        functools.partial(middle_kernel, len(parts), n_sp),
        [*parts, out_w, x, gain, shift],
        [pl.BlockSpec((n_sp, tile, group), lambda i: (0, i, 0))] * len(parts)
        + [pl.BlockSpec((D, D), lambda i: (0, 0)), block, row, row],
        [shape_of((rows, D), f32), shape_of((rows, D), bf16), shape_of((rows, D), bf16)],
        [block] * 3,
        grid=(rows // tile,),
        deps=deps,
        cost=(2 * rows * D * D, 2 * D * D + rows * D * 12, rows),
        name="middle",
    )


def turn(values, cosine, sine_up, sine_down):
    width = values.shape[1]
    half = ROT // 2
    return (
        values * cosine
        + pltpu.roll(values, width - half, 1) * sine_up
        + pltpu.roll(values, half, 1) * sine_down
    )


def joint_kernel(width, table_ref, x_ref, w_ref, bias_ref, cos_ref, up_ref, down_ref, *outs):
    projected = dot(x_ref[...], w_ref[...], NN) + bias_ref[...]
    tables = (cos_ref[...], up_ref[...], down_ref[...])
    for g in range(len(outs) // 3):
        part = projected[:, 3 * g * width : 3 * (g + 1) * width]
        outs[3 * g][...] = turn(part[:, :width], *tables).astype(bf16)
        outs[3 * g + 1][...] = turn(part[:, width : 2 * width], *tables).astype(bf16)
        outs[3 * g + 2][...] = part[:, 2 * width :].astype(bf16)


def joint_projection(table, normed, weight, bias, tables, span, groups):
    length = normed.shape[0]
    total = weight.shape[1]
    width = total // 3 // groups
    placed = pl.BlockSpec((span, width), lambda b, t: (t[b], 0))
    return pl.pallas_call(
        functools.partial(joint_kernel, width),
        grid_spec=pltpu.PrefetchScalarGridSpec(
            num_scalar_prefetch=1,
            grid=(length // span,),
            in_specs=[
                pl.BlockSpec((span, D), lambda b, t: (b, 0)),
                pl.BlockSpec((D, total), lambda b, t: (0, 0)),
                pl.BlockSpec((1, total), lambda b, t: (0, 0)),
                placed,
                placed,
                placed,
            ],
            out_specs=[placed] * (3 * groups),
        ),
        out_shape=[jax.ShapeDtypeStruct((length, width), bf16)] * (3 * groups),
        compiler_params=params(),
        cost_estimate=pl.CostEstimate(
            flops=2 * length * D * total, bytes_accessed=length * (D + total) * 2, transcendentals=0
        ),
        name="joint_projection",
    )(table, normed, weight, bias, *tables)


def attend_kernel(heads, bq, bk, q_ref, k_ref, v_ref, *rest):
    o_ref, lse_ref, qm, vt, acc, m_s, l_s = rest[-7:]
    i = pl.program_id(0)
    length, width = k_ref.shape
    lane = lax.broadcasted_iota(jnp.int32, (1, width), 1) // HEAD

    @pl.when(i == 0)
    def _():
        def flip(b, carry):
            rows = pl.ds(pl.multiple_of(b * bk, bk), bk)
            vt[:, rows] = jnp.transpose(v_ref[rows, :])
            return carry

        lax.fori_loop(0, length // bk, flip, 0)

    q = q_ref[...]
    for h in range(heads):
        qm[h] = jnp.where(lane == h, q, jnp.zeros_like(q))
    acc[...] = jnp.zeros_like(acc)
    m_s[...] = jnp.full_like(m_s, masked_value)
    l_s[...] = jnp.zeros_like(l_s)

    def body(j, masked):
        rows = pl.ds(pl.multiple_of(j * bk, bk), bk)
        k = k_ref[rows, :]
        scores = [dot(k, qm[h], NT) for h in range(heads)]
        if masked:
            key_at = lax.broadcasted_iota(jnp.int32, scores[0].shape, 0) + j * bk
            query_at = lax.broadcasted_iota(jnp.int32, scores[0].shape, 1) + i * bq
            scores = [jnp.where(key_at <= query_at, s, masked_value) for s in scores]
        m0 = m_s[...]
        l0 = l_s[...]
        m1 = jnp.maximum(m0, jnp.concatenate([jnp.max(s, axis=0, keepdims=True) for s in scores] + [m0[heads:]], 0))
        m_s[...] = m1
        kept = jnp.exp2((m0 - m1) * LOG2E_SCALE)
        base = m1 * LOG2E_SCALE
        raised = [jnp.exp2(scores[h] * LOG2E_SCALE - base[h : h + 1]) for h in range(heads)]
        l_s[...] = l0 * kept + jnp.concatenate([jnp.sum(p, axis=0, keepdims=True) for p in raised] + [l0[heads:]], 0)
        for h in range(heads):
            part = slice(h * HEAD, (h + 1) * HEAD)
            acc[part, :] = acc[part, :] * kept[h : h + 1] + dot(vt[part, rows], raised[h].astype(bf16), NN)

    whole = (i * bq) // bk
    lax.fori_loop(0, whole, lambda j, c: (body(j, False), c)[1], 0)
    for d in range(max(1, bq // bk)):
        body(whole + d, True)
    for h in range(heads):
        part = slice(h * HEAD, (h + 1) * HEAD)
        acc[part, :] = acc[part, :] * (1.0 / l_s[h : h + 1])
    o_ref[...] = jnp.transpose(acc[...].astype(bf16))
    lse_ref[...] = m_s[...] * LOG2E_SCALE + jnp.log2(l_s[...])


def attend(q, k, v, deps=()):
    deps = jax.tree.leaves(deps)
    length, width = q.shape
    heads = width // HEAD
    bq = bk = min(512, length)
    full = pl.BlockSpec((length, width), lambda i: (0, 0))
    return pl.pallas_call(
        functools.partial(attend_kernel, heads, bq, bk),
        grid=(length // bq,),
        in_specs=[pl.BlockSpec((bq, width), lambda i: (i, 0)), full, full]
        + [pl.BlockSpec(memory_space=pl.ANY)] * len(deps),
        out_specs=[pl.BlockSpec((bq, width), lambda i: (i, 0)), pl.BlockSpec((8, bq), lambda i: (0, i))],
        out_shape=[jax.ShapeDtypeStruct((length, width), bf16), jax.ShapeDtypeStruct((8, length), f32)],
        scratch_shapes=[
            pltpu.VMEM((heads, bq, width), bf16),
            pltpu.VMEM((width, length), bf16),
            pltpu.VMEM((width, bq), f32),
            pltpu.VMEM((8, bq), f32),
            pltpu.VMEM((8, bq), f32),
        ],
        compiler_params=params(),
        cost_estimate=pl.CostEstimate(
            flops=8 * length * length * width,
            bytes_accessed=length * width * 8,
            transcendentals=length * length * heads // 2,
        ),
        name="attend",
    )(q, k, v, *deps)


def attend_back_kernel(
    heads, bq, bk, place_ref, q_ref, k_ref, v_ref, do_ref, o_ref, lse_ref, cos_ref, up_ref, down_ref, *rest
):
    out_ref, dq_acc, dk_acc, dv_acc, delta = rest[-5:]
    j = pl.program_id(0)
    length, width = q_ref.shape
    lane = lax.broadcasted_iota(jnp.int32, (1, width), 1) // HEAD

    @pl.when(j == 0)
    def _():
        dq_acc[...] = jnp.zeros_like(dq_acc)
        pick = (
            lax.broadcasted_iota(jnp.int32, (8, width), 0) == lax.broadcasted_iota(jnp.int32, (8, width), 1) // HEAD
        ).astype(f32)

        def sums(b, carry):
            rows = pl.ds(pl.multiple_of(b * bq, bq), bq)
            both = do_ref[rows, :].astype(f32) * o_ref[rows, :].astype(f32)
            delta[:, rows] = lax.dot_general(
                pick, both, NT, precision=lax.Precision.HIGHEST, preferred_element_type=f32
            )
            return carry

        lax.fori_loop(0, length // bq, sums, 0)

    key_rows = pl.ds(pl.multiple_of(j * bk, bk), bk)
    k = k_ref[key_rows, :]
    v = v_ref[key_rows, :]
    kt = jnp.transpose(k)
    dk_acc[...] = jnp.zeros_like(dk_acc)
    dv_acc[...] = jnp.zeros_like(dv_acc)

    def body(i, masked):
        rows = pl.ds(pl.multiple_of(i * bq, bq), bq)
        q = q_ref[rows, :]
        do = do_ref[rows, :]
        probs, grads, queries, results = [], [], [], []
        for h in range(heads):
            qh = jnp.where(lane == h, q, jnp.zeros_like(q))
            doh = jnp.where(lane == h, do, jnp.zeros_like(do))
            s = dot(k, qh, NT)
            p = jnp.exp2(s * LOG2E_SCALE - lse_ref[h : h + 1, rows])
            if masked:
                key_at = lax.broadcasted_iota(jnp.int32, s.shape, 0) + j * bk
                query_at = lax.broadcasted_iota(jnp.int32, s.shape, 1) + i * bq
                p = jnp.where(key_at <= query_at, p, 0.0)
            dp = dot(v, doh, NT)
            ds = p * (dp - delta[h : h + 1, rows])
            probs.append(p.astype(bf16))
            grads.append(ds.astype(bf16))
            queries.append(qh)
            results.append(doh)
        dv_acc[...] += dot(jnp.concatenate(probs, 1), jnp.concatenate(results, 0), NN)
        dk_acc[...] += dot(jnp.concatenate(grads, 1), jnp.concatenate(queries, 0), NN)
        for h in range(heads):
            part = slice(h * HEAD, (h + 1) * HEAD)
            dq_acc[part, rows] += dot(kt[part], grads[h], NN)

    first = (j * bk) // bq
    near = max(1, bk // bq)
    for d in range(near):
        body(first + d, True)
    lax.fori_loop(first + near, length // bq, lambda i, c: (body(i, False), c)[1], 0)
    scale = HEAD**-0.5
    tables = (cos_ref[...], -up_ref[...], -down_ref[...])
    dq = (jnp.transpose(dq_acc[:, key_rows]) * scale).astype(bf16).astype(f32)
    dk = (dk_acc[...] * scale).astype(bf16).astype(f32)
    out_ref[:, :width] = turn(dq, *tables).astype(bf16)
    out_ref[:, width : 2 * width] = turn(dk, *tables).astype(bf16)
    out_ref[:, 2 * width :] = dv_acc[...].astype(bf16)


def attend_back(place, q, k, v, do, o, lse, tables, span, deps=()):
    deps = jax.tree.leaves(deps)
    length, width = q.shape
    heads = width // HEAD
    bq = min(512, length)
    bk = span
    full = pl.BlockSpec((length, width), lambda i, t: (0, 0))
    block = pl.BlockSpec((bk, width), lambda i, t: (i, 0))
    return pl.pallas_call(
        functools.partial(attend_back_kernel, heads, bq, bk),
        grid_spec=pltpu.PrefetchScalarGridSpec(
            num_scalar_prefetch=1,
            grid=(length // bk,),
            in_specs=[full] * 5 + [pl.BlockSpec((8, length), lambda i, t: (0, 0))] + [block] * 3
            + [pl.BlockSpec(memory_space=pl.ANY)] * len(deps),
            out_specs=pl.BlockSpec((bk, 3 * width), lambda i, t: (t[i], 0)),
            scratch_shapes=[
                pltpu.VMEM((width, length), f32),
                pltpu.VMEM((bk, width), f32),
                pltpu.VMEM((bk, width), f32),
                pltpu.VMEM((8, length), f32),
            ],
        ),
        out_shape=jax.ShapeDtypeStruct((length, 3 * width), bf16),
        compiler_params=params(60),
        cost_estimate=pl.CostEstimate(
            flops=12 * length * length * width,
            bytes_accessed=length * width * 16,
            transcendentals=length * length * heads // 2,
        ),
        name="attend_back",
    )(place, q, k, v, do, o, lse, *tables, *deps)


def feed_kernel(ff, x0, x1, c0, c1, wgu_ref, wd_ref, *rest):
    hidden_ref, grad_ref, x_ref, c_ref = rest[-4:]
    which = pl.program_id(0)

    @pl.when(which == 0)
    def _():
        x_ref[...] = x0[...]
        c_ref[...] = c0[...]

    @pl.when(which == 1)
    def _():
        x_ref[...] = x1[...]
        c_ref[...] = c1[...]

    both = dot(x_ref[...], wgu_ref[...], NN)
    hidden_grad = dot(c_ref[...], wd_ref[...], NT)
    gate = both[:, :ff]
    up = both[:, ff:]
    open_ = jax.nn.sigmoid(gate)
    swished = gate * open_
    hidden_ref[...] = (swished * up).astype(bf16)
    grad_ref[:, :ff] = (hidden_grad * up * open_ * (1.0 + gate * (1.0 - open_))).astype(bf16)
    grad_ref[:, ff:] = (hidden_grad * swished).astype(bf16)


def feed_block(pair, cot_pair, gate_up, down, at, half, buffers, deps=()):
    rows = pair[0].shape[0]
    ff = down.shape[0]
    tile = min(256, rows)
    steps = rows // tile
    length = 2 * half * rows
    early = pl.BlockSpec((tile, D), lambda p, i: (jnp.where(p == 0, i, steps - 1), 0))
    late = pl.BlockSpec((tile, D), lambda p, i: (jnp.where(p == 0, 0, i), 0))
    operands = [pair[0], pair[1], cot_pair[0], cot_pair[1], gate_up, down]
    specs = [
        early,
        late,
        early,
        late,
        pl.BlockSpec((D, 2 * ff), lambda p, i: (0, 0)),
        pl.BlockSpec((ff, D), lambda p, i: (0, 0)),
    ]
    aliases = {}
    if buffers is not None:
        aliases = {len(operands) + n: n for n in range(4)}
        operands += list(buffers)
        specs += [pl.BlockSpec(memory_space=pl.ANY)] * 4

    def place(p, i):
        return ((p * half + at) * steps + i, 0)

    return launch(
        functools.partial(feed_kernel, ff),
        operands,
        specs,
        [
            shape_of((length, ff), bf16),
            shape_of((length, 2 * ff), bf16),
            shape_of((length, D), bf16),
            shape_of((length, D), bf16),
        ],
        [
            pl.BlockSpec((tile, ff), place),
            pl.BlockSpec((tile, 2 * ff), place),
            pl.BlockSpec((tile, D), place),
            pl.BlockSpec((tile, D), place),
        ],
        grid=(2, steps),
        aliases=aliases,
        deps=deps,
        cost=(12 * rows * D * ff, 6 * D * ff + rows * D * 16, 2 * rows * ff),
        name="feed_forward",
    )


def rotary_columns(length, width):
    half = ROT // 2
    indices = np.arange(half, dtype=np.float32)
    inverse = np.float32(1.0) / np.float32(10000.0) ** (indices * np.float32(2.0 / ROT))
    angles = np.arange(length, dtype=np.float32)[:, None] * inverse[None, :].astype(np.float32)
    cosine, sine = np.cos(angles.astype(np.float64)), np.sin(angles.astype(np.float64))
    rest = np.zeros((length, HEAD - ROT))
    none = np.zeros((length, half))
    one_head = (
        np.concatenate([cosine, cosine, rest + 1.0], -1),
        np.concatenate([-sine, none, rest], -1),
        np.concatenate([none, sine, rest], -1),
    )
    return tuple(jnp.asarray(np.tile(t, (1, width // HEAD)).astype(np.float32)) for t in one_head)


def swap_sp(value):
    return lax.all_to_all(value, "sp", split_axis=0, concat_axis=0, tiled=True)


def per_device(
    tokens, cotangent, first_gain, first_shift, joint_weight, joint_bias, out_weight, second_gain, second_shift,
    gate_weight, up_weight, down_weight,
):
    n_sp = lax.axis_size("sp")
    n_z = lax.axis_size("fsdp")
    n_all = n_sp * n_z
    plane = Plane(n_sp)
    half = plane.half
    me = lax.axis_index("sp")
    span = tokens.shape[1]
    length = n_sp * span
    width = D // n_sp
    depth = joint_weight.shape[0]
    ff_rows = down_weight.shape[0]
    unit = max(16, 128 // n_z)
    ff_pad = -(-ff_rows // unit) * unit
    ff = n_z * ff_pad

    order = jnp.asarray(plane.table)[me]
    place = jnp.asarray(np.argsort(plane.table, axis=1).astype(np.int32))[me]
    groups = 2 if width % 256 == 0 else 1
    group = width // groups
    my_z = lax.axis_index("fsdp")

    small = jnp.concatenate([first_gain, first_shift, second_gain, second_shift, joint_bias])
    small = jnp.broadcast_to(small[None], (n_all, small.shape[0]))
    small_all = lax.all_to_all(small, ("fsdp", "sp"), split_axis=0, concat_axis=0, tiled=True)
    small = small_all.astype(f32)
    n_gain = first_gain.shape[0]
    gain_one, shift_one, gain_two, shift_two = (
        small[:, i * n_gain : (i + 1) * n_gain].reshape(1, D) for i in range(4)
    )
    bias_all = small[:, 4 * n_gain :].reshape(3, n_sp, width)
    bias = lax.dynamic_index_in_dim(bias_all, me, axis=1, keepdims=False)
    bias = bias.reshape(3, groups, group).transpose(1, 0, 2).reshape(1, 3 * width)

    joint_blocks = [swap_sp(cut_joint(joint_weight, n_sp, groups)).reshape(n_sp * depth, 3 * width)]
    for _ in range(n_z - 1):
        joint_blocks.append(lax.ppermute(joint_blocks[-1], "fsdp", [(i, (i + 1) % n_z) for i in range(n_z)]))
    joint_mine = jnp.zeros((D, 3 * width), bf16)
    for step, block in enumerate(joint_blocks):
        at = lax.rem(my_z - step + n_z, n_z) * (n_sp * depth)
        joint_mine = lax.dynamic_update_slice(joint_mine, block, (at, 0))

    gate_up_cols = cut_feed(gate_weight, up_weight, n_sp, n_z, ff_pad, ())
    down_rows = jnp.pad(down_weight, ((0, ff_pad - ff_rows), (0, 0)))
    down = lax.all_gather(down_rows, "fsdp", axis=0, tiled=True)

    x = tokens.reshape(span, D)
    normed = None

    def norm_next(normed, block, t, deps=()):
        return norm_block(block, gain_one, shift_one, t, n_sp, normed, deps)

    partner, one, twos = plane.gather_first(held(x, (joint_blocks[0], small_all)))
    normed = norm_next(None, x, 0)
    normed = norm_next(normed, partner, half)
    one = held(one, (normed, joint_blocks[1:3], gate_up_cols))
    one_other, two_others, threes = plane.gather_second(one, twos)
    normed = norm_next(normed, one, 1)
    for n, two in enumerate(twos):
        normed = norm_next(normed, two, 2 + 2 * n)
    normed = norm_next(normed, one_other, half + 1)
    for n, two in enumerate(two_others):
        normed = norm_next(normed, two, half + 2 + 2 * n)
    threes = [held(three, (normed, joint_blocks[3:])) if n == 0 else three for n, three in enumerate(threes)]
    for n, three in enumerate(threes):
        normed = norm_next(normed, three, 3 + 2 * n)
    for n, three in enumerate(plane.gather_third(threes)):
        normed = norm_next(normed, three, half + 3 + 2 * n)
    tables = rotary_columns(length, group)
    heads = joint_projection(order, normed, joint_mine, bias, tables, span, groups)

    out_full = lax.all_gather(held(out_weight, threes), ("fsdp", "sp"), axis=0, tiled=True)
    ring = [(i, (i + 1) % n_z) for i in range(n_z)]
    gate_up_blocks = [held(swap_sp(held(gate_up_cols, threes)).reshape(n_sp * depth, 2 * ff), heads[0])]
    gate_up_blocks.append(lax.ppermute(gate_up_blocks[0], "fsdp", ring))
    cot = cotangent.reshape(span, D)
    cot_partner, cot_one, cot_twos = plane.gather_first(held(cot, gate_up_blocks[0]))
    results = [attend(*heads[:3])]
    cot_one = held(cot_one, results[0][1])
    gate_up_blocks[1] = held(gate_up_blocks[1], results[0][1])
    gate_up_blocks.append(lax.ppermute(gate_up_blocks[1], "fsdp", ring))
    cot_one_other, cot_two_others, cot_threes = plane.gather_second(cot_one, cot_twos)
    for g in range(1, groups):
        results.append(attend(*heads[3 * g : 3 * g + 3], (cot_partner, cot_one, cot_twos, gate_up_blocks[1])))
    cot_threes = [held(c, results[-1][1]) for c in cot_threes]
    gate_up_blocks[2] = held(gate_up_blocks[2], results[-1][1])
    for _ in range(3, n_z):
        gate_up_blocks.append(lax.ppermute(gate_up_blocks[-1], "fsdp", ring))
    cot_three_others = plane.gather_third(cot_threes)
    cot_blocks, cot_partners = [cot, cot_one], [cot_partner, cot_one_other]
    for pieces in zip(cot_twos, cot_threes):
        cot_blocks += pieces
    for pieces in zip(cot_two_others, cot_three_others):
        cot_partners += pieces
    gate_up = jnp.zeros((D, 2 * ff), bf16)
    for step, block in enumerate(gate_up_blocks):
        at = lax.rem(my_z - step + n_z, n_z) * (n_sp * depth)
        gate_up = lax.dynamic_update_slice(gate_up, block, (at, 0))
    attended = [swap_sp(o).reshape(n_sp, span, group) for o, _ in results]
    middle, normed_two, attended_all = middle_of(attended, out_full, x, gain_two, shift_two, gate_up_blocks[:3])

    feed = None

    def feed_next(feed, pair, t, deps=()):
        return feed_block(pair, (cot_blocks[t], cot_partners[t]), gate_up, down, t, half, feed, deps)

    partner, one, twos = plane.gather_first(normed_two)
    feed = feed_next(None, (normed_two, partner), 0, (cot_blocks, cot_partners))
    one = held(one, feed[0])
    one_other, two_others, threes = plane.gather_second(one, twos)
    feed = feed_next(feed, (one, one_other), 1)
    for n, two in enumerate(twos):
        feed = feed_next(feed, (two, two_others[n]), 2 + 2 * n)
        three = held(threes[n], feed[0]) if n == len(twos) - 1 else threes[n]
        feed = feed_next(feed, (three, plane.send(three, plane.core)), 3 + 2 * n)
    hidden, gate_up_grad, two_all, cot_all = feed

    two_product = product_of([gate_up_grad], gate_up, NT, span)
    out_product = product_of([hidden], down, NN, span)
    two_got = plane.reduce_far(two_product)
    two_theirs = plane.reduce_near(two_product)
    gate_up_sum = dot(two_all, gate_up_grad, TN).astype(bf16)
    down_sum = dot(hidden, cot_all, TN).astype(bf16)
    gate_up_part = lax.psum_scatter(gate_up_sum, "fsdp", scatter_dimension=0, tiled=True)
    down_part = lax.psum_scatter(down_sum, "fsdp", scatter_dimension=0, tiled=True)
    two_last = plane.reduce_next(two_product, two_got, two_theirs, (gate_up_sum, down_sum))
    two_grad = plane.reduce_own(two_product, two_got, two_theirs, two_last)
    middle_grad, two_sums, branch_grad, *parts = norm_back(
        two_grad, middle, gain_two, cotangent.reshape(span, D), out_full, n_sp, groups
    )
    dos = [swap_sp(part).reshape(n_sp * span, group) for part in parts]
    out_sum = dot(attended_all, branch_grad, TN).astype(bf16).reshape(n_z, n_sp, depth, D)

    def out_weight_part(start, stop, addends, dtype, deps=()):
        parts = [lax.dynamic_index_in_dim(out_sum, order[b], 1, False).reshape(n_z * depth, D) for b in range(start, stop)]
        total = jnp.stack(parts).astype(f32)
        for addend, at in addends:
            total += addend[at : at + stop - start].astype(f32)
        return total.astype(dtype)

    rows = attend_back(place, *heads[:3], dos[0], *results[0], tables, span, out_sum)
    joint_rows = [rows]
    joint_sums = [dot(normed, rows, TN).astype(bf16)]
    joint_parts = [lax.psum_scatter(joint_sums[0], "fsdp", scatter_dimension=0, tiled=True)]
    out_got = plane.reduce_far(out_product, branch_grad)
    out_theirs = plane.reduce_near(out_product, branch_grad)
    weight_got = plane.reduce_far(out_weight_part)
    weight_theirs = plane.reduce_near(out_weight_part)
    gate_up_own = swap_sp(gate_up_part)
    for g in range(1, groups):
        deps = (joint_sums, out_got, out_theirs, weight_got, weight_theirs, gate_up_own, down_part)
        rows = attend_back(place, *heads[3 * g : 3 * g + 3], dos[g], *results[g], tables, span, deps)
        joint_rows.append(rows)
        joint_sums.append(dot(normed, rows, TN).astype(bf16))
        joint_parts.append(lax.psum_scatter(joint_sums[g], "fsdp", scatter_dimension=0, tiled=True))
    out_last = plane.reduce_next(out_product, out_got, out_theirs)
    weight_last = plane.reduce_next(out_weight_part, weight_got, weight_theirs)

    normed_product = product_of(joint_rows, joint_mine, NT, span)
    normed_got = plane.reduce_far(normed_product, (out_last, weight_last, gate_up_own))
    normed_theirs = plane.reduce_near(normed_product)
    output = (middle + plane.reduce_own(out_product, out_got, out_theirs, out_last, f32)).astype(bf16)
    out_own = plane.reduce_own(out_weight_part, weight_got, weight_theirs, weight_last)
    out_grad = lax.psum_scatter(held(out_own, joint_parts), "fsdp", scatter_dimension=0, tiled=True).astype(f32)
    down_grad = down_part[:ff_rows].astype(f32)
    gate_grad, up_grad = join_feed(gate_up_own.reshape(n_sp, depth, 2 * ff), n_z, ff_rows, ff_pad)
    bias_sum = jnp.stack([jnp.sum(r.astype(f32), axis=0).reshape(3, group) for r in joint_rows], 1)
    bias_sum = bias_sum.reshape(3, 1, width)
    bias_sum = lax.dynamic_update_slice(jnp.zeros((3, n_sp, width), f32), bias_sum, (0, me, 0))
    joint_own = [swap_sp(j).reshape(n_sp, depth, 3 * group) for j in joint_parts]
    fill = (joint_sums, output, gate_grad, up_grad, bias_sum, joint_own[:-1])
    normed_last = plane.reduce_next(normed_product, normed_got, normed_theirs, fill)
    normed_grad = plane.reduce_own(normed_product, normed_got, normed_theirs, normed_last)
    tokens_grad, one_sums = norm_back(normed_grad, x, gain_one, middle_grad)
    tokens_grad = tokens_grad.reshape(tokens.shape)

    joint_grad = join_joint(joint_own, n_sp)

    sums = [one_sums[0], one_sums[1], two_sums[0], two_sums[1]]
    sums = jnp.concatenate([s.reshape(n_all, n_gain) for s in sums] + [bias_sum.reshape(n_all, -1)], axis=1)
    sums = jnp.sum(lax.all_to_all(sums, ("fsdp", "sp"), split_axis=0, concat_axis=0, tiled=True), axis=0)
    gain_one_grad, shift_one_grad, gain_two_grad, shift_two_grad = (
        sums[i * n_gain : (i + 1) * n_gain] for i in range(4)
    )
    return (
        output.reshape(tokens.shape),
        tokens_grad,
        gain_one_grad,
        shift_one_grad,
        joint_grad,
        sums[4 * n_gain :],
        out_grad,
        gain_two_grad,
        shift_two_grad,
        gate_grad,
        up_grad,
        down_grad,
    )


def solution(mesh):
    rows = P("fsdp", "sp", None)
    vector = P(("fsdp", "sp"))
    matrix = P(("fsdp", "sp"), None)
    return jax.shard_map(
        per_device,
        mesh=mesh,
        in_specs=(rows, rows, vector, vector, matrix, vector, matrix, vector, vector, matrix, matrix, matrix),
        out_specs=(rows, rows, vector, vector, matrix, vector, matrix, vector, vector, matrix, matrix, matrix),
        check_vma=False,
    )
```

```python
import functools
import math

import jax
import jax.numpy as jnp
import numpy as np
from jax import lax
from jax.experimental import pallas as pl
from jax.experimental.pallas import tpu as pltpu
from jax.sharding import PartitionSpec as P

D = 2048
HEADS = 32
HEAD = 64
ROT = 16

epsilon = 1e-05
masked_value = -1e30
f32 = jnp.float32
bf16 = jnp.bfloat16
LOG2E_SCALE = math.log2(math.e) * HEAD**-0.5
NN = (((1,), (0,)), ((), ()))
NT = (((1,), (1,)), ((), ()))
TN = (((0,), (0,)), ((), ()))


def dot(a, b, dims):
    return lax.dot_general(a, b, dims, preferred_element_type=f32)


def params(mib=56):
    return pltpu.CompilerParams(vmem_limit_bytes=mib * 2**20)


class Plane:
    def __init__(self, count):
        outer = count // 4
        self.count = count
        self.outer = outer

        def spot(o, i, c):
            return ((o % outer) * 2 + i) * 2 + c

        def split(s):
            return s // 4, (s // 2) % 2, s % 2

        self.core = [(s, s ^ 1) for s in range(count)]
        first = []
        later = [[] for _ in range(outer - 1)]
        for s in range(count):
            o, i, c = split(s)
            swapped = outer == 2 and c == 1
            first.append((s, spot(o + 1, i, c) if swapped else spot(o, 1 - i, c)))
            for k in range(1, outer):
                later[k - 1].append((s, spot(o, 1 - i, c) if swapped else spot(o + k, i, c)))
        self.first = first
        self.later = later
        here = list(range(count))

        def moved(table, perm):
            out = [None] * count
            for a, b in perm:
                out[b] = table[a]
            return out

        blocks = [here, moved(here, first)]
        for perm in later:
            blocks += [moved(blocks[0], perm), moved(blocks[1], perm)]
        blocks += [moved(b, self.core) for b in blocks]
        self.table = np.array(blocks, np.int32).T
        self.half = 2 * outer
        self.far = list(reversed(range(2, self.half, 2)))

    @staticmethod
    def send(value, perm):
        return lax.ppermute(value, "sp", perm)

    @staticmethod
    def back(value, perm):
        return lax.ppermute(value, "sp", [(b, a) for a, b in perm])

    def gather_first(self, value):
        return (
            self.send(value, self.core),
            self.send(value, self.first),
            [self.send(value, perm) for perm in self.later],
        )

    def gather_second(self, one, twos):
        return (
            self.send(one, self.core),
            [self.send(two, self.core) for two in twos],
            [self.send(one, perm) for perm in self.later],
        )

    def gather_third(self, threes):
        return [self.send(three, self.core) for three in threes]


    def reduce_sums(self, product, deps=(), apart=False):
        far = [product(self.half + start, self.half + start + 2, (), bf16, deps) for start in self.far]
        near = product(self.half, self.half + 2, (), bf16, far)
        theirs = [self.send(value, self.core) for value in far]
        more = (True,) if apart else ()
        sums = [product(start, start + 2, ((value, 0),), bf16, near, *more) for start, value in zip(self.far, theirs)]
        return sums, self.send(near, self.core)

    def reduce_leg(self, sums):
        return [self.back(value, self.later[start // 2 - 1]) for start, value in zip(self.far, sums)]

    def reduce_next(self, product, got, theirs, deps=()):
        one = product(1, 2, tuple((t, 1) for t in [theirs] + got), bf16, deps)
        return one, self.back(one, self.first)

    def reduce_own(self, product, got, theirs, last, dtype=bf16, deps=()):
        return product(0, 1, tuple((t, 0) for t in [theirs] + got + [last]), dtype, deps)[0]


    def legs(self, sums):
        perms = [self.later[start // 2 - 1] for start in self.far]
        further = [self.back(pair[1], perm) for pair, perm in zip(sums, perms)]
        nearer = [self.back(held(pair[0], further), perm) for pair, perm in zip(sums, perms)]
        return further, nearer

    def legs_next(self, product, further, theirs, deps=()):
        one = product(1, 2, ((theirs, 1), *((t, 0) for t in further)), bf16, deps)
        return one, self.back(one, self.first)

    def legs_own(self, product, nearer, theirs, last, deps=()):
        return product(0, 1, ((theirs, 0), *((t, 0) for t in [*nearer, last])), bf16, deps)[0]


def launch(
    kernel, operands, in_specs, outs, out_specs, *, grid, name, cost, scratch=(), deps=(), aliases=None, prefetch=0, mib=60
):
    deps = jax.tree.leaves(deps)
    count = len(operands)

    def body(*refs):
        kernel(*refs[:count], *refs[count + len(deps) :])

    flops, moved, transcendentals = cost
    return pl.pallas_call(
        body,
        grid_spec=pltpu.PrefetchScalarGridSpec(
            num_scalar_prefetch=prefetch,
            grid=grid,
            in_specs=list(in_specs) + [pl.BlockSpec(memory_space=pl.ANY)] * len(deps),
            out_specs=list(out_specs),
            scratch_shapes=list(scratch),
        ),
        out_shape=list(outs),
        input_output_aliases=aliases or {},
        compiler_params=pltpu.CompilerParams(vmem_limit_bytes=mib * 2**20),
        cost_estimate=pl.CostEstimate(flops=int(flops), bytes_accessed=int(moved), transcendentals=int(transcendentals)),
        name=name,
    )(*operands, *deps)


ANYWHERE = pl.BlockSpec(memory_space=pl.ANY)


def held(value, deps):
    return launch(
        lambda *refs: None, [value], [ANYWHERE], [shape_of(value.shape, value.dtype)], [ANYWHERE],
        grid=(1,), aliases={0: 0}, deps=deps, cost=(0, 0, 0), name="held",
    )[0]


def whole(shape):
    return pl.BlockSpec(shape, lambda *_: (0,) * len(shape))


def shape_of(shape, dtype):
    return jax.ShapeDtypeStruct(shape, dtype)


def product_kernel(terms, dims, pieces, *refs):
    outs = refs[-pieces:]
    each, rows, width = outs[0].shape
    count = each * pieces
    total = dot(refs[0][...], refs[terms][...], dims)
    for t in range(1, terms):
        total += dot(refs[t][...], refs[terms + t][...], dims)
    for ref in refs[2 * terms : -pieces]:
        total += ref[...].astype(f32).reshape(count * rows, width)
    total = total.reshape(pieces, each, rows, width)
    for n, out_ref in enumerate(outs):
        out_ref[...] = total[n].astype(out_ref.dtype)


def product_of(lefts, right, dims, span):
    tile = 512
    depth = sum(left.shape[1] for left in lefts)

    def right_at(at, left):
        if dims is NT:
            return pl.BlockSpec((tile, left.shape[1]), lambda i: (i, at))
        return pl.BlockSpec((left.shape[1], tile), lambda i: (at, i))

    def product(start, stop, addends, dtype, deps=(), apart=False):
        count = stop - start
        pieces = count if apart else 1
        assert start % count == 0 and all(at % count == 0 for _, at in addends)

        def columns(at):
            return pl.BlockSpec((count, span, tile), lambda i: (at // count, 0, i))

        values = launch(
            functools.partial(product_kernel, len(lefts), dims, pieces),
            [*lefts, *[right] * len(lefts), *(value for value, _ in addends)],
            [pl.BlockSpec((count * span, a.shape[1]), lambda i: (start // count, 0)) for a in lefts]
            + [right_at(t, left) for t, left in enumerate(lefts)]
            + [columns(at) for _, at in addends],
            [shape_of((count // pieces, span, D), dtype)] * pieces,
            [pl.BlockSpec((count // pieces, span, tile), lambda i: (0, 0, i))] * pieces,
            grid=(D // tile,),
            deps=deps,
            mib=60,
            cost=(2 * count * span * D * depth, 2 * depth * (D + count * span) + 4 * count * span * D, 0),
            name="block_product",
        )
        return values if apart else values[0]

    return product


def norm_kernel(x_ref, gain_ref, shift_ref, *rest):
    out_ref = rest[-1]
    values = x_ref[...].astype(f32)
    center = values - jnp.mean(values, axis=-1, keepdims=True)
    spread = jnp.mean(center * center, axis=-1, keepdims=True)
    out_ref[...] = (center * lax.rsqrt(spread + epsilon) * gain_ref[...] + shift_ref[...]).astype(bf16)


def norm_block(x, gain, shift, at, blocks, buffer, deps=()):
    rows = x.shape[0]
    tile = min(256, rows)
    steps = rows // tile
    row = pl.BlockSpec((1, D), lambda i: (0, 0))
    held = [] if buffer is None else [buffer]
    return launch(
        norm_kernel,
        [x, gain, shift, *held],
        [pl.BlockSpec((tile, D), lambda i: (i, 0)), row, row, *[ANYWHERE] * len(held)],
        [shape_of((blocks * rows, D), bf16)],
        [pl.BlockSpec((tile, D), lambda i: (at * steps + i, 0))],
        grid=(steps,),
        aliases={3: 0} if held else {},
        deps=deps,
        mib=60,
        cost=(rows * D * 12, rows * D * 4, rows),
        name="first_norm",
    )[0]


def cut_joint_kernel(n_sp, groups, group, in_ref, out_ref):
    for j in range(n_sp):
        for g in range(groups):
            for m in range(3):
                to = (g * 3 + m) * group
                start = m * D + (j * groups + g) * group
                out_ref[j, :, to : to + group] = in_ref[:, start : start + group]


def cut_joint(weight, n_sp, groups):
    depth = weight.shape[0]
    width = D // n_sp
    return launch(
        functools.partial(cut_joint_kernel, n_sp, groups, width // groups),
        [weight], [whole(weight.shape)], [shape_of((n_sp, depth, 3 * width), bf16)], [whole((n_sp, depth, 3 * width))],
        grid=(1,), cost=(0, weight.size * 4, 0), name="cut_joint",
    )[0]


def join_joint_kernel(n_sp, groups, group, *refs):
    out_ref = refs[-1]
    for j in range(n_sp):
        for g in range(groups):
            for m in range(3):
                start = m * D + (j * groups + g) * group
                out_ref[:, start : start + group] = refs[g][j, :, m * group : (m + 1) * group].astype(f32)


def join_joint(parts, n_sp):
    groups = len(parts)
    depth = parts[0].shape[1]
    return launch(
        functools.partial(join_joint_kernel, n_sp, groups, parts[0].shape[2] // 3),
        parts, [whole(p.shape) for p in parts], [shape_of((depth, 3 * D), f32)], [whole((depth, 3 * D))],
        grid=(1,), cost=(0, depth * D * 18, 0), name="join_joint",
    )[0]


def cut_feed_kernel(n_sp, n_z, size, padded, gate_ref, up_ref, out_ref):
    out_ref[...] = jnp.zeros_like(out_ref)
    for j in range(n_sp):
        for p, ref in enumerate((gate_ref, up_ref)):
            for z in range(n_z):
                start = (z * n_sp + j) * size
                to = (p * n_z + z) * padded
                out_ref[j, :, to : to + size] = ref[:, start : start + size]


def cut_feed(gate_weight, up_weight, n_sp, n_z, padded, deps):
    depth, total = gate_weight.shape
    size = total // (n_sp * n_z)
    shape = (n_sp, depth, 2 * n_z * padded)
    return launch(
        functools.partial(cut_feed_kernel, n_sp, n_z, size, padded),
        [gate_weight, up_weight], [whole(gate_weight.shape)] * 2, [shape_of(shape, bf16)], [whole(shape)],
        grid=(1,), cost=(0, gate_weight.size * 8, 0), name="cut_feed", deps=deps,
    )[0]


def join_feed_kernel(n_sp, n_z, size, padded, in_ref, gate_ref, up_ref):
    for p, ref in enumerate((gate_ref, up_ref)):
        for z in range(n_z):
            for j in range(n_sp):
                start = (z * n_sp + j) * size
                to = (p * n_z + z) * padded
                ref[:, start : start + size] = in_ref[j, :, to : to + size].astype(f32)


def join_feed(value, n_z, size, padded):
    n_sp, depth, _ = value.shape
    shape = (depth, n_sp * n_z * size)
    return launch(
        functools.partial(join_feed_kernel, n_sp, n_z, size, padded),
        [value], [whole(value.shape)], [shape_of(shape, f32)] * 2, [whole(shape)] * 2,
        grid=(1,), cost=(0, value.size * 6, 0), name="join_feed",
    )


def norm_back_kernel(depth, n_parts, *refs):
    grad_ref, x_ref, gain_ref, beside_ref = refs[:4]
    weights = refs[4 : 4 + n_parts]
    outs = refs[4 + n_parts :]
    result_ref, sums_ref = outs[0], outs[1]
    values = x_ref[...].astype(f32)
    center = values - jnp.mean(values, axis=-1, keepdims=True)
    spread = jnp.mean(center * center, axis=-1, keepdims=True)
    inverse = lax.rsqrt(spread + epsilon)
    xhat = center * inverse
    grad = grad_ref[...].astype(f32)
    scaled = grad * gain_ref[...]
    level = jnp.mean(scaled, axis=-1, keepdims=True)
    along = jnp.mean(scaled * xhat, axis=-1, keepdims=True)
    result = beside_ref[...].astype(f32) + inverse * (scaled - level - xhat * along)
    result_ref[...] = result

    @pl.when(pl.program_id(0) == 0)
    def _():
        sums_ref[...] = jnp.zeros_like(sums_ref)

    sums_ref[0:1] += jnp.sum(grad * xhat, axis=0, keepdims=True)
    sums_ref[1:2] += jnp.sum(grad, axis=0, keepdims=True)
    if n_parts:
        branch = result.astype(bf16)
        outs[2][...] = branch
        parts = outs[3:]
        full = dot(branch, weights[0][...], NT).astype(bf16)
        for place, g, j, columns in head_pieces(parts[0].shape[0], depth, len(parts)):
            parts[g][j, :, columns] = full[:, place]


def norm_back(grad, x, gain, beside, weight=None, depth=0, n_sp=0, groups=0):
    rows = x.shape[0]
    tile = min(256, rows)
    row = pl.BlockSpec((1, D), lambda i: (0, 0))
    block = pl.BlockSpec((tile, D), lambda i: (i, 0))
    outs = [shape_of((rows, D), f32), shape_of((8, D), f32)]
    out_specs = [block, whole((8, D))]
    extra, specs = [], []
    if weight is not None:
        group = D // n_sp // groups
        extra, specs = [weight], [whole((D, D))]
        outs += [shape_of((rows, D), bf16)] + [shape_of((n_sp, rows, group), bf16)] * groups
        out_specs += [block] + [pl.BlockSpec((n_sp, tile, group), lambda i: (0, i, 0))] * groups
    return launch(
        functools.partial(norm_back_kernel, depth, len(extra)),
        [grad, x, gain, beside, *extra],
        [block, block, row, block, *specs],
        outs,
        out_specs,
        grid=(rows // tile,),
        cost=(rows * D * (20 + 2 * D * len(extra)), rows * D * 16 + 2 * D * D * len(extra), rows),
        name="norm_back",
    )


def head_pieces(n_sp, depth, groups):
    group = D // n_sp // groups
    n_z = D // n_sp // depth
    for z in range(n_z):
        for s in range(n_sp):
            j, rest = divmod((z * n_sp + s) * depth, groups * group)
            g, column = divmod(rest, group)
            yield slice((s * n_z + z) * depth, (s * n_z + z + 1) * depth), g, j, slice(column, column + depth)


def middle_kernel(groups, n_sp, depth, *refs):
    parts, (out_w, x_ref, gain_ref, shift_ref) = refs[:groups], refs[groups : groups + 4]
    middle_ref, normed_ref, again_ref, attended_ref = refs[groups + 4 :]
    for to, g, j, columns in head_pieces(n_sp, depth, groups):
        attended_ref[:, to] = parts[g][j, :, columns]
    values = x_ref[...].astype(f32) + dot(attended_ref[...], out_w[...], NN)
    middle_ref[...] = values
    center = values - jnp.mean(values, axis=-1, keepdims=True)
    spread = jnp.mean(center * center, axis=-1, keepdims=True)
    normed = (center * lax.rsqrt(spread + epsilon) * gain_ref[...] + shift_ref[...]).astype(bf16)
    normed_ref[...] = normed
    again_ref[...] = normed


def middle_of(parts, out_w, depth, x, gain, shift, deps=()):
    n_sp, rows, group = parts[0].shape
    tile = min(256, rows)
    row = pl.BlockSpec((1, D), lambda i: (0, 0))
    block = pl.BlockSpec((tile, D), lambda i: (i, 0))
    return launch(
        functools.partial(middle_kernel, len(parts), n_sp, depth),
        [*parts, out_w, x, gain, shift],
        [pl.BlockSpec((n_sp, tile, group), lambda i: (0, i, 0))] * len(parts)
        + [pl.BlockSpec((D, D), lambda i: (0, 0)), block, row, row],
        [shape_of((rows, D), f32)] + [shape_of((rows, D), bf16)] * 3,
        [block] * 4,
        grid=(rows // tile,),
        deps=deps,
        cost=(2 * rows * D * D, 2 * D * D + rows * D * 12, rows),
        name="middle",
    )


def turn(values, cosine, sine_up, sine_down):
    width = values.shape[1]
    half = ROT // 2
    return (
        values * cosine
        + pltpu.roll(values, width - half, 1) * sine_up
        + pltpu.roll(values, half, 1) * sine_down
    )


def joint_kernel(width, table_ref, x_ref, w_ref, bias_ref, cos_ref, up_ref, down_ref, *outs):
    projected = dot(x_ref[...], w_ref[...], NN) + bias_ref[...]
    tables = (cos_ref[...], up_ref[...], down_ref[...])
    for g in range(len(outs) // 3):
        part = projected[:, 3 * g * width : 3 * (g + 1) * width]
        outs[3 * g][...] = turn(part[:, :width], *tables).astype(bf16)
        outs[3 * g + 1][...] = turn(part[:, width : 2 * width], *tables).astype(bf16)
        outs[3 * g + 2][...] = part[:, 2 * width :].astype(bf16)


def joint_projection(table, normed, weight, bias, tables, span, groups):
    length = normed.shape[0]
    total = weight.shape[1]
    width = total // 3 // groups
    placed = pl.BlockSpec((span, width), lambda b, t: (t[b], 0))
    return pl.pallas_call(
        functools.partial(joint_kernel, width),
        grid_spec=pltpu.PrefetchScalarGridSpec(
            num_scalar_prefetch=1,
            grid=(length // span,),
            in_specs=[
                pl.BlockSpec((span, D), lambda b, t: (b, 0)),
                pl.BlockSpec((D, total), lambda b, t: (0, 0)),
                pl.BlockSpec((1, total), lambda b, t: (0, 0)),
                placed,
                placed,
                placed,
            ],
            out_specs=[placed] * (3 * groups),
        ),
        out_shape=[jax.ShapeDtypeStruct((length, width), bf16)] * (3 * groups),
        compiler_params=params(),
        cost_estimate=pl.CostEstimate(
            flops=2 * length * D * total, bytes_accessed=length * (D + total) * 2, transcendentals=0
        ),
        name="joint_projection",
    )(table, normed, weight, bias, *tables)


def attend_kernel(heads, bq, bk, q_ref, k_ref, v_ref, o_ref, lse_ref, qm, vt, acc, m_s, l_s):
    i = pl.program_id(0)
    length, width = k_ref.shape
    lane = lax.broadcasted_iota(jnp.int32, (1, width), 1) // HEAD

    @pl.when(i == 0)
    def _():
        def flip(b, carry):
            rows = pl.ds(pl.multiple_of(b * bk, bk), bk)
            vt[:, rows] = jnp.transpose(v_ref[rows, :])
            return carry

        lax.fori_loop(0, length // bk, flip, 0)

    q = q_ref[...]
    for h in range(heads):
        qm[h] = jnp.where(lane == h, q, jnp.zeros_like(q))
    acc[...] = jnp.zeros_like(acc)
    m_s[...] = jnp.full_like(m_s, masked_value)
    l_s[...] = jnp.zeros_like(l_s)

    def body(j, masked):
        rows = pl.ds(pl.multiple_of(j * bk, bk), bk)
        k = k_ref[rows, :]
        scores = [dot(k, qm[h], NT) for h in range(heads)]
        if masked:
            key_at = lax.broadcasted_iota(jnp.int32, scores[0].shape, 0) + j * bk
            query_at = lax.broadcasted_iota(jnp.int32, scores[0].shape, 1) + i * bq
            scores = [jnp.where(key_at <= query_at, s, masked_value) for s in scores]
        m0 = m_s[...]
        l0 = l_s[...]
        m1 = jnp.maximum(m0, jnp.concatenate([jnp.max(s, axis=0, keepdims=True) for s in scores] + [m0[heads:]], 0))
        m_s[...] = m1
        kept = jnp.exp2((m0 - m1) * LOG2E_SCALE)
        base = m1 * LOG2E_SCALE
        raised = [jnp.exp2(scores[h] * LOG2E_SCALE - base[h : h + 1]) for h in range(heads)]
        l_s[...] = l0 * kept + jnp.concatenate([jnp.sum(p, axis=0, keepdims=True) for p in raised] + [l0[heads:]], 0)
        for h in range(heads):
            part = slice(h * HEAD, (h + 1) * HEAD)
            acc[part, :] = acc[part, :] * kept[h : h + 1] + dot(vt[part, rows], raised[h].astype(bf16), NN)

    whole = (i * bq) // bk
    lax.fori_loop(0, whole, lambda j, c: (body(j, False), c)[1], 0)
    for d in range(max(1, bq // bk)):
        body(whole + d, True)
    for h in range(heads):
        part = slice(h * HEAD, (h + 1) * HEAD)
        acc[part, :] = acc[part, :] * (1.0 / l_s[h : h + 1])
    o_ref[...] = jnp.transpose(acc[...].astype(bf16))
    lse_ref[...] = m_s[...] * LOG2E_SCALE + jnp.log2(l_s[...])


def attend(q, k, v, deps=()):
    length, width = q.shape
    heads = width // HEAD
    bq, bk = min(1024, length), min(512, length)
    full = pl.BlockSpec((length, width), lambda i: (0, 0))
    return launch(
        functools.partial(attend_kernel, heads, bq, bk),
        [q, k, v],
        [pl.BlockSpec((bq, width), lambda i: (i, 0)), full, full],
        [shape_of((length, width), bf16), shape_of((8, length), f32)],
        [pl.BlockSpec((bq, width), lambda i: (i, 0)), pl.BlockSpec((8, bq), lambda i: (0, i))],
        grid=(length // bq,),
        scratch=[
            pltpu.VMEM((heads, bq, width), bf16),
            pltpu.VMEM((width, length), bf16),
            pltpu.VMEM((width, bq), f32),
            pltpu.VMEM((8, bq), f32),
            pltpu.VMEM((8, bq), f32),
        ],
        deps=deps,
        cost=(8 * length * length * width, length * width * 8, length * length * heads // 2),
        name="attend",
    )


def attend_back_kernel(
    heads, bq, bk, place_ref, q_ref, k_ref, v_ref, do_ref, o_ref, lse_ref, cos_ref, up_ref, down_ref, out_ref,
    dq_acc, dk_acc, dv_acc, delta,
):
    j = pl.program_id(0)
    length, width = q_ref.shape
    lane = lax.broadcasted_iota(jnp.int32, (1, width), 1) // HEAD

    @pl.when(j == 0)
    def _():
        dq_acc[...] = jnp.zeros_like(dq_acc)
        pick = (
            lax.broadcasted_iota(jnp.int32, (8, width), 0) == lax.broadcasted_iota(jnp.int32, (8, width), 1) // HEAD
        ).astype(f32)

        def sums(b, carry):
            rows = pl.ds(pl.multiple_of(b * bq, bq), bq)
            both = do_ref[rows, :].astype(f32) * o_ref[rows, :].astype(f32)
            delta[:, rows] = lax.dot_general(
                pick, both, NT, precision=lax.Precision.HIGHEST, preferred_element_type=f32
            )
            return carry

        lax.fori_loop(0, length // bq, sums, 0)

    key_rows = pl.ds(pl.multiple_of(j * bk, bk), bk)
    k = k_ref[key_rows, :]
    v = v_ref[key_rows, :]
    kt = jnp.transpose(k)
    dk_acc[...] = jnp.zeros_like(dk_acc)
    dv_acc[...] = jnp.zeros_like(dv_acc)

    def body(i, masked):
        rows = pl.ds(pl.multiple_of(i * bq, bq), bq)
        q = q_ref[rows, :]
        do = do_ref[rows, :]
        probs, grads, queries, results = [], [], [], []
        for h in range(heads):
            qh = jnp.where(lane == h, q, jnp.zeros_like(q))
            doh = jnp.where(lane == h, do, jnp.zeros_like(do))
            s = dot(k, qh, NT)
            p = jnp.exp2(s * LOG2E_SCALE - lse_ref[h : h + 1, rows])
            if masked:
                key_at = lax.broadcasted_iota(jnp.int32, s.shape, 0) + j * bk
                query_at = lax.broadcasted_iota(jnp.int32, s.shape, 1) + i * bq
                p = jnp.where(key_at <= query_at, p, 0.0)
            dp = dot(v, doh, NT)
            ds = p * (dp - delta[h : h + 1, rows])
            probs.append(p.astype(bf16))
            grads.append(ds.astype(bf16))
            queries.append(qh)
            results.append(doh)
        dv_acc[...] += dot(jnp.concatenate(probs, 1), jnp.concatenate(results, 0), NN)
        dk_acc[...] += dot(jnp.concatenate(grads, 1), jnp.concatenate(queries, 0), NN)
        for h in range(heads):
            part = slice(h * HEAD, (h + 1) * HEAD)
            dq_acc[part, rows] += dot(kt[part], grads[h], NN)

    first = (j * bk) // bq
    near = max(1, bk // bq)
    for d in range(near):
        body(first + d, True)
    lax.fori_loop(first + near, length // bq, lambda i, c: (body(i, False), c)[1], 0)
    scale = HEAD**-0.5
    tables = (cos_ref[...], -up_ref[...], -down_ref[...])
    dq = (jnp.transpose(dq_acc[:, key_rows]) * scale).astype(bf16).astype(f32)
    dk = (dk_acc[...] * scale).astype(bf16).astype(f32)
    out_ref[:, :width] = turn(dq, *tables).astype(bf16)
    out_ref[:, width : 2 * width] = turn(dk, *tables).astype(bf16)
    out_ref[:, 2 * width :] = dv_acc[...].astype(bf16)


def attend_back(place, q, k, v, do, o, lse, tables, span, deps=()):
    length, width = q.shape
    heads = width // HEAD
    bq = min(512, length)
    bk = span
    full = pl.BlockSpec((length, width), lambda i, t: (0, 0))
    block = pl.BlockSpec((bk, width), lambda i, t: (i, 0))
    return launch(
        functools.partial(attend_back_kernel, heads, bq, bk),
        [place, q, k, v, do, o, lse, *tables],
        [full] * 5 + [pl.BlockSpec((8, length), lambda i, t: (0, 0))] + [block] * 3,
        [shape_of((length, 3 * width), bf16)],
        [pl.BlockSpec((bk, 3 * width), lambda i, t: (t[i], 0))],
        grid=(length // bk,),
        prefetch=1,
        scratch=[
            pltpu.VMEM((width, length), f32),
            pltpu.VMEM((bk, width), f32),
            pltpu.VMEM((bk, width), f32),
            pltpu.VMEM((8, length), f32),
        ],
        deps=deps,
        cost=(12 * length * length * width, length * width * 16, length * length * heads // 2),
        name="attend_back",
    )[0]


def feed_kernel(ff, x0, x1, c0, c1, wgu_ref, wd_ref, *rest):
    hidden_ref, grad_ref, x_ref, c_ref = rest[-4:]
    which = pl.program_id(0)

    @pl.when(which == 0)
    def _():
        x_ref[...] = x0[...]
        c_ref[...] = c0[...]

    @pl.when(which == 1)
    def _():
        x_ref[...] = x1[...]
        c_ref[...] = c1[...]

    both = dot(x_ref[...], wgu_ref[...], NN)
    hidden_grad = dot(c_ref[...], wd_ref[...], NT)
    gate = both[:, :ff]
    up = both[:, ff:]
    open_ = jax.nn.sigmoid(gate)
    swished = gate * open_
    hidden_ref[...] = (swished * up).astype(bf16)
    grad_ref[:, :ff] = (hidden_grad * up * open_ * (1.0 + gate * (1.0 - open_))).astype(bf16)
    grad_ref[:, ff:] = (hidden_grad * swished).astype(bf16)


def feed_block(pair, cot_pair, gate_up, down, at, half, buffers, deps=()):
    rows = pair[0].shape[0]
    ff = down.shape[0]
    tile = min(256, rows)
    steps = rows // tile
    length = 2 * half * rows
    early = pl.BlockSpec((tile, D), lambda p, i: (jnp.where(p == 0, i, steps - 1), 0))
    late = pl.BlockSpec((tile, D), lambda p, i: (jnp.where(p == 0, 0, i), 0))
    operands = [pair[0], pair[1], cot_pair[0], cot_pair[1], gate_up, down]
    specs = [
        early,
        late,
        early,
        late,
        pl.BlockSpec((D, 2 * ff), lambda p, i: (0, 0)),
        pl.BlockSpec((ff, D), lambda p, i: (0, 0)),
    ]
    aliases = {}
    if buffers is not None:
        aliases = {len(operands) + n: n for n in range(4)}
        operands += list(buffers)
        specs += [pl.BlockSpec(memory_space=pl.ANY)] * 4

    def place(p, i):
        return ((p * half + at) * steps + i, 0)

    return launch(
        functools.partial(feed_kernel, ff),
        operands,
        specs,
        [
            shape_of((length, ff), bf16),
            shape_of((length, 2 * ff), bf16),
            shape_of((length, D), bf16),
            shape_of((length, D), bf16),
        ],
        [
            pl.BlockSpec((tile, ff), place),
            pl.BlockSpec((tile, 2 * ff), place),
            pl.BlockSpec((tile, D), place),
            pl.BlockSpec((tile, D), place),
        ],
        grid=(2, steps),
        aliases=aliases,
        deps=deps,
        cost=(12 * rows * D * ff, 6 * D * ff + rows * D * 16, 2 * rows * ff),
        name="feed_forward",
    )


def rotary_columns(length, width):
    half = ROT // 2
    indices = np.arange(half, dtype=np.float32)
    inverse = np.float32(1.0) / np.float32(10000.0) ** (indices * np.float32(2.0 / ROT))
    angles = np.arange(length, dtype=np.float32)[:, None] * inverse[None, :].astype(np.float32)
    cosine, sine = np.cos(angles.astype(np.float64)), np.sin(angles.astype(np.float64))
    rest = np.zeros((length, HEAD - ROT))
    none = np.zeros((length, half))
    one_head = (
        np.concatenate([cosine, cosine, rest + 1.0], -1),
        np.concatenate([-sine, none, rest], -1),
        np.concatenate([none, sine, rest], -1),
    )
    return tuple(jnp.asarray(np.tile(t, (1, width // HEAD)).astype(np.float32)) for t in one_head)


def swap_sp(value):
    return lax.all_to_all(value, "sp", split_axis=0, concat_axis=0, tiled=True)


def in_line(blocks, mine):
    count, rows = len(blocks), blocks[0].shape[0]
    total = jnp.zeros((count * rows, blocks[0].shape[1]), blocks[0].dtype)
    for step, block in enumerate(blocks):
        total = lax.dynamic_update_slice(total, block, (lax.rem(mine - step + count, count) * rows, 0))
    return total


def per_device(
    tokens, cotangent, first_gain, first_shift, joint_weight, joint_bias, out_weight, second_gain, second_shift,
    gate_weight, up_weight, down_weight,
):
    n_sp = lax.axis_size("sp")
    n_z = lax.axis_size("fsdp")
    n_all = n_sp * n_z
    plane = Plane(n_sp)
    half = plane.half
    me = lax.axis_index("sp")
    span = tokens.shape[1]
    length = n_sp * span
    width = D // n_sp
    depth = joint_weight.shape[0]
    ff_rows = down_weight.shape[0]
    unit = max(16, 128 // n_z)
    ff_pad = -(-ff_rows // unit) * unit
    ff = n_z * ff_pad

    order = jnp.asarray(plane.table)[me]
    place = jnp.asarray(np.argsort(plane.table, axis=1).astype(np.int32))[me]
    groups = 2 if width % 256 == 0 else 1
    group = width // groups
    my_z = lax.axis_index("fsdp")

    small = jnp.concatenate([first_gain, first_shift, second_gain, second_shift, joint_bias])
    small = jnp.broadcast_to(small[None], (n_all, small.shape[0]))
    small_all = lax.all_to_all(small, ("fsdp", "sp"), split_axis=0, concat_axis=0, tiled=True)
    small = small_all.astype(f32)
    n_gain = first_gain.shape[0]
    gain_one, shift_one, gain_two, shift_two = (
        small[:, i * n_gain : (i + 1) * n_gain].reshape(1, D) for i in range(4)
    )
    bias_all = small[:, 4 * n_gain :].reshape(3, n_sp, width)
    bias = lax.dynamic_index_in_dim(bias_all, me, axis=1, keepdims=False)
    bias = bias.reshape(3, groups, group).transpose(1, 0, 2).reshape(1, 3 * width)

    ring = [(i, (i + 1) % n_z) for i in range(n_z)]
    joint_block = swap_sp(cut_joint(joint_weight, n_sp, groups)).reshape(n_sp * depth, 3 * width)
    out_blocks = [out_weight]
    for _ in range(n_z - 1):
        out_blocks.append(lax.ppermute(out_blocks[-1], "fsdp", ring))
    out_rows = in_line(out_blocks, my_z)
    joint_blocks = [held(joint_block, out_blocks[1:])]
    for _ in range(n_z - 1):
        joint_blocks.append(lax.ppermute(joint_blocks[-1], "fsdp", ring))
    joint_mine = in_line(joint_blocks, my_z)

    gate_up_cols = cut_feed(gate_weight, up_weight, n_sp, n_z, ff_pad, ())
    down_rows = jnp.pad(down_weight, ((0, ff_pad - ff_rows), (0, 0)))
    x = tokens.reshape(span, D)
    normed = None

    def norm_next(normed, block, t, deps=()):
        return norm_block(block, gain_one, shift_one, t, n_sp, normed, deps)

    partner, one, twos = plane.gather_first(x)
    normed = norm_next(None, x, 0)
    normed = norm_next(normed, partner, half)
    one = held(one, (normed, joint_blocks[1:3], gate_up_cols))
    one_other, two_others, threes = plane.gather_second(one, twos)
    normed = norm_next(normed, one, 1)
    for n, two in enumerate(twos):
        normed = norm_next(normed, two, 2 + 2 * n)
    normed = norm_next(normed, one_other, half + 1)
    for n, two in enumerate(two_others):
        normed = norm_next(normed, two, half + 2 + 2 * n)
    threes = [held(three, (normed, joint_mine, bias)) if n == 0 else three for n, three in enumerate(threes)]
    for n, three in enumerate(threes):
        normed = norm_next(normed, three, 3 + 2 * n)
    for n, three in enumerate(plane.gather_third(threes)):
        normed = norm_next(normed, three, half + 3 + 2 * n)
    tables = rotary_columns(length, group)
    heads = joint_projection(order, normed, joint_mine, bias, tables, span, groups)

    out_full = lax.all_gather(held(out_rows, threes), "sp", axis=0, tiled=True)
    down = lax.all_gather(held(down_rows, threes), "fsdp", axis=0, tiled=True)
    gate_up_blocks = [held(swap_sp(held(gate_up_cols, threes)).reshape(n_sp * depth, 2 * ff), heads[0])]
    gate_up_blocks.append(lax.ppermute(gate_up_blocks[0], "fsdp", ring))
    cot = cotangent.reshape(span, D)
    cot_held = held(cot, gate_up_blocks[0])
    cot_partner, cot_one, cot_twos = plane.gather_first(cot_held)
    results = [attend(*heads[:3])]
    cot_one = held(cot_one, results[0][1])
    gate_up_blocks[1] = held(gate_up_blocks[1], results[0][1])
    gate_up_blocks.append(lax.ppermute(gate_up_blocks[1], "fsdp", ring))
    cot_one_other, cot_two_others, cot_threes = plane.gather_second(cot_one, cot_twos)
    for g in range(1, groups):
        results.append(attend(*heads[3 * g : 3 * g + 3], (cot_partner, cot_one, cot_twos, gate_up_blocks[1])))
    cot_threes = [held(c, results[-1][1]) for c in cot_threes]
    for _ in range(3, n_z):
        gate_up_blocks.append(lax.ppermute(gate_up_blocks[-1], "fsdp", ring))
    cot_three_others = plane.gather_third(cot_threes)
    cot_blocks, cot_partners = [cot, cot_one], [cot_partner, cot_one_other]
    for pieces in zip(cot_twos, cot_threes):
        cot_blocks += pieces
    for pieces in zip(cot_two_others, cot_three_others):
        cot_partners += pieces
    gate_up = in_line(gate_up_blocks, my_z)
    attended = [swap_sp(o).reshape(n_sp, span, group) for o, _ in results]
    middle, normed_two, normed_again, attended_all = middle_of(
        attended, out_full, depth, x, gain_two, shift_two, (gate_up_blocks[:3], down)
    )

    feed = None

    def feed_next(feed, pair, t, deps=()):
        return feed_block(pair, (cot_blocks[t], cot_partners[t]), gate_up, down, t, half, feed, deps)

    partner = plane.send(normed_two, plane.core)
    one = plane.send(normed_two, plane.first)
    feed = feed_next(None, (normed_two, partner), 0, (cot_blocks, cot_partners))
    one_other = plane.send(one, plane.core)
    again = held(normed_again, one)
    for n, perm in enumerate(plane.later):
        two = plane.send(again, perm)
        if n == 0:
            feed = feed_next(feed, (one, one_other), 1)
        one = held(one, (two, one_other, feed[0]))
        three = plane.send(one, perm)
        feed = feed_next(feed, (two, plane.send(two, plane.core)), 2 + 2 * n)
        three = held(three, feed[0])
        feed = feed_next(feed, (three, plane.send(three, plane.core)), 3 + 2 * n)
    hidden, gate_up_grad, two_all, cot_all = feed

    two_product = product_of([gate_up_grad], gate_up, NT, span)
    out_product = product_of([hidden], down, NN, span)
    two_far, two_theirs = plane.reduce_sums(two_product, (), True)
    further, nearer = plane.legs(two_far)
    down_sum = dot(hidden, held(cot_all, two_far), TN).astype(bf16)
    two_one, two_last = plane.legs_next(two_product, further, two_theirs, down_sum)
    gate_up_sum = dot(held(two_all, two_one), gate_up_grad, TN).astype(bf16)
    down_part = lax.psum_scatter(held(down_sum, two_one), "fsdp", scatter_dimension=0, tiled=True)
    two_grad = plane.legs_own(two_product, nearer, two_theirs, two_last, gate_up_sum)
    gate_up_part = lax.psum_scatter(held(gate_up_sum, two_grad), "fsdp", scatter_dimension=0, tiled=True)
    middle_grad, two_sums, branch_grad, *parts = norm_back(
        two_grad, middle, gain_two, cot, out_full, depth, n_sp, groups
    )
    dos = [swap_sp(part).reshape(n_sp * span, group) for part in parts]
    out_sum = dot(attended_all, branch_grad, TN).astype(bf16).reshape(n_sp, n_z * depth, D)

    def out_weight_part(start, stop, addends, dtype, deps=()):
        parts = [lax.dynamic_index_in_dim(out_sum, order[b], 0, False) for b in range(start, stop)]
        total = jnp.stack(parts).astype(f32)
        for addend, at in addends:
            total += addend[at : at + stop - start].astype(f32)
        return total.astype(dtype)

    out_sums, out_theirs = plane.reduce_sums(out_product, branch_grad)
    out_got = plane.reduce_leg(out_sums)
    rows = attend_back(place, *heads[:3], dos[0], *results[0], tables, span, out_sums)
    joint_rows = [rows]
    joint_sums = [dot(normed, rows, TN).astype(bf16)]
    joint_parts = [lax.psum_scatter(joint_sums[0], "fsdp", scatter_dimension=0, tiled=True)]
    out_one, out_last = plane.reduce_next(out_product, out_got, out_theirs)
    weight_sums, weight_theirs = plane.reduce_sums(out_weight_part)
    weight_got = plane.reduce_leg(weight_sums)
    gate_up_own = swap_sp(gate_up_part)
    for g in range(1, groups):
        deps = (joint_sums, out_one, weight_sums, weight_theirs)
        rows = attend_back(place, *heads[3 * g : 3 * g + 3], dos[g], *results[g], tables, span, deps)
        joint_rows.append(rows)
    _, weight_last = plane.reduce_next(out_weight_part, weight_got, weight_theirs)

    normed_product = product_of(joint_rows, joint_mine, NT, span)
    normed_far, normed_theirs = plane.reduce_sums(normed_product, (out_last, weight_got, joint_parts, down_part, gate_up_own), True)
    further, nearer = plane.legs(normed_far)
    last_normed = held(normed, (normed_far, joint_sums))
    for g in range(1, groups):
        joint_sums.append(dot(last_normed, joint_rows[g], TN).astype(bf16))
        joint_parts.append(lax.psum_scatter(joint_sums[g], "fsdp", scatter_dimension=0, tiled=True))
    joint_own = [swap_sp(j).reshape(n_sp, depth, 3 * group) for j in joint_parts]
    normed_one, normed_last = plane.legs_next(
        normed_product, further, normed_theirs, (joint_sums, joint_own[:-1])
    )
    output = (middle + plane.reduce_own(out_product, out_got, out_theirs, out_last, f32)).astype(bf16)
    out_own = plane.reduce_own(out_weight_part, weight_got, weight_theirs, weight_last)
    out_grad = lax.psum_scatter(held(out_own, joint_parts), "fsdp", scatter_dimension=0, tiled=True).astype(f32)
    down_grad = down_part[:ff_rows].astype(f32)
    gate_grad, up_grad = join_feed(gate_up_own.reshape(n_sp, depth, 2 * ff), n_z, ff_rows, ff_pad)
    bias_sum = jnp.stack([jnp.sum(r.astype(f32), axis=0).reshape(3, group) for r in joint_rows], 1)
    bias_sum = bias_sum.reshape(3, 1, width)
    bias_sum = lax.dynamic_update_slice(jnp.zeros((3, n_sp, width), f32), bias_sum, (0, me, 0))
    fill = (output, out_own, gate_grad, up_grad, bias_sum)
    normed_grad = plane.legs_own(normed_product, nearer, normed_theirs, normed_last, fill)
    tokens_grad, one_sums = norm_back(normed_grad, x, gain_one, middle_grad)
    tokens_grad = tokens_grad.reshape(tokens.shape)

    joint_grad = join_joint(joint_own, n_sp)

    sums = [one_sums[0], one_sums[1], two_sums[0], two_sums[1]]
    sums = jnp.concatenate([s.reshape(n_all, n_gain) for s in sums] + [bias_sum.reshape(n_all, -1)], axis=1)
    sums = jnp.sum(lax.all_to_all(sums, ("fsdp", "sp"), split_axis=0, concat_axis=0, tiled=True), axis=0)
    gain_one_grad, shift_one_grad, gain_two_grad, shift_two_grad = (
        sums[i * n_gain : (i + 1) * n_gain] for i in range(4)
    )
    return (
        output.reshape(tokens.shape),
        tokens_grad,
        gain_one_grad,
        shift_one_grad,
        joint_grad,
        sums[4 * n_gain :],
        out_grad,
        gain_two_grad,
        shift_two_grad,
        gate_grad,
        up_grad,
        down_grad,
    )


def solution(mesh):
    rows = P("fsdp", "sp", None)
    vector = P(("fsdp", "sp"))
    matrix = P(("fsdp", "sp"), None)
    return jax.shard_map(
        per_device,
        mesh=mesh,
        in_specs=(rows, rows, vector, vector, matrix, vector, matrix, vector, vector, matrix, matrix, matrix),
        out_specs=(rows, rows, vector, vector, matrix, vector, matrix, vector, vector, matrix, matrix, matrix),
        check_vma=False,
    )
```

```python
import functools
import math

import jax
import jax.numpy as jnp
import numpy as np
from jax import lax
from jax.experimental import pallas as pl
from jax.experimental.pallas import tpu as pltpu
from jax.sharding import PartitionSpec as P

D = 2048
HEADS = 32
HEAD = 64
ROT = 16

epsilon = 1e-05
masked_value = -1e30
f32 = jnp.float32
bf16 = jnp.bfloat16
LOG2E_SCALE = math.log2(math.e) * HEAD**-0.5
NN = (((1,), (0,)), ((), ()))
NT = (((1,), (1,)), ((), ()))
TN = (((0,), (0,)), ((), ()))


def dot(a, b, dims):
    return lax.dot_general(a, b, dims, preferred_element_type=f32)


def params(mib=56):
    return pltpu.CompilerParams(vmem_limit_bytes=mib * 2**20)


class Plane:
    def __init__(self, count):
        outer = count // 4
        self.count = count
        self.outer = outer

        def spot(o, i, c):
            return ((o % outer) * 2 + i) * 2 + c

        def split(s):
            return s // 4, (s // 2) % 2, s % 2

        self.core = [(s, s ^ 1) for s in range(count)]
        first = []
        later = [[] for _ in range(outer - 1)]
        for s in range(count):
            o, i, c = split(s)
            swapped = outer == 2 and c == 1
            first.append((s, spot(o + 1, i, c) if swapped else spot(o, 1 - i, c)))
            for k in range(1, outer):
                later[k - 1].append((s, spot(o, 1 - i, c) if swapped else spot(o + k, i, c)))
        self.first = first
        self.later = later
        here = list(range(count))

        def moved(table, perm):
            out = [None] * count
            for a, b in perm:
                out[b] = table[a]
            return out

        blocks = [here, moved(here, first)]
        for perm in later:
            blocks += [moved(blocks[0], perm), moved(blocks[1], perm)]
        blocks += [moved(b, self.core) for b in blocks]
        self.table = np.array(blocks, np.int32).T
        self.half = 2 * outer
        self.far = list(reversed(range(2, self.half, 2)))

    @staticmethod
    def send(value, perm):
        return lax.ppermute(value, "sp", perm)

    @staticmethod
    def back(value, perm):
        return lax.ppermute(value, "sp", [(b, a) for a, b in perm])

    def gather_first(self, value):
        return (
            self.send(value, self.core),
            self.send(value, self.first),
            [self.send(value, perm) for perm in self.later],
        )

    def gather_second(self, one, twos):
        return (
            self.send(one, self.core),
            [self.send(two, self.core) for two in twos],
            [self.send(one, perm) for perm in self.later],
        )

    def gather_third(self, threes):
        return [self.send(three, self.core) for three in threes]


    def reduce_sums(self, product, deps=(), apart=False):
        far = [product(self.half + start, self.half + start + 2, (), bf16, deps) for start in self.far]
        near = product(self.half, self.half + 2, (), bf16, far)
        theirs = [self.send(value, self.core) for value in far]
        more = (True,) if apart else ()
        sums = [product(start, start + 2, ((value, 0),), bf16, near, *more) for start, value in zip(self.far, theirs)]
        return sums, self.send(near, self.core)

    def reduce_leg(self, sums):
        return [self.back(value, self.later[start // 2 - 1]) for start, value in zip(self.far, sums)]

    def reduce_next(self, product, got, theirs, deps=()):
        one = product(1, 2, tuple((t, 1) for t in [theirs] + got), bf16, deps)
        return one, self.back(one, self.first)

    def reduce_own(self, product, got, theirs, last, dtype=bf16, deps=()):
        return product(0, 1, tuple((t, 0) for t in [theirs] + got + [last]), dtype, deps)[0]


    def legs(self, sums):
        perms = [self.later[start // 2 - 1] for start in self.far]
        further = [self.back(pair[1], perm) for pair, perm in zip(sums, perms)]
        nearer = [self.back(held(pair[0], further), perm) for pair, perm in zip(sums, perms)]
        return further, nearer

    def legs_next(self, product, further, theirs, deps=()):
        one = product(1, 2, ((theirs, 1), *((t, 0) for t in further)), bf16, deps)
        return one, self.back(one, self.first)

    def legs_own(self, product, nearer, theirs, last, deps=()):
        return product(0, 1, ((theirs, 0), *((t, 0) for t in [*nearer, last])), bf16, deps)[0]


def launch(
    kernel, operands, in_specs, outs, out_specs, *, grid, name, cost, scratch=(), deps=(), aliases=None, prefetch=0, mib=60
):
    deps = jax.tree.leaves(deps)
    count = len(operands)

    def body(*refs):
        kernel(*refs[:count], *refs[count + len(deps) :])

    flops, moved, transcendentals = cost
    return pl.pallas_call(
        body,
        grid_spec=pltpu.PrefetchScalarGridSpec(
            num_scalar_prefetch=prefetch,
            grid=grid,
            in_specs=list(in_specs) + [pl.BlockSpec(memory_space=pl.ANY)] * len(deps),
            out_specs=list(out_specs),
            scratch_shapes=list(scratch),
        ),
        out_shape=list(outs),
        input_output_aliases=aliases or {},
        compiler_params=pltpu.CompilerParams(vmem_limit_bytes=mib * 2**20),
        cost_estimate=pl.CostEstimate(flops=int(flops), bytes_accessed=int(moved), transcendentals=int(transcendentals)),
        name=name,
    )(*operands, *deps)


ANYWHERE = pl.BlockSpec(memory_space=pl.ANY)


def held(value, deps):
    return launch(
        lambda *refs: None, [value], [ANYWHERE], [shape_of(value.shape, value.dtype)], [ANYWHERE],
        grid=(1,), aliases={0: 0}, deps=deps, cost=(0, 0, 0), name="held",
    )[0]


def whole(shape):
    return pl.BlockSpec(shape, lambda *_: (0,) * len(shape))


def shape_of(shape, dtype):
    return jax.ShapeDtypeStruct(shape, dtype)


def product_kernel(terms, dims, pieces, *refs):
    outs = refs[-pieces:]
    each, rows, width = outs[0].shape
    count = each * pieces
    total = dot(refs[0][...], refs[terms][...], dims)
    for t in range(1, terms):
        total += dot(refs[t][...], refs[terms + t][...], dims)
    for ref in refs[2 * terms : -pieces]:
        total += ref[...].astype(f32).reshape(count * rows, width)
    total = total.reshape(pieces, each, rows, width)
    for n, out_ref in enumerate(outs):
        out_ref[...] = total[n].astype(out_ref.dtype)


def product_of(lefts, right, dims, span):
    tile = 512
    depth = sum(left.shape[1] for left in lefts)

    def right_at(at, left):
        if dims is NT:
            return pl.BlockSpec((tile, left.shape[1]), lambda i: (i, at))
        return pl.BlockSpec((left.shape[1], tile), lambda i: (at, i))

    def product(start, stop, addends, dtype, deps=(), apart=False):
        count = stop - start
        pieces = count if apart else 1
        assert start % count == 0 and all(at % count == 0 for _, at in addends)

        def columns(at):
            return pl.BlockSpec((count, span, tile), lambda i: (at // count, 0, i))

        values = launch(
            functools.partial(product_kernel, len(lefts), dims, pieces),
            [*lefts, *[right] * len(lefts), *(value for value, _ in addends)],
            [pl.BlockSpec((count * span, a.shape[1]), lambda i: (start // count, 0)) for a in lefts]
            + [right_at(t, left) for t, left in enumerate(lefts)]
            + [columns(at) for _, at in addends],
            [shape_of((count // pieces, span, D), dtype)] * pieces,
            [pl.BlockSpec((count // pieces, span, tile), lambda i: (0, 0, i))] * pieces,
            grid=(D // tile,),
            deps=deps,
            mib=60,
            cost=(2 * count * span * D * depth, 2 * depth * (D + count * span) + 4 * count * span * D, 0),
            name="block_product",
        )
        return values if apart else values[0]

    return product


def norm_kernel(x_ref, gain_ref, shift_ref, *rest):
    out_ref = rest[-1]
    values = x_ref[...].astype(f32)
    center = values - jnp.mean(values, axis=-1, keepdims=True)
    spread = jnp.mean(center * center, axis=-1, keepdims=True)
    out_ref[...] = (center * lax.rsqrt(spread + epsilon) * gain_ref[...] + shift_ref[...]).astype(bf16)


def norm_block(x, gain, shift, at, blocks, buffer, deps=()):
    rows = x.shape[0]
    tile = min(256, rows)
    steps = rows // tile
    row = pl.BlockSpec((1, D), lambda i: (0, 0))
    held = [] if buffer is None else [buffer]
    return launch(
        norm_kernel,
        [x, gain, shift, *held],
        [pl.BlockSpec((tile, D), lambda i: (i, 0)), row, row, *[ANYWHERE] * len(held)],
        [shape_of((blocks * rows, D), bf16)],
        [pl.BlockSpec((tile, D), lambda i: (at * steps + i, 0))],
        grid=(steps,),
        aliases={3: 0} if held else {},
        deps=deps,
        mib=60,
        cost=(rows * D * 12, rows * D * 4, rows),
        name="first_norm",
    )[0]


def cut_joint_kernel(n_sp, groups, group, in_ref, out_ref):
    for j in range(n_sp):
        for g in range(groups):
            for m in range(3):
                to = (g * 3 + m) * group
                start = m * D + (j * groups + g) * group
                out_ref[j, :, to : to + group] = in_ref[:, start : start + group]


def cut_joint(weight, n_sp, groups):
    depth = weight.shape[0]
    width = D // n_sp
    return launch(
        functools.partial(cut_joint_kernel, n_sp, groups, width // groups),
        [weight], [whole(weight.shape)], [shape_of((n_sp, depth, 3 * width), bf16)], [whole((n_sp, depth, 3 * width))],
        grid=(1,), cost=(0, weight.size * 4, 0), name="cut_joint",
    )[0]


def join_joint_kernel(n_sp, groups, group, *refs):
    out_ref = refs[-1]
    for j in range(n_sp):
        for g in range(groups):
            for m in range(3):
                start = m * D + (j * groups + g) * group
                out_ref[:, start : start + group] = refs[g][j, :, m * group : (m + 1) * group].astype(f32)


def join_joint(parts, n_sp):
    groups = len(parts)
    depth = parts[0].shape[1]
    return launch(
        functools.partial(join_joint_kernel, n_sp, groups, parts[0].shape[2] // 3),
        parts, [whole(p.shape) for p in parts], [shape_of((depth, 3 * D), f32)], [whole((depth, 3 * D))],
        grid=(1,), cost=(0, depth * D * 18, 0), name="join_joint",
    )[0]


def cut_feed_kernel(n_sp, n_z, size, padded, gate_ref, up_ref, out_ref):
    out_ref[...] = jnp.zeros_like(out_ref)
    for j in range(n_sp):
        for p, ref in enumerate((gate_ref, up_ref)):
            for z in range(n_z):
                start = (z * n_sp + j) * size
                to = (p * n_z + z) * padded
                out_ref[j, :, to : to + size] = ref[:, start : start + size]


def cut_feed(gate_weight, up_weight, n_sp, n_z, padded, deps):
    depth, total = gate_weight.shape
    size = total // (n_sp * n_z)
    shape = (n_sp, depth, 2 * n_z * padded)
    return launch(
        functools.partial(cut_feed_kernel, n_sp, n_z, size, padded),
        [gate_weight, up_weight], [whole(gate_weight.shape)] * 2, [shape_of(shape, bf16)], [whole(shape)],
        grid=(1,), cost=(0, gate_weight.size * 8, 0), name="cut_feed", deps=deps,
    )[0]


def join_feed_kernel(n_sp, n_z, size, padded, in_ref, gate_ref, up_ref):
    for p, ref in enumerate((gate_ref, up_ref)):
        for z in range(n_z):
            for j in range(n_sp):
                start = (z * n_sp + j) * size
                to = (p * n_z + z) * padded
                ref[:, start : start + size] = in_ref[j, :, to : to + size].astype(f32)


def join_feed(value, n_z, size, padded):
    n_sp, depth, _ = value.shape
    shape = (depth, n_sp * n_z * size)
    return launch(
        functools.partial(join_feed_kernel, n_sp, n_z, size, padded),
        [value], [whole(value.shape)], [shape_of(shape, f32)] * 2, [whole(shape)] * 2,
        grid=(1,), cost=(0, value.size * 6, 0), name="join_feed",
    )


def norm_back_kernel(depth, n_parts, *refs):
    grad_ref, x_ref, gain_ref, beside_ref = refs[:4]
    weights = refs[4 : 4 + n_parts]
    outs = refs[4 + n_parts :]
    result_ref, sums_ref = outs[0], outs[1]
    values = x_ref[...].astype(f32)
    center = values - jnp.mean(values, axis=-1, keepdims=True)
    spread = jnp.mean(center * center, axis=-1, keepdims=True)
    inverse = lax.rsqrt(spread + epsilon)
    xhat = center * inverse
    grad = grad_ref[...].astype(f32)
    scaled = grad * gain_ref[...]
    level = jnp.mean(scaled, axis=-1, keepdims=True)
    along = jnp.mean(scaled * xhat, axis=-1, keepdims=True)
    result = beside_ref[...].astype(f32) + inverse * (scaled - level - xhat * along)
    result_ref[...] = result

    @pl.when(pl.program_id(0) == 0)
    def _():
        sums_ref[...] = jnp.zeros_like(sums_ref)

    sums_ref[0:1] += jnp.sum(grad * xhat, axis=0, keepdims=True)
    sums_ref[1:2] += jnp.sum(grad, axis=0, keepdims=True)
    if n_parts:
        branch = result.astype(bf16)
        outs[2][...] = branch
        parts = outs[3:]
        full = dot(branch, weights[0][...], NT).astype(bf16)
        for place, g, j, columns in head_pieces(parts[0].shape[0], depth, len(parts)):
            parts[g][j, :, columns] = full[:, place]


def norm_back(grad, x, gain, beside, weight=None, depth=0, n_sp=0, groups=0):
    rows = x.shape[0]
    tile = min(256, rows)
    row = pl.BlockSpec((1, D), lambda i: (0, 0))
    block = pl.BlockSpec((tile, D), lambda i: (i, 0))
    outs = [shape_of((rows, D), f32), shape_of((8, D), f32)]
    out_specs = [block, whole((8, D))]
    extra, specs = [], []
    if weight is not None:
        group = D // n_sp // groups
        extra, specs = [weight], [whole((D, D))]
        outs += [shape_of((rows, D), bf16)] + [shape_of((n_sp, rows, group), bf16)] * groups
        out_specs += [block] + [pl.BlockSpec((n_sp, tile, group), lambda i: (0, i, 0))] * groups
    return launch(
        functools.partial(norm_back_kernel, depth, len(extra)),
        [grad, x, gain, beside, *extra],
        [block, block, row, block, *specs],
        outs,
        out_specs,
        grid=(rows // tile,),
        cost=(rows * D * (20 + 2 * D * len(extra)), rows * D * 16 + 2 * D * D * len(extra), rows),
        name="norm_back",
    )


def head_pieces(n_sp, depth, groups):
    group = D // n_sp // groups
    n_z = D // n_sp // depth
    for z in range(n_z):
        for s in range(n_sp):
            j, rest = divmod((z * n_sp + s) * depth, groups * group)
            g, column = divmod(rest, group)
            yield slice((s * n_z + z) * depth, (s * n_z + z + 1) * depth), g, j, slice(column, column + depth)


def middle_kernel(groups, n_sp, depth, *refs):
    parts, (out_w, x_ref, gain_ref, shift_ref) = refs[:groups], refs[groups : groups + 4]
    middle_ref, normed_ref, again_ref, attended_ref = refs[groups + 4 :]
    for to, g, j, columns in head_pieces(n_sp, depth, groups):
        attended_ref[:, to] = parts[g][j, :, columns]
    values = x_ref[...].astype(f32) + dot(attended_ref[...], out_w[...], NN)
    middle_ref[...] = values
    center = values - jnp.mean(values, axis=-1, keepdims=True)
    spread = jnp.mean(center * center, axis=-1, keepdims=True)
    normed = (center * lax.rsqrt(spread + epsilon) * gain_ref[...] + shift_ref[...]).astype(bf16)
    normed_ref[...] = normed
    again_ref[...] = normed


def middle_of(parts, out_w, depth, x, gain, shift, deps=()):
    n_sp, rows, group = parts[0].shape
    tile = min(256, rows)
    row = pl.BlockSpec((1, D), lambda i: (0, 0))
    block = pl.BlockSpec((tile, D), lambda i: (i, 0))
    return launch(
        functools.partial(middle_kernel, len(parts), n_sp, depth),
        [*parts, out_w, x, gain, shift],
        [pl.BlockSpec((n_sp, tile, group), lambda i: (0, i, 0))] * len(parts)
        + [pl.BlockSpec((D, D), lambda i: (0, 0)), block, row, row],
        [shape_of((rows, D), f32)] + [shape_of((rows, D), bf16)] * 3,
        [block] * 4,
        grid=(rows // tile,),
        deps=deps,
        cost=(2 * rows * D * D, 2 * D * D + rows * D * 12, rows),
        name="middle",
    )


def turn(values, cosine, sine_up, sine_down):
    width = values.shape[1]
    half = ROT // 2
    return (
        values * cosine
        + pltpu.roll(values, width - half, 1) * sine_up
        + pltpu.roll(values, half, 1) * sine_down
    )


def joint_kernel(width, table_ref, x_ref, w_ref, bias_ref, cos_ref, up_ref, down_ref, *outs):
    projected = dot(x_ref[...], w_ref[...], NN) + bias_ref[...]
    tables = (cos_ref[...], up_ref[...], down_ref[...])
    for g in range(len(outs) // 3):
        part = projected[:, 3 * g * width : 3 * (g + 1) * width]
        outs[3 * g][...] = turn(part[:, :width], *tables).astype(bf16)
        outs[3 * g + 1][...] = turn(part[:, width : 2 * width], *tables).astype(bf16)
        outs[3 * g + 2][...] = part[:, 2 * width :].astype(bf16)


def joint_projection(table, normed, weight, bias, tables, span, groups):
    length = normed.shape[0]
    total = weight.shape[1]
    width = total // 3 // groups
    placed = pl.BlockSpec((span, width), lambda b, t: (t[b], 0))
    return pl.pallas_call(
        functools.partial(joint_kernel, width),
        grid_spec=pltpu.PrefetchScalarGridSpec(
            num_scalar_prefetch=1,
            grid=(length // span,),
            in_specs=[
                pl.BlockSpec((span, D), lambda b, t: (b, 0)),
                pl.BlockSpec((D, total), lambda b, t: (0, 0)),
                pl.BlockSpec((1, total), lambda b, t: (0, 0)),
                placed,
                placed,
                placed,
            ],
            out_specs=[placed] * (3 * groups),
        ),
        out_shape=[jax.ShapeDtypeStruct((length, width), bf16)] * (3 * groups),
        compiler_params=params(),
        cost_estimate=pl.CostEstimate(
            flops=2 * length * D * total, bytes_accessed=length * (D + total) * 2, transcendentals=0
        ),
        name="joint_projection",
    )(table, normed, weight, bias, *tables)


def attend_kernel(heads, bq, bk, q_ref, k_ref, v_ref, o_ref, lse_ref, qm, vt, acc, m_s, l_s):
    i = pl.program_id(0)
    length, width = k_ref.shape
    lane = lax.broadcasted_iota(jnp.int32, (1, width), 1) // HEAD

    @pl.when(i == 0)
    def _():
        def flip(b, carry):
            rows = pl.ds(pl.multiple_of(b * bk, bk), bk)
            vt[:, rows] = jnp.transpose(v_ref[rows, :])
            return carry

        lax.fori_loop(0, length // bk, flip, 0)

    q = q_ref[...]
    for h in range(heads):
        qm[h] = jnp.where(lane == h, q, jnp.zeros_like(q))
    acc[...] = jnp.zeros_like(acc)
    m_s[...] = jnp.full_like(m_s, masked_value)
    l_s[...] = jnp.zeros_like(l_s)

    def body(j, masked):
        rows = pl.ds(pl.multiple_of(j * bk, bk), bk)
        k = k_ref[rows, :]
        scores = [dot(k, qm[h], NT) for h in range(heads)]
        if masked:
            key_at = lax.broadcasted_iota(jnp.int32, scores[0].shape, 0) + j * bk
            query_at = lax.broadcasted_iota(jnp.int32, scores[0].shape, 1) + i * bq
            scores = [jnp.where(key_at <= query_at, s, masked_value) for s in scores]
        m0 = m_s[...]
        l0 = l_s[...]
        m1 = jnp.maximum(m0, jnp.concatenate([jnp.max(s, axis=0, keepdims=True) for s in scores] + [m0[heads:]], 0))
        m_s[...] = m1
        kept = jnp.exp2((m0 - m1) * LOG2E_SCALE)
        base = m1 * LOG2E_SCALE
        raised = [jnp.exp2(scores[h] * LOG2E_SCALE - base[h : h + 1]) for h in range(heads)]
        l_s[...] = l0 * kept + jnp.concatenate([jnp.sum(p, axis=0, keepdims=True) for p in raised] + [l0[heads:]], 0)
        for h in range(heads):
            part = slice(h * HEAD, (h + 1) * HEAD)
            acc[part, :] = acc[part, :] * kept[h : h + 1] + dot(vt[part, rows], raised[h].astype(bf16), NN)

    whole = (i * bq) // bk
    lax.fori_loop(0, whole, lambda j, c: (body(j, False), c)[1], 0)
    for d in range(max(1, bq // bk)):
        body(whole + d, True)
    for h in range(heads):
        part = slice(h * HEAD, (h + 1) * HEAD)
        acc[part, :] = acc[part, :] * (1.0 / l_s[h : h + 1])
    o_ref[...] = jnp.transpose(acc[...].astype(bf16))
    lse_ref[...] = m_s[...] * LOG2E_SCALE + jnp.log2(l_s[...])


def attend(q, k, v, deps=()):
    length, width = q.shape
    heads = width // HEAD
    bq, bk = min(1024, length), min(512, length)
    full = pl.BlockSpec((length, width), lambda i: (0, 0))
    return launch(
        functools.partial(attend_kernel, heads, bq, bk),
        [q, k, v],
        [pl.BlockSpec((bq, width), lambda i: (i, 0)), full, full],
        [shape_of((length, width), bf16), shape_of((8, length), f32)],
        [pl.BlockSpec((bq, width), lambda i: (i, 0)), pl.BlockSpec((8, bq), lambda i: (0, i))],
        grid=(length // bq,),
        scratch=[
            pltpu.VMEM((heads, bq, width), bf16),
            pltpu.VMEM((width, length), bf16),
            pltpu.VMEM((width, bq), f32),
            pltpu.VMEM((8, bq), f32),
            pltpu.VMEM((8, bq), f32),
        ],
        deps=deps,
        cost=(8 * length * length * width, length * width * 8, length * length * heads // 2),
        name="attend",
    )


def attend_back_kernel(
    heads, bq, bk, place_ref, q_ref, k_ref, v_ref, do_ref, o_ref, lse_ref, cos_ref, up_ref, down_ref, out_ref,
    dq_acc, dk_acc, dv_acc, delta,
):
    j = pl.program_id(0)
    length, width = q_ref.shape
    lane = lax.broadcasted_iota(jnp.int32, (1, width), 1) // HEAD

    @pl.when(j == 0)
    def _():
        dq_acc[...] = jnp.zeros_like(dq_acc)
        pick = (
            lax.broadcasted_iota(jnp.int32, (8, width), 0) == lax.broadcasted_iota(jnp.int32, (8, width), 1) // HEAD
        ).astype(f32)

        def sums(b, carry):
            rows = pl.ds(pl.multiple_of(b * bq, bq), bq)
            both = do_ref[rows, :].astype(f32) * o_ref[rows, :].astype(f32)
            delta[:, rows] = lax.dot_general(
                pick, both, NT, precision=lax.Precision.HIGHEST, preferred_element_type=f32
            )
            return carry

        lax.fori_loop(0, length // bq, sums, 0)

    key_rows = pl.ds(pl.multiple_of(j * bk, bk), bk)
    k = k_ref[key_rows, :]
    v = v_ref[key_rows, :]
    kt = jnp.transpose(k)
    dk_acc[...] = jnp.zeros_like(dk_acc)
    dv_acc[...] = jnp.zeros_like(dv_acc)

    def body(i, masked):
        rows = pl.ds(pl.multiple_of(i * bq, bq), bq)
        q = q_ref[rows, :]
        do = do_ref[rows, :]
        probs, grads, queries, results = [], [], [], []
        for h in range(heads):
            qh = jnp.where(lane == h, q, jnp.zeros_like(q))
            doh = jnp.where(lane == h, do, jnp.zeros_like(do))
            s = dot(k, qh, NT)
            p = jnp.exp2(s * LOG2E_SCALE - lse_ref[h : h + 1, rows])
            if masked:
                key_at = lax.broadcasted_iota(jnp.int32, s.shape, 0) + j * bk
                query_at = lax.broadcasted_iota(jnp.int32, s.shape, 1) + i * bq
                p = jnp.where(key_at <= query_at, p, 0.0)
            dp = dot(v, doh, NT)
            ds = p * (dp - delta[h : h + 1, rows])
            probs.append(p.astype(bf16))
            grads.append(ds.astype(bf16))
            queries.append(qh)
            results.append(doh)
        dv_acc[...] += dot(jnp.concatenate(probs, 1), jnp.concatenate(results, 0), NN)
        dk_acc[...] += dot(jnp.concatenate(grads, 1), jnp.concatenate(queries, 0), NN)
        for h in range(heads):
            part = slice(h * HEAD, (h + 1) * HEAD)
            dq_acc[part, rows] += dot(kt[part], grads[h], NN)

    first = (j * bk) // bq
    near = max(1, bk // bq)
    for d in range(near):
        body(first + d, True)
    lax.fori_loop(first + near, length // bq, lambda i, c: (body(i, False), c)[1], 0)
    scale = HEAD**-0.5
    tables = (cos_ref[...], -up_ref[...], -down_ref[...])
    dq = (jnp.transpose(dq_acc[:, key_rows]) * scale).astype(bf16).astype(f32)
    dk = (dk_acc[...] * scale).astype(bf16).astype(f32)
    out_ref[:, :width] = turn(dq, *tables).astype(bf16)
    out_ref[:, width : 2 * width] = turn(dk, *tables).astype(bf16)
    out_ref[:, 2 * width :] = dv_acc[...].astype(bf16)


def attend_back(place, q, k, v, do, o, lse, tables, span, deps=()):
    length, width = q.shape
    heads = width // HEAD
    bq = min(512, length)
    bk = span
    full = pl.BlockSpec((length, width), lambda i, t: (0, 0))
    block = pl.BlockSpec((bk, width), lambda i, t: (i, 0))
    return launch(
        functools.partial(attend_back_kernel, heads, bq, bk),
        [place, q, k, v, do, o, lse, *tables],
        [full] * 5 + [pl.BlockSpec((8, length), lambda i, t: (0, 0))] + [block] * 3,
        [shape_of((length, 3 * width), bf16)],
        [pl.BlockSpec((bk, 3 * width), lambda i, t: (t[i], 0))],
        grid=(length // bk,),
        prefetch=1,
        scratch=[
            pltpu.VMEM((width, length), f32),
            pltpu.VMEM((bk, width), f32),
            pltpu.VMEM((bk, width), f32),
            pltpu.VMEM((8, length), f32),
        ],
        deps=deps,
        cost=(12 * length * length * width, length * width * 16, length * length * heads // 2),
        name="attend_back",
    )[0]


def feed_kernel(ff, x0, x1, c0, c1, wgu_ref, wd_ref, *rest):
    hidden_ref, grad_ref, x_ref, c_ref = rest[-4:]
    which = pl.program_id(0)

    @pl.when(which == 0)
    def _():
        x_ref[...] = x0[...]
        c_ref[...] = c0[...]

    @pl.when(which == 1)
    def _():
        x_ref[...] = x1[...]
        c_ref[...] = c1[...]

    both = dot(x_ref[...], wgu_ref[...], NN)
    hidden_grad = dot(c_ref[...], wd_ref[...], NT)
    gate = both[:, :ff]
    up = both[:, ff:]
    open_ = jax.nn.sigmoid(gate)
    swished = gate * open_
    hidden_ref[...] = (swished * up).astype(bf16)
    grad_ref[:, :ff] = (hidden_grad * up * open_ * (1.0 + gate * (1.0 - open_))).astype(bf16)
    grad_ref[:, ff:] = (hidden_grad * swished).astype(bf16)


def feed_block(pair, cot_pair, gate_up, down, at, half, buffers, deps=()):
    rows = pair[0].shape[0]
    ff = down.shape[0]
    tile = min(256, rows)
    steps = rows // tile
    length = 2 * half * rows
    early = pl.BlockSpec((tile, D), lambda p, i: (jnp.where(p == 0, i, steps - 1), 0))
    late = pl.BlockSpec((tile, D), lambda p, i: (jnp.where(p == 0, 0, i), 0))
    operands = [pair[0], pair[1], cot_pair[0], cot_pair[1], gate_up, down]
    specs = [
        early,
        late,
        early,
        late,
        pl.BlockSpec((D, 2 * ff), lambda p, i: (0, 0)),
        pl.BlockSpec((ff, D), lambda p, i: (0, 0)),
    ]
    aliases = {}
    if buffers is not None:
        aliases = {len(operands) + n: n for n in range(4)}
        operands += list(buffers)
        specs += [pl.BlockSpec(memory_space=pl.ANY)] * 4

    def place(p, i):
        return ((p * half + at) * steps + i, 0)

    return launch(
        functools.partial(feed_kernel, ff),
        operands,
        specs,
        [
            shape_of((length, ff), bf16),
            shape_of((length, 2 * ff), bf16),
            shape_of((length, D), bf16),
            shape_of((length, D), bf16),
        ],
        [
            pl.BlockSpec((tile, ff), place),
            pl.BlockSpec((tile, 2 * ff), place),
            pl.BlockSpec((tile, D), place),
            pl.BlockSpec((tile, D), place),
        ],
        grid=(2, steps),
        aliases=aliases,
        deps=deps,
        cost=(12 * rows * D * ff, 6 * D * ff + rows * D * 16, 2 * rows * ff),
        name="feed_forward",
    )


def rotary_columns(length, width):
    half = ROT // 2
    indices = np.arange(half, dtype=np.float32)
    inverse = np.float32(1.0) / np.float32(10000.0) ** (indices * np.float32(2.0 / ROT))
    angles = np.arange(length, dtype=np.float32)[:, None] * inverse[None, :].astype(np.float32)
    cosine, sine = np.cos(angles.astype(np.float64)), np.sin(angles.astype(np.float64))
    rest = np.zeros((length, HEAD - ROT))
    none = np.zeros((length, half))
    one_head = (
        np.concatenate([cosine, cosine, rest + 1.0], -1),
        np.concatenate([-sine, none, rest], -1),
        np.concatenate([none, sine, rest], -1),
    )
    return tuple(jnp.asarray(np.tile(t, (1, width // HEAD)).astype(np.float32)) for t in one_head)


def swap_sp(value):
    return lax.all_to_all(value, "sp", split_axis=0, concat_axis=0, tiled=True)


def in_line(blocks, mine):
    count, rows = len(blocks), blocks[0].shape[0]
    total = jnp.zeros((count * rows, blocks[0].shape[1]), blocks[0].dtype)
    for step, block in enumerate(blocks):
        total = lax.dynamic_update_slice(total, block, (lax.rem(mine - step + count, count) * rows, 0))
    return total


def per_device(
    tokens, cotangent, first_gain, first_shift, joint_weight, joint_bias, out_weight, second_gain, second_shift,
    gate_weight, up_weight, down_weight,
):
    n_sp = lax.axis_size("sp")
    n_z = lax.axis_size("fsdp")
    n_all = n_sp * n_z
    plane = Plane(n_sp)
    half = plane.half
    me = lax.axis_index("sp")
    span = tokens.shape[1]
    length = n_sp * span
    width = D // n_sp
    depth = joint_weight.shape[0]
    ff_rows = down_weight.shape[0]
    unit = max(16, 128 // n_z)
    ff_pad = -(-ff_rows // unit) * unit
    ff = n_z * ff_pad

    order = jnp.asarray(plane.table)[me]
    place = jnp.asarray(np.argsort(plane.table, axis=1).astype(np.int32))[me]
    groups = 2 if width % 256 == 0 else 1
    group = width // groups
    my_z = lax.axis_index("fsdp")

    small = jnp.concatenate([first_gain, first_shift, second_gain, second_shift, joint_bias])
    small = jnp.broadcast_to(small[None], (n_all, small.shape[0]))
    small_all = lax.all_to_all(small, ("fsdp", "sp"), split_axis=0, concat_axis=0, tiled=True)
    small = small_all.astype(f32)
    n_gain = first_gain.shape[0]
    gain_one, shift_one, gain_two, shift_two = (
        small[:, i * n_gain : (i + 1) * n_gain].reshape(1, D) for i in range(4)
    )
    bias_all = small[:, 4 * n_gain :].reshape(3, n_sp, width)
    bias = lax.dynamic_index_in_dim(bias_all, me, axis=1, keepdims=False)
    bias = bias.reshape(3, groups, group).transpose(1, 0, 2).reshape(1, 3 * width)

    ring = [(i, (i + 1) % n_z) for i in range(n_z)]
    joint_block = swap_sp(cut_joint(joint_weight, n_sp, groups)).reshape(n_sp * depth, 3 * width)
    out_blocks = [out_weight]
    for _ in range(n_z - 1):
        out_blocks.append(lax.ppermute(out_blocks[-1], "fsdp", ring))
    out_rows = in_line(out_blocks, my_z)
    joint_blocks = [held(joint_block, out_blocks[1:])]
    for _ in range(n_z - 1):
        joint_blocks.append(lax.ppermute(joint_blocks[-1], "fsdp", ring))
    joint_mine = in_line(joint_blocks, my_z)

    gate_up_cols = cut_feed(gate_weight, up_weight, n_sp, n_z, ff_pad, ())
    down_rows = jnp.pad(down_weight, ((0, ff_pad - ff_rows), (0, 0)))
    x = tokens.reshape(span, D)
    normed = None

    def norm_next(normed, block, t, deps=()):
        return norm_block(block, gain_one, shift_one, t, n_sp, normed, deps)

    partner, one, twos = plane.gather_first(x)
    normed = norm_next(None, x, 0)
    normed = norm_next(normed, partner, half)
    cot = held(cotangent.reshape(span, D), small_all)
    one = held(one, (normed, joint_blocks[1:3], gate_up_cols, cot))
    one_other, two_others, threes = plane.gather_second(one, twos)
    normed = norm_next(normed, one, 1)
    for n, two in enumerate(twos):
        normed = norm_next(normed, two, 2 + 2 * n)
    normed = norm_next(normed, one_other, half + 1)
    for n, two in enumerate(two_others):
        normed = norm_next(normed, two, half + 2 + 2 * n)
    threes = [held(three, (normed, joint_mine, bias)) if n == 0 else three for n, three in enumerate(threes)]
    for n, three in enumerate(threes):
        normed = norm_next(normed, three, 3 + 2 * n)
    for n, three in enumerate(plane.gather_third(threes)):
        normed = norm_next(normed, three, half + 3 + 2 * n)
    tables = rotary_columns(length, group)
    heads = joint_projection(order, normed, joint_mine, bias, tables, span, groups)

    out_full = lax.all_gather(held(out_rows, threes), "sp", axis=0, tiled=True)
    down = lax.all_gather(held(down_rows, threes), "fsdp", axis=0, tiled=True)
    gate_up_blocks = [held(swap_sp(held(gate_up_cols, threes)).reshape(n_sp * depth, 2 * ff), heads[0])]
    gate_up_blocks.append(lax.ppermute(gate_up_blocks[0], "fsdp", ring))
    cot = held(cot, gate_up_blocks[0])
    cot_partner, cot_one, cot_twos = plane.gather_first(cot)
    results = [attend(*heads[:3])]
    cot_one = held(cot_one, results[0][1])
    gate_up_blocks[1] = held(gate_up_blocks[1], results[0][1])
    gate_up_blocks.append(lax.ppermute(gate_up_blocks[1], "fsdp", ring))
    cot_one_other, cot_two_others, cot_threes = plane.gather_second(cot_one, cot_twos)
    for g in range(1, groups):
        results.append(attend(*heads[3 * g : 3 * g + 3], (cot_partner, cot_one, cot_twos, gate_up_blocks[1])))
    gate_up_blocks[2] = held(gate_up_blocks[2], results[-1][1])
    for _ in range(3, n_z):
        gate_up_blocks.append(lax.ppermute(gate_up_blocks[-1], "fsdp", ring))
    cot_three_others = plane.gather_third(cot_threes)
    cot_blocks, cot_partners = [cot, cot_one], [cot_partner, cot_one_other]
    for pieces in zip(cot_twos, cot_threes):
        cot_blocks += pieces
    for pieces in zip(cot_two_others, cot_three_others):
        cot_partners += pieces
    gate_up = in_line(gate_up_blocks, my_z)
    results[-1] = (held(results[-1][0], cot_threes), results[-1][1])
    attended = [swap_sp(o).reshape(n_sp, span, group) for o, _ in results]
    middle, normed_two, normed_again, attended_all = middle_of(
        attended, out_full, depth, x, gain_two, shift_two, (gate_up, down)
    )

    feed = None

    def feed_next(feed, pair, t, deps=()):
        return feed_block(pair, (cot_blocks[t], cot_partners[t]), gate_up, down, t, half, feed, deps)

    partner = plane.send(normed_two, plane.core)
    one = plane.send(normed_two, plane.first)
    feed = feed_next(None, (normed_two, partner), 0)
    one = held(one, feed[0])
    one_other = plane.send(one, plane.core)
    again = held(normed_again, one)
    for n, perm in enumerate(plane.later):
        two = plane.send(again, perm)
        if n == 0:
            feed = feed_next(feed, (one, one_other), 1, again)
        two = held(two, feed[0])
        one = held(one, (two, one_other))
        three = plane.send(one, perm)
        feed = feed_next(feed, (two, plane.send(two, plane.core)), 2 + 2 * n)
        three = held(three, feed[0])
        feed = feed_next(feed, (three, plane.send(three, plane.core)), 3 + 2 * n)
    hidden, gate_up_grad, two_all, cot_all = feed

    two_product = product_of([gate_up_grad], gate_up, NT, span)
    out_product = product_of([hidden], down, NN, span)
    two_far, two_theirs = plane.reduce_sums(two_product, (), True)
    further, nearer = plane.legs(two_far)
    down_sum = dot(hidden, held(cot_all, two_far), TN).astype(bf16)
    two_one, two_last = plane.legs_next(two_product, further, two_theirs, down_sum)
    gate_up_sum = dot(held(two_all, two_one), gate_up_grad, TN).astype(bf16)
    down_part = lax.psum_scatter(held(down_sum, two_one), "fsdp", scatter_dimension=0, tiled=True)
    two_grad = plane.legs_own(two_product, nearer, two_theirs, two_last, gate_up_sum)
    gate_up_part = lax.psum_scatter(held(gate_up_sum, two_grad), "fsdp", scatter_dimension=0, tiled=True)
    middle_grad, two_sums, branch_grad, *parts = norm_back(
        two_grad, middle, gain_two, cot, out_full, depth, n_sp, groups
    )
    dos = [swap_sp(part).reshape(n_sp * span, group) for part in parts]
    out_sum = dot(attended_all, branch_grad, TN).astype(bf16).reshape(n_sp, n_z * depth, D)

    def out_weight_part(start, stop, addends, dtype, deps=()):
        parts = [lax.dynamic_index_in_dim(out_sum, order[b], 0, False) for b in range(start, stop)]
        total = jnp.stack(parts).astype(f32)
        for addend, at in addends:
            total += addend[at : at + stop - start].astype(f32)
        return total.astype(dtype)

    out_sums, out_theirs = plane.reduce_sums(out_product, branch_grad)
    out_got = plane.reduce_leg(out_sums)
    rows = attend_back(place, *heads[:3], dos[0], *results[0], tables, span, out_sums)
    joint_rows = [rows]
    joint_sums = [dot(normed, rows, TN).astype(bf16)]
    joint_parts = [lax.psum_scatter(joint_sums[0], "fsdp", scatter_dimension=0, tiled=True)]
    out_one, out_last = plane.reduce_next(out_product, out_got, out_theirs)
    weight_sums, weight_theirs = plane.reduce_sums(out_weight_part)
    weight_got = plane.reduce_leg(weight_sums)
    gate_up_own = swap_sp(gate_up_part)
    for g in range(1, groups):
        deps = (joint_sums, out_one, weight_sums, weight_theirs)
        rows = attend_back(place, *heads[3 * g : 3 * g + 3], dos[g], *results[g], tables, span, deps)
        joint_rows.append(rows)
    _, weight_last = plane.reduce_next(out_weight_part, weight_got, weight_theirs)

    normed_product = product_of(joint_rows, joint_mine, NT, span)
    normed_far, normed_theirs = plane.reduce_sums(normed_product, (out_last, weight_got, joint_parts, down_part, gate_up_own), True)
    further, nearer = plane.legs(normed_far)
    last_normed = held(normed, (normed_far, joint_sums))
    for g in range(1, groups):
        joint_sums.append(dot(last_normed, joint_rows[g], TN).astype(bf16))
        joint_parts.append(lax.psum_scatter(joint_sums[g], "fsdp", scatter_dimension=0, tiled=True))
    joint_own = [swap_sp(j).reshape(n_sp, depth, 3 * group) for j in joint_parts]
    normed_one, normed_last = plane.legs_next(
        normed_product, further, normed_theirs, joint_sums
    )
    output = (middle + plane.reduce_own(out_product, out_got, out_theirs, out_last, f32)).astype(bf16)
    out_own = plane.reduce_own(out_weight_part, weight_got, weight_theirs, weight_last)
    out_grad = lax.psum_scatter(held(out_own, joint_parts), "fsdp", scatter_dimension=0, tiled=True).astype(f32)
    down_grad = down_part[:ff_rows].astype(f32)
    gate_grad, up_grad = join_feed(gate_up_own.reshape(n_sp, depth, 2 * ff), n_z, ff_rows, ff_pad)
    bias_sum = jnp.stack([jnp.sum(r.astype(f32), axis=0).reshape(3, group) for r in joint_rows], 1)
    bias_sum = bias_sum.reshape(3, 1, width)
    bias_sum = lax.dynamic_update_slice(jnp.zeros((3, n_sp, width), f32), bias_sum, (0, me, 0))
    fill = (output, out_own, gate_grad, up_grad, bias_sum)
    normed_grad = plane.legs_own(normed_product, nearer, normed_theirs, normed_last, fill)
    tokens_grad, one_sums = norm_back(normed_grad, x, gain_one, middle_grad)
    tokens_grad = tokens_grad.reshape(tokens.shape)

    joint_grad = join_joint(joint_own, n_sp)

    sums = [one_sums[0], one_sums[1], two_sums[0], two_sums[1]]
    sums = jnp.concatenate([s.reshape(n_all, n_gain) for s in sums] + [bias_sum.reshape(n_all, -1)], axis=1)
    sums = jnp.sum(lax.all_to_all(sums, ("fsdp", "sp"), split_axis=0, concat_axis=0, tiled=True), axis=0)
    gain_one_grad, shift_one_grad, gain_two_grad, shift_two_grad = (
        sums[i * n_gain : (i + 1) * n_gain] for i in range(4)
    )
    return (
        output.reshape(tokens.shape),
        tokens_grad,
        gain_one_grad,
        shift_one_grad,
        joint_grad,
        sums[4 * n_gain :],
        out_grad,
        gain_two_grad,
        shift_two_grad,
        gate_grad,
        up_grad,
        down_grad,
    )


def solution(mesh):
    rows = P("fsdp", "sp", None)
    vector = P(("fsdp", "sp"))
    matrix = P(("fsdp", "sp"), None)
    return jax.shard_map(
        per_device,
        mesh=mesh,
        in_specs=(rows, rows, vector, vector, matrix, vector, matrix, vector, vector, matrix, matrix, matrix),
        out_specs=(rows, rows, vector, vector, matrix, vector, matrix, vector, vector, matrix, matrix, matrix),
        check_vma=False,
    )
```

```python
import functools
import math

import jax
import jax.numpy as jnp
import numpy as np
from jax import lax
from jax.experimental import pallas as pl
from jax.experimental.pallas import tpu as pltpu
from jax.sharding import PartitionSpec as P

D = 2048
HEADS = 32
HEAD = 64
ROT = 16

epsilon = 1e-05
masked_value = -1e30
f32 = jnp.float32
bf16 = jnp.bfloat16
LOG2E_SCALE = math.log2(math.e) * HEAD**-0.5
NN = (((1,), (0,)), ((), ()))
NT = (((1,), (1,)), ((), ()))
TN = (((0,), (0,)), ((), ()))


def dot(a, b, dims):
    return lax.dot_general(a, b, dims, preferred_element_type=f32)


def params(mib=56):
    return pltpu.CompilerParams(vmem_limit_bytes=mib * 2**20)


class Plane:
    def __init__(self, count):
        outer = count // 4
        self.count = count
        self.outer = outer

        def spot(o, i, c):
            return ((o % outer) * 2 + i) * 2 + c

        def split(s):
            return s // 4, (s // 2) % 2, s % 2

        self.core = [(s, s ^ 1) for s in range(count)]
        first = []
        later = [[] for _ in range(outer - 1)]
        for s in range(count):
            o, i, c = split(s)
            swapped = outer == 2 and c == 1
            first.append((s, spot(o + 1, i, c) if swapped else spot(o, 1 - i, c)))
            for k in range(1, outer):
                later[k - 1].append((s, spot(o, 1 - i, c) if swapped else spot(o + k, i, c)))
        self.first = first
        self.later = later
        here = list(range(count))

        def moved(table, perm):
            out = [None] * count
            for a, b in perm:
                out[b] = table[a]
            return out

        blocks = [here, moved(here, first)]
        for perm in later:
            blocks += [moved(blocks[0], perm), moved(blocks[1], perm)]
        blocks += [moved(b, self.core) for b in blocks]
        self.table = np.array(blocks, np.int32).T
        self.half = 2 * outer
        self.far = list(reversed(range(2, self.half, 2)))

    @staticmethod
    def send(value, perm):
        return lax.ppermute(value, "sp", perm)

    @staticmethod
    def back(value, perm):
        return lax.ppermute(value, "sp", [(b, a) for a, b in perm])

    def gather_first(self, value):
        return (
            self.send(value, self.core),
            self.send(value, self.first),
            [self.send(value, perm) for perm in self.later],
        )

    def gather_second(self, one, twos):
        return (
            self.send(one, self.core),
            [self.send(two, self.core) for two in twos],
            [self.send(one, perm) for perm in self.later],
        )

    def gather_third(self, threes):
        return [self.send(three, self.core) for three in threes]


    def reduce_sums(self, product, deps=(), apart=False):
        far = [product(self.half + start, self.half + start + 2, (), bf16, deps) for start in self.far]
        near = product(self.half, self.half + 2, (), bf16, far)
        theirs = [self.send(value, self.core) for value in far]
        more = (True,) if apart else ()
        sums = [product(start, start + 2, ((value, 0),), bf16, near, *more) for start, value in zip(self.far, theirs)]
        return sums, self.send(near, self.core)

    def reduce_leg(self, sums):
        return [self.back(value, self.later[start // 2 - 1]) for start, value in zip(self.far, sums)]

    def reduce_next(self, product, got, theirs, deps=()):
        one = product(1, 2, tuple((t, 1) for t in [theirs] + got), bf16, deps)
        return one, self.back(one, self.first)

    def reduce_own(self, product, got, theirs, last, dtype=bf16, deps=()):
        return product(0, 1, tuple((t, 0) for t in [theirs] + got + [last]), dtype, deps)[0]


    def legs(self, sums):
        perms = [self.later[start // 2 - 1] for start in self.far]
        further = [self.back(pair[1], perm) for pair, perm in zip(sums, perms)]
        nearer = [self.back(held(pair[0], further), perm) for pair, perm in zip(sums, perms)]
        return further, nearer

    def legs_next(self, product, further, theirs, deps=()):
        one = product(1, 2, ((theirs, 1), *((t, 0) for t in further)), bf16, deps)
        return one, self.back(one, self.first)

    def legs_own(self, product, nearer, theirs, last, deps=()):
        return product(0, 1, ((theirs, 0), *((t, 0) for t in [*nearer, last])), bf16, deps)[0]


def launch(
    kernel, operands, in_specs, outs, out_specs, *, grid, name, cost, scratch=(), deps=(), aliases=None, prefetch=0, mib=60
):
    deps = jax.tree.leaves(deps)
    count = len(operands)

    def body(*refs):
        kernel(*refs[:count], *refs[count + len(deps) :])

    flops, moved, transcendentals = cost
    return pl.pallas_call(
        body,
        grid_spec=pltpu.PrefetchScalarGridSpec(
            num_scalar_prefetch=prefetch,
            grid=grid,
            in_specs=list(in_specs) + [pl.BlockSpec(memory_space=pl.ANY)] * len(deps),
            out_specs=list(out_specs),
            scratch_shapes=list(scratch),
        ),
        out_shape=list(outs),
        input_output_aliases=aliases or {},
        compiler_params=pltpu.CompilerParams(vmem_limit_bytes=mib * 2**20),
        cost_estimate=pl.CostEstimate(flops=int(flops), bytes_accessed=int(moved), transcendentals=int(transcendentals)),
        name=name,
    )(*operands, *deps)


ANYWHERE = pl.BlockSpec(memory_space=pl.ANY)


def held(value, deps):
    return launch(
        lambda *refs: None, [value], [ANYWHERE], [shape_of(value.shape, value.dtype)], [ANYWHERE],
        grid=(1,), aliases={0: 0}, deps=deps, cost=(0, 0, 0), name="held",
    )[0]


def whole(shape):
    return pl.BlockSpec(shape, lambda *_: (0,) * len(shape))


def shape_of(shape, dtype):
    return jax.ShapeDtypeStruct(shape, dtype)


def product_kernel(terms, dims, pieces, *refs):
    outs = refs[-pieces:]
    each, rows, width = outs[0].shape
    count = each * pieces
    total = dot(refs[0][...], refs[terms][...], dims)
    for t in range(1, terms):
        total += dot(refs[t][...], refs[terms + t][...], dims)
    for ref in refs[2 * terms : -pieces]:
        total += ref[...].astype(f32).reshape(count * rows, width)
    total = total.reshape(pieces, each, rows, width)
    for n, out_ref in enumerate(outs):
        out_ref[...] = total[n].astype(out_ref.dtype)


def product_of(lefts, right, dims, span):
    tile = 512
    depth = sum(left.shape[1] for left in lefts)

    def right_at(at, left):
        if dims is NT:
            return pl.BlockSpec((tile, left.shape[1]), lambda i: (i, at))
        return pl.BlockSpec((left.shape[1], tile), lambda i: (at, i))

    def product(start, stop, addends, dtype, deps=(), apart=False):
        count = stop - start
        pieces = count if apart else 1
        assert start % count == 0 and all(at % count == 0 for _, at in addends)

        def columns(at):
            return pl.BlockSpec((count, span, tile), lambda i: (at // count, 0, i))

        values = launch(
            functools.partial(product_kernel, len(lefts), dims, pieces),
            [*lefts, *[right] * len(lefts), *(value for value, _ in addends)],
            [pl.BlockSpec((count * span, a.shape[1]), lambda i: (start // count, 0)) for a in lefts]
            + [right_at(t, left) for t, left in enumerate(lefts)]
            + [columns(at) for _, at in addends],
            [shape_of((count // pieces, span, D), dtype)] * pieces,
            [pl.BlockSpec((count // pieces, span, tile), lambda i: (0, 0, i))] * pieces,
            grid=(D // tile,),
            deps=deps,
            mib=60,
            cost=(2 * count * span * D * depth, 2 * depth * (D + count * span) + 4 * count * span * D, 0),
            name="block_product",
        )
        return values if apart else values[0]

    return product


def part_kernel(table_ref, sum_ref, *refs):
    total = sum_ref[...].astype(f32)
    for ref in refs[:-1]:
        total += ref[...].astype(f32)
    refs[-1][...] = total.astype(refs[-1].dtype)


def parts_of(sums, order):
    rows = sums.shape[1]

    def part(start, stop, addends, dtype, deps=()):
        def block(at):
            return pl.BlockSpec((1, rows, D), lambda b, t: (at + b, 0, 0))

        return launch(
            part_kernel,
            [order, sums, *(value for value, _ in addends)],
            [pl.BlockSpec((1, rows, D), lambda b, t: (t[start + b], 0, 0))] + [block(at) for _, at in addends],
            [shape_of((stop - start, rows, D), dtype)],
            [block(0)],
            grid=(stop - start,),
            prefetch=1,
            deps=deps,
            cost=((stop - start) * rows * D, (stop - start) * rows * D * 4, 0),
            name="part",
        )[0]

    return part


def norm_kernel(x_ref, gain_ref, shift_ref, *rest):
    out_ref = rest[-1]
    values = x_ref[...].astype(f32)
    center = values - jnp.mean(values, axis=-1, keepdims=True)
    spread = jnp.mean(center * center, axis=-1, keepdims=True)
    out_ref[...] = (center * lax.rsqrt(spread + epsilon) * gain_ref[...] + shift_ref[...]).astype(bf16)


def norm_block(x, gain, shift, at, blocks, buffer, deps=()):
    rows = x.shape[0]
    tile = min(256, rows)
    steps = rows // tile
    row = pl.BlockSpec((1, D), lambda i: (0, 0))
    held = [] if buffer is None else [buffer]
    return launch(
        norm_kernel,
        [x, gain, shift, *held],
        [pl.BlockSpec((tile, D), lambda i: (i, 0)), row, row, *[ANYWHERE] * len(held)],
        [shape_of((blocks * rows, D), bf16)],
        [pl.BlockSpec((tile, D), lambda i: (at * steps + i, 0))],
        grid=(steps,),
        aliases={3: 0} if held else {},
        deps=deps,
        mib=60,
        cost=(rows * D * 12, rows * D * 4, rows),
        name="first_norm",
    )[0]


def cut_joint_kernel(n_sp, groups, group, in_ref, out_ref):
    for j in range(n_sp):
        for g in range(groups):
            for m in range(3):
                to = (g * 3 + m) * group
                start = m * D + (j * groups + g) * group
                out_ref[j, :, to : to + group] = in_ref[:, start : start + group]


def cut_joint(weight, n_sp, groups):
    depth = weight.shape[0]
    width = D // n_sp
    return launch(
        functools.partial(cut_joint_kernel, n_sp, groups, width // groups),
        [weight], [whole(weight.shape)], [shape_of((n_sp, depth, 3 * width), bf16)], [whole((n_sp, depth, 3 * width))],
        grid=(1,), cost=(0, weight.size * 4, 0), name="cut_joint",
    )[0]


def join_joint_kernel(n_sp, groups, group, in_ref, out_ref):
    for j in range(n_sp):
        for g in range(groups):
            for m in range(3):
                start = m * D + (j * groups + g) * group
                to = (g * 3 + m) * group
                out_ref[:, start : start + group] = in_ref[j, :, to : to + group].astype(f32)


def join_joint(value, groups):
    n_sp, depth, width = value.shape
    return launch(
        functools.partial(join_joint_kernel, n_sp, groups, width // 3 // groups),
        [value], [whole(value.shape)], [shape_of((depth, 3 * D), f32)], [whole((depth, 3 * D))],
        grid=(1,), cost=(0, depth * D * 18, 0), name="join_joint",
    )[0]


def cut_feed_kernel(n_sp, n_z, size, padded, gate_ref, up_ref, out_ref):
    out_ref[...] = jnp.zeros_like(out_ref)
    for j in range(n_sp):
        for p, ref in enumerate((gate_ref, up_ref)):
            for z in range(n_z):
                start = (z * n_sp + j) * size
                to = (p * n_z + z) * padded
                out_ref[j, :, to : to + size] = ref[:, start : start + size]


def cut_feed(gate_weight, up_weight, n_sp, n_z, padded, deps):
    depth, total = gate_weight.shape
    size = total // (n_sp * n_z)
    shape = (n_sp, depth, 2 * n_z * padded)
    return launch(
        functools.partial(cut_feed_kernel, n_sp, n_z, size, padded),
        [gate_weight, up_weight], [whole(gate_weight.shape)] * 2, [shape_of(shape, bf16)], [whole(shape)],
        grid=(1,), cost=(0, gate_weight.size * 8, 0), name="cut_feed", deps=deps,
    )[0]


def join_feed_kernel(n_sp, n_z, size, padded, in_ref, gate_ref, up_ref):
    for p, ref in enumerate((gate_ref, up_ref)):
        for z in range(n_z):
            for j in range(n_sp):
                start = (z * n_sp + j) * size
                to = (p * n_z + z) * padded
                ref[:, start : start + size] = in_ref[j, :, to : to + size].astype(f32)


def join_feed(value, n_z, size, padded):
    n_sp, depth, _ = value.shape
    shape = (depth, n_sp * n_z * size)
    return launch(
        functools.partial(join_feed_kernel, n_sp, n_z, size, padded),
        [value], [whole(value.shape)], [shape_of(shape, f32)] * 2, [whole(shape)] * 2,
        grid=(1,), cost=(0, value.size * 6, 0), name="join_feed",
    )


def norm_back_kernel(depth, n_parts, *refs):
    grad_ref, x_ref, gain_ref, beside_ref = refs[:4]
    weights = refs[4 : 4 + n_parts]
    outs = refs[4 + n_parts :]
    result_ref, sums_ref = outs[0], outs[1]
    values = x_ref[...].astype(f32)
    center = values - jnp.mean(values, axis=-1, keepdims=True)
    spread = jnp.mean(center * center, axis=-1, keepdims=True)
    inverse = lax.rsqrt(spread + epsilon)
    xhat = center * inverse
    grad = grad_ref[...].astype(f32)
    scaled = grad * gain_ref[...]
    level = jnp.mean(scaled, axis=-1, keepdims=True)
    along = jnp.mean(scaled * xhat, axis=-1, keepdims=True)
    result = beside_ref[...].astype(f32) + inverse * (scaled - level - xhat * along)
    result_ref[...] = result

    @pl.when(pl.program_id(0) == 0)
    def _():
        sums_ref[...] = jnp.zeros_like(sums_ref)

    sums_ref[0:1] += jnp.sum(grad * xhat, axis=0, keepdims=True)
    sums_ref[1:2] += jnp.sum(grad, axis=0, keepdims=True)
    if n_parts:
        branch = result.astype(bf16)
        outs[2][...] = branch
        parts = outs[3:]
        full = dot(branch, weights[0][...], NT).astype(bf16)
        for place, g, j, columns in head_pieces(parts[0].shape[0], depth, len(parts)):
            parts[g][j, :, columns] = full[:, place]


def norm_back(grad, x, gain, beside, weight=None, depth=0, n_sp=0, groups=0):
    rows = x.shape[0]
    tile = min(256, rows)
    row = pl.BlockSpec((1, D), lambda i: (0, 0))
    block = pl.BlockSpec((tile, D), lambda i: (i, 0))
    outs = [shape_of((rows, D), f32), shape_of((8, D), f32)]
    out_specs = [block, whole((8, D))]
    extra, specs = [], []
    if weight is not None:
        group = D // n_sp // groups
        extra, specs = [weight], [whole((D, D))]
        outs += [shape_of((rows, D), bf16)] + [shape_of((n_sp, rows, group), bf16)] * groups
        out_specs += [block] + [pl.BlockSpec((n_sp, tile, group), lambda i: (0, i, 0))] * groups
    return launch(
        functools.partial(norm_back_kernel, depth, len(extra)),
        [grad, x, gain, beside, *extra],
        [block, block, row, block, *specs],
        outs,
        out_specs,
        grid=(rows // tile,),
        cost=(rows * D * (20 + 2 * D * len(extra)), rows * D * 16 + 2 * D * D * len(extra), rows),
        name="norm_back",
    )


def head_pieces(n_sp, depth, groups):
    group = D // n_sp // groups
    n_z = D // n_sp // depth
    for z in range(n_z):
        for s in range(n_sp):
            j, rest = divmod((z * n_sp + s) * depth, groups * group)
            g, column = divmod(rest, group)
            yield slice((s * n_z + z) * depth, (s * n_z + z + 1) * depth), g, j, slice(column, column + depth)


def middle_kernel(groups, n_sp, depth, *refs):
    parts, (out_w, x_ref, gain_ref, shift_ref) = refs[:groups], refs[groups : groups + 4]
    middle_ref, normed_ref, again_ref, attended_ref = refs[groups + 4 :]
    for to, g, j, columns in head_pieces(n_sp, depth, groups):
        attended_ref[:, to] = parts[g][j, :, columns]
    values = x_ref[...].astype(f32) + dot(attended_ref[...], out_w[...], NN)
    middle_ref[...] = values
    center = values - jnp.mean(values, axis=-1, keepdims=True)
    spread = jnp.mean(center * center, axis=-1, keepdims=True)
    normed = (center * lax.rsqrt(spread + epsilon) * gain_ref[...] + shift_ref[...]).astype(bf16)
    normed_ref[...] = normed
    again_ref[...] = normed


def middle_of(parts, out_w, depth, x, gain, shift, deps=()):
    n_sp, rows, group = parts[0].shape
    tile = min(256, rows)
    row = pl.BlockSpec((1, D), lambda i: (0, 0))
    block = pl.BlockSpec((tile, D), lambda i: (i, 0))
    return launch(
        functools.partial(middle_kernel, len(parts), n_sp, depth),
        [*parts, out_w, x, gain, shift],
        [pl.BlockSpec((n_sp, tile, group), lambda i: (0, i, 0))] * len(parts)
        + [pl.BlockSpec((D, D), lambda i: (0, 0)), block, row, row],
        [shape_of((rows, D), f32)] + [shape_of((rows, D), bf16)] * 3,
        [block] * 4,
        grid=(rows // tile,),
        deps=deps,
        cost=(2 * rows * D * D, 2 * D * D + rows * D * 12, rows),
        name="middle",
    )


def turn(values, cosine, sine_up, sine_down):
    width = values.shape[1]
    half = ROT // 2
    return (
        values * cosine
        + pltpu.roll(values, width - half, 1) * sine_up
        + pltpu.roll(values, half, 1) * sine_down
    )


def joint_kernel(width, table_ref, x_ref, w_ref, bias_ref, cos_ref, up_ref, down_ref, *outs):
    projected = dot(x_ref[...], w_ref[...], NN) + bias_ref[...]
    tables = (cos_ref[...], up_ref[...], down_ref[...])
    for g in range(len(outs) // 3):
        part = projected[:, 3 * g * width : 3 * (g + 1) * width]
        outs[3 * g][...] = turn(part[:, :width], *tables).astype(bf16)
        outs[3 * g + 1][...] = turn(part[:, width : 2 * width], *tables).astype(bf16)
        outs[3 * g + 2][...] = part[:, 2 * width :].astype(bf16)


def joint_projection(table, normed, weight, bias, tables, span, groups):
    length = normed.shape[0]
    total = weight.shape[1]
    width = total // 3 // groups
    placed = pl.BlockSpec((span, width), lambda b, t: (t[b], 0))
    return pl.pallas_call(
        functools.partial(joint_kernel, width),
        grid_spec=pltpu.PrefetchScalarGridSpec(
            num_scalar_prefetch=1,
            grid=(length // span,),
            in_specs=[
                pl.BlockSpec((span, D), lambda b, t: (b, 0)),
                pl.BlockSpec((D, total), lambda b, t: (0, 0)),
                pl.BlockSpec((1, total), lambda b, t: (0, 0)),
                placed,
                placed,
                placed,
            ],
            out_specs=[placed] * (3 * groups),
        ),
        out_shape=[jax.ShapeDtypeStruct((length, width), bf16)] * (3 * groups),
        compiler_params=params(),
        cost_estimate=pl.CostEstimate(
            flops=2 * length * D * total, bytes_accessed=length * (D + total) * 2, transcendentals=0
        ),
        name="joint_projection",
    )(table, normed, weight, bias, *tables)


def attend_kernel(heads, bq, bk, q_ref, k_ref, v_ref, o_ref, lse_ref, qm, vt, acc, m_s, l_s):
    i = pl.program_id(0)
    length, width = k_ref.shape
    lane = lax.broadcasted_iota(jnp.int32, (1, width), 1) // HEAD

    @pl.when(i == 0)
    def _():
        def flip(b, carry):
            rows = pl.ds(pl.multiple_of(b * bk, bk), bk)
            vt[:, rows] = jnp.transpose(v_ref[rows, :])
            return carry

        lax.fori_loop(0, length // bk, flip, 0)

    q = q_ref[...]
    for h in range(heads):
        qm[h] = jnp.where(lane == h, q, jnp.zeros_like(q))
    acc[...] = jnp.zeros_like(acc)
    m_s[...] = jnp.full_like(m_s, masked_value)
    l_s[...] = jnp.zeros_like(l_s)

    def body(j, masked):
        rows = pl.ds(pl.multiple_of(j * bk, bk), bk)
        k = k_ref[rows, :]
        scores = [dot(k, qm[h], NT) for h in range(heads)]
        if masked:
            key_at = lax.broadcasted_iota(jnp.int32, scores[0].shape, 0) + j * bk
            query_at = lax.broadcasted_iota(jnp.int32, scores[0].shape, 1) + i * bq
            scores = [jnp.where(key_at <= query_at, s, masked_value) for s in scores]
        m0 = m_s[...]
        l0 = l_s[...]
        m1 = jnp.maximum(m0, jnp.concatenate([jnp.max(s, axis=0, keepdims=True) for s in scores] + [m0[heads:]], 0))
        m_s[...] = m1
        kept = jnp.exp2((m0 - m1) * LOG2E_SCALE)
        base = m1 * LOG2E_SCALE
        raised = [jnp.exp2(scores[h] * LOG2E_SCALE - base[h : h + 1]) for h in range(heads)]
        l_s[...] = l0 * kept + jnp.concatenate([jnp.sum(p, axis=0, keepdims=True) for p in raised] + [l0[heads:]], 0)
        for h in range(heads):
            part = slice(h * HEAD, (h + 1) * HEAD)
            acc[part, :] = acc[part, :] * kept[h : h + 1] + dot(vt[part, rows], raised[h].astype(bf16), NN)

    whole = (i * bq) // bk
    lax.fori_loop(0, whole, lambda j, c: (body(j, False), c)[1], 0)
    for d in range(max(1, bq // bk)):
        body(whole + d, True)
    for h in range(heads):
        part = slice(h * HEAD, (h + 1) * HEAD)
        acc[part, :] = acc[part, :] * (1.0 / l_s[h : h + 1])
    o_ref[...] = jnp.transpose(acc[...].astype(bf16))
    lse_ref[...] = m_s[...] * LOG2E_SCALE + jnp.log2(l_s[...])


def attend(q, k, v, deps=()):
    length, width = q.shape
    heads = width // HEAD
    bq, bk = min(1024, length), min(512, length)
    full = pl.BlockSpec((length, width), lambda i: (0, 0))
    return launch(
        functools.partial(attend_kernel, heads, bq, bk),
        [q, k, v],
        [pl.BlockSpec((bq, width), lambda i: (i, 0)), full, full],
        [shape_of((length, width), bf16), shape_of((8, length), f32)],
        [pl.BlockSpec((bq, width), lambda i: (i, 0)), pl.BlockSpec((8, bq), lambda i: (0, i))],
        grid=(length // bq,),
        scratch=[
            pltpu.VMEM((heads, bq, width), bf16),
            pltpu.VMEM((width, length), bf16),
            pltpu.VMEM((width, bq), f32),
            pltpu.VMEM((8, bq), f32),
            pltpu.VMEM((8, bq), f32),
        ],
        deps=deps,
        cost=(8 * length * length * width, length * width * 8, length * length * heads // 2),
        name="attend",
    )


def attend_back_kernel(
    heads, bq, bk, place_ref, q_ref, k_ref, v_ref, do_ref, o_ref, lse_ref, cos_ref, up_ref, down_ref, out_ref,
    dq_acc, dk_acc, dv_acc, delta,
):
    j = pl.program_id(0)
    length, width = q_ref.shape
    lane = lax.broadcasted_iota(jnp.int32, (1, width), 1) // HEAD

    @pl.when(j == 0)
    def _():
        dq_acc[...] = jnp.zeros_like(dq_acc)
        pick = (
            lax.broadcasted_iota(jnp.int32, (8, width), 0) == lax.broadcasted_iota(jnp.int32, (8, width), 1) // HEAD
        ).astype(f32)

        def sums(b, carry):
            rows = pl.ds(pl.multiple_of(b * bq, bq), bq)
            both = do_ref[rows, :].astype(f32) * o_ref[rows, :].astype(f32)
            delta[:, rows] = lax.dot_general(
                pick, both, NT, precision=lax.Precision.HIGHEST, preferred_element_type=f32
            )
            return carry

        lax.fori_loop(0, length // bq, sums, 0)

    key_rows = pl.ds(pl.multiple_of(j * bk, bk), bk)
    k = k_ref[key_rows, :]
    v = v_ref[key_rows, :]
    kt = jnp.transpose(k)
    dk_acc[...] = jnp.zeros_like(dk_acc)
    dv_acc[...] = jnp.zeros_like(dv_acc)

    def body(i, masked):
        rows = pl.ds(pl.multiple_of(i * bq, bq), bq)
        q = q_ref[rows, :]
        do = do_ref[rows, :]
        probs, grads, queries, results = [], [], [], []
        for h in range(heads):
            qh = jnp.where(lane == h, q, jnp.zeros_like(q))
            doh = jnp.where(lane == h, do, jnp.zeros_like(do))
            s = dot(k, qh, NT)
            p = jnp.exp2(s * LOG2E_SCALE - lse_ref[h : h + 1, rows])
            if masked:
                key_at = lax.broadcasted_iota(jnp.int32, s.shape, 0) + j * bk
                query_at = lax.broadcasted_iota(jnp.int32, s.shape, 1) + i * bq
                p = jnp.where(key_at <= query_at, p, 0.0)
            dp = dot(v, doh, NT)
            ds = p * (dp - delta[h : h + 1, rows])
            probs.append(p.astype(bf16))
            grads.append(ds.astype(bf16))
            queries.append(qh)
            results.append(doh)
        dv_acc[...] += dot(jnp.concatenate(probs, 1), jnp.concatenate(results, 0), NN)
        dk_acc[...] += dot(jnp.concatenate(grads, 1), jnp.concatenate(queries, 0), NN)
        for h in range(heads):
            part = slice(h * HEAD, (h + 1) * HEAD)
            dq_acc[part, rows] += dot(kt[part], grads[h], NN)

    first = (j * bk) // bq
    near = max(1, bk // bq)
    for d in range(near):
        body(first + d, True)
    lax.fori_loop(first + near, length // bq, lambda i, c: (body(i, False), c)[1], 0)
    scale = HEAD**-0.5
    tables = (cos_ref[...], -up_ref[...], -down_ref[...])
    dq = (jnp.transpose(dq_acc[:, key_rows]) * scale).astype(bf16).astype(f32)
    dk = (dk_acc[...] * scale).astype(bf16).astype(f32)
    out_ref[:, :width] = turn(dq, *tables).astype(bf16)
    out_ref[:, width : 2 * width] = turn(dk, *tables).astype(bf16)
    out_ref[:, 2 * width :] = dv_acc[...].astype(bf16)


def attend_back(place, q, k, v, do, o, lse, tables, span, deps=()):
    length, width = q.shape
    heads = width // HEAD
    bq = min(512, length)
    bk = span
    full = pl.BlockSpec((length, width), lambda i, t: (0, 0))
    block = pl.BlockSpec((bk, width), lambda i, t: (i, 0))
    return launch(
        functools.partial(attend_back_kernel, heads, bq, bk),
        [place, q, k, v, do, o, lse, *tables],
        [full] * 5 + [pl.BlockSpec((8, length), lambda i, t: (0, 0))] + [block] * 3,
        [shape_of((length, 3 * width), bf16)],
        [pl.BlockSpec((bk, 3 * width), lambda i, t: (t[i], 0))],
        grid=(length // bk,),
        prefetch=1,
        scratch=[
            pltpu.VMEM((width, length), f32),
            pltpu.VMEM((bk, width), f32),
            pltpu.VMEM((bk, width), f32),
            pltpu.VMEM((8, length), f32),
        ],
        deps=deps,
        cost=(12 * length * length * width, length * width * 16, length * length * heads // 2),
        name="attend_back",
    )[0]


def feed_kernel(ff, x0, x1, c0, c1, wgu_ref, wd_ref, *rest):
    hidden_ref, grad_ref, x_ref, c_ref = rest[-4:]
    which = pl.program_id(0)

    @pl.when(which == 0)
    def _():
        x_ref[...] = x0[...]
        c_ref[...] = c0[...]

    @pl.when(which == 1)
    def _():
        x_ref[...] = x1[...]
        c_ref[...] = c1[...]

    both = dot(x_ref[...], wgu_ref[...], NN)
    hidden_grad = dot(c_ref[...], wd_ref[...], NT)
    gate = both[:, :ff]
    up = both[:, ff:]
    open_ = jax.nn.sigmoid(gate)
    swished = gate * open_
    hidden_ref[...] = (swished * up).astype(bf16)
    grad_ref[:, :ff] = (hidden_grad * up * open_ * (1.0 + gate * (1.0 - open_))).astype(bf16)
    grad_ref[:, ff:] = (hidden_grad * swished).astype(bf16)


def feed_block(pair, cot_pair, gate_up, down, at, half, buffers, deps=()):
    rows = pair[0].shape[0]
    ff = down.shape[0]
    tile = min(256, rows)
    steps = rows // tile
    length = 2 * half * rows
    early = pl.BlockSpec((tile, D), lambda p, i: (jnp.where(p == 0, i, steps - 1), 0))
    late = pl.BlockSpec((tile, D), lambda p, i: (jnp.where(p == 0, 0, i), 0))
    operands = [pair[0], pair[1], cot_pair[0], cot_pair[1], gate_up, down]
    specs = [
        early,
        late,
        early,
        late,
        pl.BlockSpec((D, 2 * ff), lambda p, i: (0, 0)),
        pl.BlockSpec((ff, D), lambda p, i: (0, 0)),
    ]
    aliases = {}
    if buffers is not None:
        aliases = {len(operands) + n: n for n in range(4)}
        operands += list(buffers)
        specs += [pl.BlockSpec(memory_space=pl.ANY)] * 4

    def place(p, i):
        return ((p * half + at) * steps + i, 0)

    return launch(
        functools.partial(feed_kernel, ff),
        operands,
        specs,
        [
            shape_of((length, ff), bf16),
            shape_of((length, 2 * ff), bf16),
            shape_of((length, D), bf16),
            shape_of((length, D), bf16),
        ],
        [
            pl.BlockSpec((tile, ff), place),
            pl.BlockSpec((tile, 2 * ff), place),
            pl.BlockSpec((tile, D), place),
            pl.BlockSpec((tile, D), place),
        ],
        grid=(2, steps),
        aliases=aliases,
        deps=deps,
        cost=(12 * rows * D * ff, 6 * D * ff + rows * D * 16, 2 * rows * ff),
        name="feed_forward",
    )


def rotary_columns(length, width):
    half = ROT // 2
    indices = np.arange(half, dtype=np.float32)
    inverse = np.float32(1.0) / np.float32(10000.0) ** (indices * np.float32(2.0 / ROT))
    angles = np.arange(length, dtype=np.float32)[:, None] * inverse[None, :].astype(np.float32)
    cosine, sine = np.cos(angles.astype(np.float64)), np.sin(angles.astype(np.float64))
    rest = np.zeros((length, HEAD - ROT))
    none = np.zeros((length, half))
    one_head = (
        np.concatenate([cosine, cosine, rest + 1.0], -1),
        np.concatenate([-sine, none, rest], -1),
        np.concatenate([none, sine, rest], -1),
    )
    return tuple(jnp.asarray(np.tile(t, (1, width // HEAD)).astype(np.float32)) for t in one_head)


def swap_sp(value):
    return lax.all_to_all(value, "sp", split_axis=0, concat_axis=0, tiled=True)


def in_line(blocks, mine):
    count, rows = len(blocks), blocks[0].shape[0]
    total = jnp.zeros((count * rows, blocks[0].shape[1]), blocks[0].dtype)
    for step, block in enumerate(blocks):
        total = lax.dynamic_update_slice(total, block, (lax.rem(mine - step + count, count) * rows, 0))
    return total


def per_device(
    tokens, cotangent, first_gain, first_shift, joint_weight, joint_bias, out_weight, second_gain, second_shift,
    gate_weight, up_weight, down_weight,
):
    n_sp = lax.axis_size("sp")
    n_z = lax.axis_size("fsdp")
    n_all = n_sp * n_z
    plane = Plane(n_sp)
    half = plane.half
    me = lax.axis_index("sp")
    span = tokens.shape[1]
    length = n_sp * span
    width = D // n_sp
    depth = joint_weight.shape[0]
    ff_rows = down_weight.shape[0]
    unit = max(16, 128 // n_z)
    ff_pad = -(-ff_rows // unit) * unit
    ff = n_z * ff_pad

    order = jnp.asarray(plane.table)[me]
    place = jnp.asarray(np.argsort(plane.table, axis=1).astype(np.int32))[me]
    groups = 2 if width % 256 == 0 else 1
    group = width // groups
    my_z = lax.axis_index("fsdp")

    small = jnp.concatenate([first_gain, first_shift, second_gain, second_shift, joint_bias])
    small = jnp.broadcast_to(small[None], (n_all, small.shape[0]))
    small_all = lax.all_to_all(small, ("fsdp", "sp"), split_axis=0, concat_axis=0, tiled=True)
    small = small_all.astype(f32)
    n_gain = first_gain.shape[0]
    gain_one, shift_one, gain_two, shift_two = (
        small[:, i * n_gain : (i + 1) * n_gain].reshape(1, D) for i in range(4)
    )
    bias_all = small[:, 4 * n_gain :].reshape(3, n_sp, width)
    bias = lax.dynamic_index_in_dim(bias_all, me, axis=1, keepdims=False)
    bias = bias.reshape(3, groups, group).transpose(1, 0, 2).reshape(1, 3 * width)

    ring = [(i, (i + 1) % n_z) for i in range(n_z)]
    joint_block = swap_sp(cut_joint(joint_weight, n_sp, groups)).reshape(n_sp * depth, 3 * width)
    out_blocks = [out_weight]
    for _ in range(n_z - 1):
        out_blocks.append(lax.ppermute(out_blocks[-1], "fsdp", ring))
    out_rows = in_line(out_blocks, my_z)
    joint_blocks = [held(joint_block, out_blocks[1:])]
    for _ in range(n_z - 1):
        joint_blocks.append(lax.ppermute(joint_blocks[-1], "fsdp", ring))
    joint_mine = in_line(joint_blocks, my_z)

    gate_up_cols = cut_feed(gate_weight, up_weight, n_sp, n_z, ff_pad, ())
    down_rows = jnp.pad(down_weight, ((0, ff_pad - ff_rows), (0, 0)))
    x = tokens.reshape(span, D)
    normed = None

    def norm_next(normed, block, t, deps=()):
        return norm_block(block, gain_one, shift_one, t, n_sp, normed, deps)

    partner, one, twos = plane.gather_first(x)
    normed = norm_next(None, x, 0)
    normed = norm_next(normed, partner, half)
    cot = held(cotangent.reshape(span, D), small_all)
    one = held(one, (normed, joint_blocks[1:3], gate_up_cols, cot))
    one_other, two_others, threes = plane.gather_second(one, twos)
    normed = norm_next(normed, one, 1)
    for n, two in enumerate(twos):
        normed = norm_next(normed, two, 2 + 2 * n)
    normed = norm_next(normed, one_other, half + 1)
    for n, two in enumerate(two_others):
        normed = norm_next(normed, two, half + 2 + 2 * n)
    threes = [held(three, (normed, joint_mine, bias)) if n == 0 else three for n, three in enumerate(threes)]
    for n, three in enumerate(threes):
        normed = norm_next(normed, three, 3 + 2 * n)
    for n, three in enumerate(plane.gather_third(threes)):
        normed = norm_next(normed, three, half + 3 + 2 * n)
    tables = rotary_columns(length, group)
    heads = joint_projection(order, normed, joint_mine, bias, tables, span, groups)

    out_full = lax.all_gather(held(out_rows, threes), "sp", axis=0, tiled=True)
    down = lax.all_gather(held(down_rows, threes), "fsdp", axis=0, tiled=True)
    gate_up_blocks = [held(swap_sp(held(gate_up_cols, threes)).reshape(n_sp * depth, 2 * ff), heads[0])]
    gate_up_blocks.append(lax.ppermute(gate_up_blocks[0], "fsdp", ring))
    cot = held(cot, gate_up_blocks[0])
    cot_partner, cot_one, cot_twos = plane.gather_first(cot)
    results = [attend(*heads[:3])]
    cot_one = held(cot_one, results[0][1])
    gate_up_blocks[1] = held(gate_up_blocks[1], results[0][1])
    gate_up_blocks.append(lax.ppermute(gate_up_blocks[1], "fsdp", ring))
    cot_one_other, cot_two_others, cot_threes = plane.gather_second(cot_one, cot_twos)
    for g in range(1, groups):
        results.append(attend(*heads[3 * g : 3 * g + 3], (cot_partner, cot_one, cot_twos, gate_up_blocks[1])))
    gate_up_blocks[2] = held(gate_up_blocks[2], results[-1][1])
    for _ in range(3, n_z):
        gate_up_blocks.append(lax.ppermute(gate_up_blocks[-1], "fsdp", ring))
    cot_three_others = plane.gather_third(cot_threes)
    cot_blocks, cot_partners = [cot, cot_one], [cot_partner, cot_one_other]
    for pieces in zip(cot_twos, cot_threes):
        cot_blocks += pieces
    for pieces in zip(cot_two_others, cot_three_others):
        cot_partners += pieces
    gate_up = in_line(gate_up_blocks, my_z)
    results[-1] = (held(results[-1][0], cot_threes), results[-1][1])
    attended = [swap_sp(o).reshape(n_sp, span, group) for o, _ in results]
    middle, normed_two, normed_again, attended_all = middle_of(
        attended, out_full, depth, x, gain_two, shift_two, (gate_up, down)
    )

    feed = None

    def feed_next(feed, pair, t, deps=()):
        return feed_block(pair, (cot_blocks[t], cot_partners[t]), gate_up, down, t, half, feed, deps)

    partner = plane.send(normed_two, plane.core)
    one = plane.send(normed_two, plane.first)
    feed = feed_next(None, (normed_two, partner), 0)
    one = held(one, feed[0])
    one_other = plane.send(one, plane.core)
    again = held(normed_again, one)
    for n, perm in enumerate(plane.later):
        two = plane.send(again, perm)
        if n == 0:
            feed = feed_next(feed, (one, one_other), 1, again)
        two = held(two, feed[0])
        one = held(one, (two, one_other))
        three = plane.send(one, perm)
        feed = feed_next(feed, (two, plane.send(two, plane.core)), 2 + 2 * n)
        three = held(three, feed[0])
        feed = feed_next(feed, (three, plane.send(three, plane.core)), 3 + 2 * n)
    hidden, gate_up_grad, two_all, cot_all = feed

    two_product = product_of([gate_up_grad], gate_up, NT, span)
    out_product = product_of([hidden], down, NN, span)
    two_far, two_theirs = plane.reduce_sums(two_product, (), True)
    further, nearer = plane.legs(two_far)
    down_sum = dot(hidden, held(cot_all, two_far), TN).astype(bf16)
    two_one, two_last = plane.legs_next(two_product, further, two_theirs, down_sum)
    gate_up_sum = dot(held(two_all, two_one), gate_up_grad, TN).astype(bf16)
    down_part = lax.psum_scatter(held(down_sum, two_one), "fsdp", scatter_dimension=0, tiled=True)
    two_grad = plane.legs_own(two_product, nearer, two_theirs, two_last, gate_up_sum)
    gate_up_part = lax.psum_scatter(held(gate_up_sum, two_grad), "fsdp", scatter_dimension=0, tiled=True)
    middle_grad, two_sums, branch_grad, *parts = norm_back(
        two_grad, middle, gain_two, cot, out_full, depth, n_sp, groups
    )
    dos = [swap_sp(part).reshape(n_sp * span, group) for part in parts]
    out_sum = dot(attended_all, branch_grad, TN).astype(bf16).reshape(n_sp, n_z * depth, D)

    out_sums, out_theirs = plane.reduce_sums(out_product, branch_grad)
    out_got = plane.reduce_leg(out_sums)
    rows = attend_back(place, *heads[:3], dos[0], *results[0], tables, span, out_sums)
    joint_rows = [rows]
    joint_sums = [dot(normed, rows, TN).astype(bf16)]
    joint_parts = [lax.psum_scatter(joint_sums[0], "fsdp", scatter_dimension=0, tiled=True)]
    out_one, out_last = plane.reduce_next(out_product, out_got, out_theirs)
    out_weight_part = parts_of(out_sum, order)
    weight_sums, weight_theirs = plane.reduce_sums(out_weight_part)
    weight_got = plane.reduce_leg(weight_sums)
    gate_up_own = swap_sp(gate_up_part)
    for g in range(1, groups):
        deps = (joint_sums, out_one, weight_sums, weight_theirs)
        rows = attend_back(place, *heads[3 * g : 3 * g + 3], dos[g], *results[g], tables, span, deps)
        joint_rows.append(rows)
    _, weight_last = plane.reduce_next(out_weight_part, weight_got, weight_theirs)

    normed_product = product_of(joint_rows, joint_mine, NT, span)
    normed_far, normed_theirs = plane.reduce_sums(normed_product, (out_last, weight_got, joint_parts, down_part, gate_up_own), True)
    further, nearer = plane.legs(normed_far)
    last_normed = held(normed, (normed_far, joint_sums))
    for g in range(1, groups):
        joint_sums.append(dot(last_normed, joint_rows[g], TN).astype(bf16))
        joint_parts.append(lax.psum_scatter(joint_sums[g], "fsdp", scatter_dimension=0, tiled=True))
    normed_one, normed_last = plane.legs_next(
        normed_product, further, normed_theirs, joint_sums
    )
    output = (middle + plane.reduce_own(out_product, out_got, out_theirs, out_last, f32)).astype(bf16)
    out_own = plane.reduce_own(out_weight_part, weight_got, weight_theirs, weight_last)
    out_grad = lax.psum_scatter(held(out_own, joint_parts), "fsdp", scatter_dimension=0, tiled=True).astype(f32)
    down_grad = down_part[:ff_rows].astype(f32)
    gate_grad, up_grad = join_feed(gate_up_own.reshape(n_sp, depth, 2 * ff), n_z, ff_rows, ff_pad)
    bias_sum = jnp.stack([jnp.sum(r.astype(f32), axis=0).reshape(3, group) for r in joint_rows], 1)
    bias_sum = bias_sum.reshape(3, 1, width)
    bias_sum = lax.dynamic_update_slice(jnp.zeros((3, n_sp, width), f32), bias_sum, (0, me, 0))
    joint_own = jnp.concatenate(joint_parts, axis=1)
    joint_grad = join_joint(swap_sp(joint_own).reshape(n_sp, depth, 3 * width), groups)
    fill = (output, out_own, gate_grad, up_grad, bias_sum, joint_grad)
    normed_grad = plane.legs_own(normed_product, nearer, normed_theirs, normed_last, fill)
    tokens_grad, one_sums = norm_back(normed_grad, x, gain_one, middle_grad)
    tokens_grad = tokens_grad.reshape(tokens.shape)

    sums = [one_sums[0], one_sums[1], two_sums[0], two_sums[1]]
    sums = jnp.concatenate([s.reshape(n_all, n_gain) for s in sums] + [bias_sum.reshape(n_all, -1)], axis=1)
    sums = jnp.sum(lax.all_to_all(sums, ("fsdp", "sp"), split_axis=0, concat_axis=0, tiled=True), axis=0)
    gain_one_grad, shift_one_grad, gain_two_grad, shift_two_grad = (
        sums[i * n_gain : (i + 1) * n_gain] for i in range(4)
    )
    return (
        output.reshape(tokens.shape),
        tokens_grad,
        gain_one_grad,
        shift_one_grad,
        joint_grad,
        sums[4 * n_gain :],
        out_grad,
        gain_two_grad,
        shift_two_grad,
        gate_grad,
        up_grad,
        down_grad,
    )


def solution(mesh):
    rows = P("fsdp", "sp", None)
    vector = P(("fsdp", "sp"))
    matrix = P(("fsdp", "sp"), None)
    return jax.shard_map(
        per_device,
        mesh=mesh,
        in_specs=(rows, rows, vector, vector, matrix, vector, matrix, vector, vector, matrix, matrix, matrix),
        out_specs=(rows, rows, vector, vector, matrix, vector, matrix, vector, vector, matrix, matrix, matrix),
        check_vma=False,
    )
```

```python
import functools
import math

import jax
import jax.numpy as jnp
import numpy as np
from jax import lax
from jax.experimental import pallas as pl
from jax.experimental.pallas import tpu as pltpu
from jax.sharding import PartitionSpec as P

D = 2048
HEADS = 32
HEAD = 64
ROT = 16

epsilon = 1e-05
masked_value = -1e30
f32 = jnp.float32
bf16 = jnp.bfloat16
LOG2E_SCALE = math.log2(math.e) * HEAD**-0.5
NN = (((1,), (0,)), ((), ()))
NT = (((1,), (1,)), ((), ()))
TN = (((0,), (0,)), ((), ()))


def dot(a, b, dims):
    return lax.dot_general(a, b, dims, preferred_element_type=f32)


def params(mib=56):
    return pltpu.CompilerParams(vmem_limit_bytes=mib * 2**20)


class Plane:
    def __init__(self, count):
        outer = count // 4
        self.count = count
        self.outer = outer

        def spot(o, i, c):
            return ((o % outer) * 2 + i) * 2 + c

        def split(s):
            return s // 4, (s // 2) % 2, s % 2

        self.core = [(s, s ^ 1) for s in range(count)]
        first = []
        later = [[] for _ in range(outer - 1)]
        for s in range(count):
            o, i, c = split(s)
            swapped = outer == 2 and c == 1
            first.append((s, spot(o + 1, i, c) if swapped else spot(o, 1 - i, c)))
            for k in range(1, outer):
                later[k - 1].append((s, spot(o, 1 - i, c) if swapped else spot(o + k, i, c)))
        self.first = first
        self.later = later
        here = list(range(count))

        def moved(table, perm):
            out = [None] * count
            for a, b in perm:
                out[b] = table[a]
            return out

        blocks = [here, moved(here, first)]
        for perm in later:
            blocks += [moved(blocks[0], perm), moved(blocks[1], perm)]
        blocks += [moved(b, self.core) for b in blocks]
        self.table = np.array(blocks, np.int32).T
        self.half = 2 * outer
        self.far = list(reversed(range(2, self.half, 2)))

    @staticmethod
    def send(value, perm):
        return lax.ppermute(value, "sp", perm)

    @staticmethod
    def back(value, perm):
        return lax.ppermute(value, "sp", [(b, a) for a, b in perm])

    def gather_first(self, value):
        return (
            self.send(value, self.core),
            self.send(value, self.first),
            [self.send(value, perm) for perm in self.later],
        )

    def gather_second(self, one, twos):
        return (
            self.send(one, self.core),
            [self.send(two, self.core) for two in twos],
            [self.send(one, perm) for perm in self.later],
        )

    def gather_third(self, threes):
        return [self.send(three, self.core) for three in threes]


    def reduce_sums(self, product, deps=(), apart=False):
        far = [product(self.half + start, self.half + start + 2, (), bf16, deps) for start in self.far]
        near = product(self.half, self.half + 2, (), bf16, far)
        theirs = [self.send(value, self.core) for value in far]
        more = (True,) if apart else ()
        sums = [product(start, start + 2, ((value, 0),), bf16, near, *more) for start, value in zip(self.far, theirs)]
        return sums, self.send(near, self.core)

    def reduce_leg(self, sums):
        return [self.back(value, self.later[start // 2 - 1]) for start, value in zip(self.far, sums)]

    def reduce_next(self, product, got, theirs, deps=()):
        one = product(1, 2, tuple((t, 1) for t in [theirs] + got), bf16, deps)
        return one, self.back(one, self.first)

    def reduce_own(self, product, got, theirs, last, dtype=bf16, deps=()):
        return product(0, 1, tuple((t, 0) for t in [theirs] + got + [last]), dtype, deps)[0]


    def legs(self, sums):
        perms = [self.later[start // 2 - 1] for start in self.far]
        further = [self.back(pair[1], perm) for pair, perm in zip(sums, perms)]
        nearer = [self.back(held(pair[0], further), perm) for pair, perm in zip(sums, perms)]
        return further, nearer

    def legs_next(self, product, further, theirs, deps=()):
        one = product(1, 2, ((theirs, 1), *((t, 0) for t in further)), bf16, deps)
        return one, self.back(one, self.first)

    def legs_own(self, product, nearer, theirs, last, deps=()):
        return product(0, 1, ((theirs, 0), *((t, 0) for t in [*nearer, last])), bf16, deps)[0]


def launch(
    kernel, operands, in_specs, outs, out_specs, *, grid, name, cost, scratch=(), deps=(), aliases=None, prefetch=0, mib=60
):
    deps = jax.tree.leaves(deps)
    count = len(operands)

    def body(*refs):
        kernel(*refs[:count], *refs[count + len(deps) :])

    flops, moved, transcendentals = cost
    return pl.pallas_call(
        body,
        grid_spec=pltpu.PrefetchScalarGridSpec(
            num_scalar_prefetch=prefetch,
            grid=grid,
            in_specs=list(in_specs) + [pl.BlockSpec(memory_space=pl.ANY)] * len(deps),
            out_specs=list(out_specs),
            scratch_shapes=list(scratch),
        ),
        out_shape=list(outs),
        input_output_aliases=aliases or {},
        compiler_params=pltpu.CompilerParams(vmem_limit_bytes=mib * 2**20),
        cost_estimate=pl.CostEstimate(flops=int(flops), bytes_accessed=int(moved), transcendentals=int(transcendentals)),
        name=name,
    )(*operands, *deps)


ANYWHERE = pl.BlockSpec(memory_space=pl.ANY)


def held(value, deps):
    return launch(
        lambda *refs: None, [value], [ANYWHERE], [shape_of(value.shape, value.dtype)], [ANYWHERE],
        grid=(1,), aliases={0: 0}, deps=deps, cost=(0, 0, 0), name="held",
    )[0]


def whole(shape):
    return pl.BlockSpec(shape, lambda *_: (0,) * len(shape))


def shape_of(shape, dtype):
    return jax.ShapeDtypeStruct(shape, dtype)


def product_kernel(terms, dims, pieces, *refs):
    outs = refs[-pieces:]
    each, rows, width = outs[0].shape
    count = each * pieces
    total = dot(refs[0][...], refs[terms][...], dims)
    for t in range(1, terms):
        total += dot(refs[t][...], refs[terms + t][...], dims)
    for ref in refs[2 * terms : -pieces]:
        total += ref[...].astype(f32).reshape(count * rows, width)
    total = total.reshape(pieces, each, rows, width)
    for n, out_ref in enumerate(outs):
        out_ref[...] = total[n].astype(out_ref.dtype)


def product_of(lefts, right, dims, span):
    tile = 512
    depth = sum(left.shape[1] for left in lefts)

    def right_at(at, left):
        if dims is NT:
            return pl.BlockSpec((tile, left.shape[1]), lambda i: (i, at))
        return pl.BlockSpec((left.shape[1], tile), lambda i: (at, i))

    def product(start, stop, addends, dtype, deps=(), apart=False):
        count = stop - start
        pieces = count if apart else 1
        assert start % count == 0 and all(at % count == 0 for _, at in addends)

        def columns(at):
            return pl.BlockSpec((count, span, tile), lambda i: (at // count, 0, i))

        values = launch(
            functools.partial(product_kernel, len(lefts), dims, pieces),
            [*lefts, *[right] * len(lefts), *(value for value, _ in addends)],
            [pl.BlockSpec((count * span, a.shape[1]), lambda i: (start // count, 0)) for a in lefts]
            + [right_at(t, left) for t, left in enumerate(lefts)]
            + [columns(at) for _, at in addends],
            [shape_of((count // pieces, span, D), dtype)] * pieces,
            [pl.BlockSpec((count // pieces, span, tile), lambda i: (0, 0, i))] * pieces,
            grid=(D // tile,),
            deps=deps,
            mib=60,
            cost=(2 * count * span * D * depth, 2 * depth * (D + count * span) + 4 * count * span * D, 0),
            name="block_product",
        )
        return values if apart else values[0]

    return product


def part_kernel(table_ref, sum_ref, *refs):
    total = sum_ref[...].astype(f32)
    for ref in refs[:-1]:
        total += ref[...].astype(f32)
    refs[-1][...] = total.astype(refs[-1].dtype)


def parts_of(sums, order):
    rows = sums.shape[1]

    def part(start, stop, addends, dtype, deps=()):
        def block(at):
            return pl.BlockSpec((1, rows, D), lambda b, t: (at + b, 0, 0))

        return launch(
            part_kernel,
            [order, sums, *(value for value, _ in addends)],
            [pl.BlockSpec((1, rows, D), lambda b, t: (t[start + b], 0, 0))] + [block(at) for _, at in addends],
            [shape_of((stop - start, rows, D), dtype)],
            [block(0)],
            grid=(stop - start,),
            prefetch=1,
            deps=deps,
            cost=((stop - start) * rows * D, (stop - start) * rows * D * 4, 0),
            name="part",
        )[0]

    return part


def norm_kernel(x_ref, gain_ref, shift_ref, *rest):
    out_ref = rest[-1]
    values = x_ref[...].astype(f32)
    center = values - jnp.mean(values, axis=-1, keepdims=True)
    spread = jnp.mean(center * center, axis=-1, keepdims=True)
    out_ref[...] = (center * lax.rsqrt(spread + epsilon) * gain_ref[...] + shift_ref[...]).astype(bf16)


def norm_block(x, gain, shift, at, blocks, buffer, deps=()):
    rows = x.shape[0]
    tile = min(256, rows)
    steps = rows // tile
    row = pl.BlockSpec((1, D), lambda i: (0, 0))
    held = [] if buffer is None else [buffer]
    return launch(
        norm_kernel,
        [x, gain, shift, *held],
        [pl.BlockSpec((tile, D), lambda i: (i, 0)), row, row, *[ANYWHERE] * len(held)],
        [shape_of((blocks * rows, D), bf16)],
        [pl.BlockSpec((tile, D), lambda i: (at * steps + i, 0))],
        grid=(steps,),
        aliases={3: 0} if held else {},
        deps=deps,
        mib=60,
        cost=(rows * D * 12, rows * D * 4, rows),
        name="first_norm",
    )[0]


def cut_joint_kernel(n_sp, groups, group, in_ref, out_ref):
    for j in range(n_sp):
        for g in range(groups):
            for m in range(3):
                to = (g * 3 + m) * group
                start = m * D + (j * groups + g) * group
                out_ref[j, :, to : to + group] = in_ref[:, start : start + group]


def cut_joint(weight, n_sp, groups):
    depth = weight.shape[0]
    width = D // n_sp
    return launch(
        functools.partial(cut_joint_kernel, n_sp, groups, width // groups),
        [weight], [whole(weight.shape)], [shape_of((n_sp, depth, 3 * width), bf16)], [whole((n_sp, depth, 3 * width))],
        grid=(1,), cost=(0, weight.size * 4, 0), name="cut_joint",
    )[0]


def join_joint_kernel(n_sp, groups, group, in_ref, out_ref):
    for j in range(n_sp):
        for g in range(groups):
            for m in range(3):
                start = m * D + (j * groups + g) * group
                to = (g * 3 + m) * group
                out_ref[:, start : start + group] = in_ref[j, :, to : to + group].astype(f32)


def join_joint(value, groups):
    n_sp, depth, width = value.shape
    return launch(
        functools.partial(join_joint_kernel, n_sp, groups, width // 3 // groups),
        [value], [whole(value.shape)], [shape_of((depth, 3 * D), f32)], [whole((depth, 3 * D))],
        grid=(1,), cost=(0, depth * D * 18, 0), name="join_joint",
    )[0]


def cut_feed_kernel(n_sp, n_z, size, padded, gate_ref, up_ref, beside_ref, out_ref, copy_ref):
    copy_ref[...] = beside_ref[...]
    out_ref[...] = jnp.zeros_like(out_ref)
    for j in range(n_sp):
        for p, ref in enumerate((gate_ref, up_ref)):
            for z in range(n_z):
                start = (z * n_sp + j) * size
                to = (p * n_z + z) * padded
                out_ref[j, :, to : to + size] = ref[:, start : start + size]


def cut_feed(gate_weight, up_weight, beside, n_sp, n_z, padded):
    depth, total = gate_weight.shape
    size = total // (n_sp * n_z)
    shape = (n_sp, depth, 2 * n_z * padded)
    return launch(
        functools.partial(cut_feed_kernel, n_sp, n_z, size, padded),
        [gate_weight, up_weight, beside],
        [whole(gate_weight.shape)] * 2 + [whole(beside.shape)],
        [shape_of(shape, bf16), shape_of(beside.shape, beside.dtype)],
        [whole(shape), whole(beside.shape)],
        grid=(1,), cost=(0, gate_weight.size * 8, 0), name="cut_feed",
    )


def join_feed_kernel(n_sp, n_z, size, padded, in_ref, gate_ref, up_ref):
    for p, ref in enumerate((gate_ref, up_ref)):
        for z in range(n_z):
            for j in range(n_sp):
                start = (z * n_sp + j) * size
                to = (p * n_z + z) * padded
                ref[:, start : start + size] = in_ref[j, :, to : to + size].astype(f32)


def join_feed(value, n_z, size, padded):
    n_sp, depth, _ = value.shape
    shape = (depth, n_sp * n_z * size)
    return launch(
        functools.partial(join_feed_kernel, n_sp, n_z, size, padded),
        [value], [whole(value.shape)], [shape_of(shape, f32)] * 2, [whole(shape)] * 2,
        grid=(1,), cost=(0, value.size * 6, 0), name="join_feed",
    )


def norm_back_kernel(depth, n_parts, *refs):
    grad_ref, x_ref, gain_ref, beside_ref = refs[:4]
    weights = refs[4 : 4 + n_parts]
    outs = refs[4 + n_parts :]
    result_ref, sums_ref = outs[0], outs[1]
    values = x_ref[...].astype(f32)
    center = values - jnp.mean(values, axis=-1, keepdims=True)
    spread = jnp.mean(center * center, axis=-1, keepdims=True)
    inverse = lax.rsqrt(spread + epsilon)
    xhat = center * inverse
    grad = grad_ref[...].astype(f32)
    scaled = grad * gain_ref[...]
    level = jnp.mean(scaled, axis=-1, keepdims=True)
    along = jnp.mean(scaled * xhat, axis=-1, keepdims=True)
    result = beside_ref[...].astype(f32) + inverse * (scaled - level - xhat * along)
    result_ref[...] = result

    @pl.when(pl.program_id(0) == 0)
    def _():
        sums_ref[...] = jnp.zeros_like(sums_ref)

    sums_ref[0:1] += jnp.sum(grad * xhat, axis=0, keepdims=True)
    sums_ref[1:2] += jnp.sum(grad, axis=0, keepdims=True)
    if n_parts:
        branch = result.astype(bf16)
        outs[2][...] = branch
        parts = outs[3:]
        full = dot(branch, weights[0][...], NT).astype(bf16)
        for place, g, j, columns in head_pieces(parts[0].shape[0], depth, len(parts)):
            parts[g][j, :, columns] = full[:, place]


def norm_back(grad, x, gain, beside, weight=None, depth=0, n_sp=0, groups=0, deps=()):
    rows = x.shape[0]
    tile = min(256, rows)
    row = pl.BlockSpec((1, D), lambda i: (0, 0))
    block = pl.BlockSpec((tile, D), lambda i: (i, 0))
    outs = [shape_of((rows, D), f32), shape_of((8, D), f32)]
    out_specs = [block, whole((8, D))]
    extra, specs = [], []
    if weight is not None:
        group = D // n_sp // groups
        extra, specs = [weight], [whole((D, D))]
        outs += [shape_of((rows, D), bf16)] + [shape_of((n_sp, rows, group), bf16)] * groups
        out_specs += [block] + [pl.BlockSpec((n_sp, tile, group), lambda i: (0, i, 0))] * groups
    return launch(
        functools.partial(norm_back_kernel, depth, len(extra)),
        [grad, x, gain, beside, *extra],
        [block, block, row, block, *specs],
        outs,
        out_specs,
        grid=(rows // tile,),
        cost=(rows * D * (20 + 2 * D * len(extra)), rows * D * 16 + 2 * D * D * len(extra), rows),
        deps=deps,
        name="norm_back",
    )


def head_pieces(n_sp, depth, groups):
    group = D // n_sp // groups
    n_z = D // n_sp // depth
    for z in range(n_z):
        for s in range(n_sp):
            j, rest = divmod((z * n_sp + s) * depth, groups * group)
            g, column = divmod(rest, group)
            yield slice((s * n_z + z) * depth, (s * n_z + z + 1) * depth), g, j, slice(column, column + depth)


def middle_kernel(groups, n_sp, depth, *refs):
    parts, (out_w, x_ref, gain_ref, shift_ref) = refs[:groups], refs[groups : groups + 4]
    middle_ref, normed_ref, again_ref, attended_ref = refs[groups + 4 :]
    for to, g, j, columns in head_pieces(n_sp, depth, groups):
        attended_ref[:, to] = parts[g][j, :, columns]
    values = x_ref[...].astype(f32) + dot(attended_ref[...], out_w[...], NN)
    middle_ref[...] = values
    center = values - jnp.mean(values, axis=-1, keepdims=True)
    spread = jnp.mean(center * center, axis=-1, keepdims=True)
    normed = (center * lax.rsqrt(spread + epsilon) * gain_ref[...] + shift_ref[...]).astype(bf16)
    normed_ref[...] = normed
    again_ref[...] = normed


def middle_of(parts, out_w, depth, x, gain, shift, deps=()):
    n_sp, rows, group = parts[0].shape
    tile = min(256, rows)
    row = pl.BlockSpec((1, D), lambda i: (0, 0))
    block = pl.BlockSpec((tile, D), lambda i: (i, 0))
    return launch(
        functools.partial(middle_kernel, len(parts), n_sp, depth),
        [*parts, out_w, x, gain, shift],
        [pl.BlockSpec((n_sp, tile, group), lambda i: (0, i, 0))] * len(parts)
        + [pl.BlockSpec((D, D), lambda i: (0, 0)), block, row, row],
        [shape_of((rows, D), f32)] + [shape_of((rows, D), bf16)] * 3,
        [block] * 4,
        grid=(rows // tile,),
        deps=deps,
        cost=(2 * rows * D * D, 2 * D * D + rows * D * 12, rows),
        name="middle",
    )


def turn(values, cosine, sine_up, sine_down):
    width = values.shape[1]
    half = ROT // 2
    return (
        values * cosine
        + pltpu.roll(values, width - half, 1) * sine_up
        + pltpu.roll(values, half, 1) * sine_down
    )


def joint_kernel(width, table_ref, x_ref, w_ref, bias_ref, cos_ref, up_ref, down_ref, *outs):
    rows = x_ref.shape[0]
    tile = min(256, rows)
    for start in range(0, rows, tile):
        at = slice(start, start + tile)
        projected = dot(x_ref[at], w_ref[...], NN) + bias_ref[...]
        tables = (cos_ref[at], up_ref[at], down_ref[at])
        for g in range(len(outs) // 3):
            part = projected[:, 3 * g * width : 3 * (g + 1) * width]
            outs[3 * g][at] = turn(part[:, :width], *tables).astype(bf16)
            outs[3 * g + 1][at] = turn(part[:, width : 2 * width], *tables).astype(bf16)
            outs[3 * g + 2][at] = part[:, 2 * width :].astype(bf16)


def joint_projection(table, normed, weight, bias, tables, span, groups):
    length = normed.shape[0]
    total = weight.shape[1]
    width = total // 3 // groups
    placed = pl.BlockSpec((span, width), lambda b, t: (t[b], 0))
    return pl.pallas_call(
        functools.partial(joint_kernel, width),
        grid_spec=pltpu.PrefetchScalarGridSpec(
            num_scalar_prefetch=1,
            grid=(length // span,),
            in_specs=[
                pl.BlockSpec((span, D), lambda b, t: (b, 0)),
                pl.BlockSpec((D, total), lambda b, t: (0, 0)),
                pl.BlockSpec((1, total), lambda b, t: (0, 0)),
                placed,
                placed,
                placed,
            ],
            out_specs=[placed] * (3 * groups),
        ),
        out_shape=[jax.ShapeDtypeStruct((length, width), bf16)] * (3 * groups),
        compiler_params=params(),
        cost_estimate=pl.CostEstimate(
            flops=2 * length * D * total, bytes_accessed=length * (D + total) * 2, transcendentals=0
        ),
        name="joint_projection",
    )(table, normed, weight, bias, *tables)


def attend_kernel(heads, bq, bk, q_ref, k_ref, v_ref, o_ref, lse_ref, qm, vt, acc, m_s, l_s):
    i = pl.program_id(0)
    length, width = k_ref.shape
    lane = lax.broadcasted_iota(jnp.int32, (1, width), 1) // HEAD

    @pl.when(i == 0)
    def _():
        def flip(b, carry):
            rows = pl.ds(pl.multiple_of(b * bk, bk), bk)
            vt[:, rows] = jnp.transpose(v_ref[rows, :])
            return carry

        lax.fori_loop(0, length // bk, flip, 0)

    q = q_ref[...]
    for h in range(heads):
        qm[h] = jnp.where(lane == h, q, jnp.zeros_like(q))
    acc[...] = jnp.zeros_like(acc)
    m_s[...] = jnp.full_like(m_s, masked_value)
    l_s[...] = jnp.zeros_like(l_s)

    def body(j, masked):
        rows = pl.ds(pl.multiple_of(j * bk, bk), bk)
        k = k_ref[rows, :]
        scores = [dot(k, qm[h], NT) for h in range(heads)]
        if masked:
            key_at = lax.broadcasted_iota(jnp.int32, scores[0].shape, 0) + j * bk
            query_at = lax.broadcasted_iota(jnp.int32, scores[0].shape, 1) + i * bq
            scores = [jnp.where(key_at <= query_at, s, masked_value) for s in scores]
        m0 = m_s[...]
        l0 = l_s[...]
        m1 = jnp.maximum(m0, jnp.concatenate([jnp.max(s, axis=0, keepdims=True) for s in scores] + [m0[heads:]], 0))
        m_s[...] = m1
        kept = jnp.exp2((m0 - m1) * LOG2E_SCALE)
        base = m1 * LOG2E_SCALE
        raised = [jnp.exp2(scores[h] * LOG2E_SCALE - base[h : h + 1]) for h in range(heads)]
        l_s[...] = l0 * kept + jnp.concatenate([jnp.sum(p, axis=0, keepdims=True) for p in raised] + [l0[heads:]], 0)
        for h in range(heads):
            part = slice(h * HEAD, (h + 1) * HEAD)
            acc[part, :] = acc[part, :] * kept[h : h + 1] + dot(vt[part, rows], raised[h].astype(bf16), NN)

    whole = (i * bq) // bk
    lax.fori_loop(0, whole, lambda j, c: (body(j, False), c)[1], 0)
    for d in range(max(1, bq // bk)):
        body(whole + d, True)
    for h in range(heads):
        part = slice(h * HEAD, (h + 1) * HEAD)
        acc[part, :] = acc[part, :] * (1.0 / l_s[h : h + 1])
    o_ref[...] = jnp.transpose(acc[...].astype(bf16))
    lse_ref[...] = m_s[...] * LOG2E_SCALE + jnp.log2(l_s[...])


def attend(q, k, v, deps=()):
    length, width = q.shape
    heads = width // HEAD
    bq, bk = min(1024, length), min(512, length)
    full = pl.BlockSpec((length, width), lambda i: (0, 0))
    return launch(
        functools.partial(attend_kernel, heads, bq, bk),
        [q, k, v],
        [pl.BlockSpec((bq, width), lambda i: (i, 0)), full, full],
        [shape_of((length, width), bf16), shape_of((8, length), f32)],
        [pl.BlockSpec((bq, width), lambda i: (i, 0)), pl.BlockSpec((8, bq), lambda i: (0, i))],
        grid=(length // bq,),
        scratch=[
            pltpu.VMEM((heads, bq, width), bf16),
            pltpu.VMEM((width, length), bf16),
            pltpu.VMEM((width, bq), f32),
            pltpu.VMEM((8, bq), f32),
            pltpu.VMEM((8, bq), f32),
        ],
        deps=deps,
        cost=(8 * length * length * width, length * width * 8, length * length * heads // 2),
        name="attend",
    )


def attend_back_kernel(
    heads, bq, bk, place_ref, q_ref, k_ref, v_ref, do_ref, o_ref, lse_ref, cos_ref, up_ref, down_ref, out_ref,
    dq_acc, dk_acc, dv_acc, delta,
):
    j = pl.program_id(0)
    length, width = q_ref.shape
    lane = lax.broadcasted_iota(jnp.int32, (1, width), 1) // HEAD

    @pl.when(j == 0)
    def _():
        dq_acc[...] = jnp.zeros_like(dq_acc)
        pick = (
            lax.broadcasted_iota(jnp.int32, (8, width), 0) == lax.broadcasted_iota(jnp.int32, (8, width), 1) // HEAD
        ).astype(f32)

        def sums(b, carry):
            rows = pl.ds(pl.multiple_of(b * bq, bq), bq)
            both = do_ref[rows, :].astype(f32) * o_ref[rows, :].astype(f32)
            delta[:, rows] = lax.dot_general(
                pick, both, NT, precision=lax.Precision.HIGHEST, preferred_element_type=f32
            )
            return carry

        lax.fori_loop(0, length // bq, sums, 0)

    key_rows = pl.ds(pl.multiple_of(j * bk, bk), bk)
    k = k_ref[key_rows, :]
    v = v_ref[key_rows, :]
    kt = jnp.transpose(k)
    dk_acc[...] = jnp.zeros_like(dk_acc)
    dv_acc[...] = jnp.zeros_like(dv_acc)

    def body(i, masked):
        rows = pl.ds(pl.multiple_of(i * bq, bq), bq)
        q = q_ref[rows, :]
        do = do_ref[rows, :]
        probs, grads, queries, results = [], [], [], []
        for h in range(heads):
            qh = jnp.where(lane == h, q, jnp.zeros_like(q))
            doh = jnp.where(lane == h, do, jnp.zeros_like(do))
            s = dot(k, qh, NT)
            p = jnp.exp2(s * LOG2E_SCALE - lse_ref[h : h + 1, rows])
            if masked:
                key_at = lax.broadcasted_iota(jnp.int32, s.shape, 0) + j * bk
                query_at = lax.broadcasted_iota(jnp.int32, s.shape, 1) + i * bq
                p = jnp.where(key_at <= query_at, p, 0.0)
            dp = dot(v, doh, NT)
            ds = p * (dp - delta[h : h + 1, rows])
            probs.append(p.astype(bf16))
            grads.append(ds.astype(bf16))
            queries.append(qh)
            results.append(doh)
        dv_acc[...] += dot(jnp.concatenate(probs, 1), jnp.concatenate(results, 0), NN)
        dk_acc[...] += dot(jnp.concatenate(grads, 1), jnp.concatenate(queries, 0), NN)
        for h in range(heads):
            part = slice(h * HEAD, (h + 1) * HEAD)
            dq_acc[part, rows] += dot(kt[part], grads[h], NN)

    first = (j * bk) // bq
    near = max(1, bk // bq)
    for d in range(near):
        body(first + d, True)
    lax.fori_loop(first + near, length // bq, lambda i, c: (body(i, False), c)[1], 0)
    scale = HEAD**-0.5
    tables = (cos_ref[...], -up_ref[...], -down_ref[...])
    dq = (jnp.transpose(dq_acc[:, key_rows]) * scale).astype(bf16).astype(f32)
    dk = (dk_acc[...] * scale).astype(bf16).astype(f32)
    out_ref[:, :width] = turn(dq, *tables).astype(bf16)
    out_ref[:, width : 2 * width] = turn(dk, *tables).astype(bf16)
    out_ref[:, 2 * width :] = dv_acc[...].astype(bf16)


def attend_back(place, q, k, v, do, o, lse, tables, span, deps=()):
    length, width = q.shape
    heads = width // HEAD
    bq = min(512, length)
    bk = span
    full = pl.BlockSpec((length, width), lambda i, t: (0, 0))
    block = pl.BlockSpec((bk, width), lambda i, t: (i, 0))
    return launch(
        functools.partial(attend_back_kernel, heads, bq, bk),
        [place, q, k, v, do, o, lse, *tables],
        [full] * 5 + [pl.BlockSpec((8, length), lambda i, t: (0, 0))] + [block] * 3,
        [shape_of((length, 3 * width), bf16)],
        [pl.BlockSpec((bk, 3 * width), lambda i, t: (t[i], 0))],
        grid=(length // bk,),
        prefetch=1,
        scratch=[
            pltpu.VMEM((width, length), f32),
            pltpu.VMEM((bk, width), f32),
            pltpu.VMEM((bk, width), f32),
            pltpu.VMEM((8, length), f32),
        ],
        deps=deps,
        cost=(12 * length * length * width, length * width * 16, length * length * heads // 2),
        name="attend_back",
    )[0]


def feed_kernel(ff, x0, x1, c0, c1, wgu_ref, wd_ref, *rest):
    hidden_ref, grad_ref, x_ref, c_ref = rest[-4:]
    which = pl.program_id(0)

    @pl.when(which == 0)
    def _():
        x_ref[...] = x0[...]
        c_ref[...] = c0[...]

    @pl.when(which == 1)
    def _():
        x_ref[...] = x1[...]
        c_ref[...] = c1[...]

    both = dot(x_ref[...], wgu_ref[...], NN)
    hidden_grad = dot(c_ref[...], wd_ref[...], NT)
    gate = both[:, :ff]
    up = both[:, ff:]
    open_ = jax.nn.sigmoid(gate)
    swished = gate * open_
    hidden_ref[...] = (swished * up).astype(bf16)
    grad_ref[:, :ff] = (hidden_grad * up * open_ * (1.0 + gate * (1.0 - open_))).astype(bf16)
    grad_ref[:, ff:] = (hidden_grad * swished).astype(bf16)


def feed_block(pair, cot_pair, gate_up, down, at, half, buffers, deps=()):
    rows = pair[0].shape[0]
    ff = down.shape[0]
    tile = min(256, rows)
    steps = rows // tile
    length = 2 * half * rows
    early = pl.BlockSpec((tile, D), lambda p, i: (jnp.where(p == 0, i, steps - 1), 0))
    late = pl.BlockSpec((tile, D), lambda p, i: (jnp.where(p == 0, 0, i), 0))
    operands = [pair[0], pair[1], cot_pair[0], cot_pair[1], gate_up, down]
    specs = [
        early,
        late,
        early,
        late,
        pl.BlockSpec((D, 2 * ff), lambda p, i: (0, 0)),
        pl.BlockSpec((ff, D), lambda p, i: (0, 0)),
    ]
    aliases = {}
    if buffers is not None:
        aliases = {len(operands) + n: n for n in range(4)}
        operands += list(buffers)
        specs += [pl.BlockSpec(memory_space=pl.ANY)] * 4

    def place(p, i):
        return ((p * half + at) * steps + i, 0)

    return launch(
        functools.partial(feed_kernel, ff),
        operands,
        specs,
        [
            shape_of((length, ff), bf16),
            shape_of((length, 2 * ff), bf16),
            shape_of((length, D), bf16),
            shape_of((length, D), bf16),
        ],
        [
            pl.BlockSpec((tile, ff), place),
            pl.BlockSpec((tile, 2 * ff), place),
            pl.BlockSpec((tile, D), place),
            pl.BlockSpec((tile, D), place),
        ],
        grid=(2, steps),
        aliases=aliases,
        deps=deps,
        cost=(12 * rows * D * ff, 6 * D * ff + rows * D * 16, 2 * rows * ff),
        name="feed_forward",
    )


def rotary_columns(length, width):
    half = ROT // 2
    indices = np.arange(half, dtype=np.float32)
    inverse = np.float32(1.0) / np.float32(10000.0) ** (indices * np.float32(2.0 / ROT))
    angles = np.arange(length, dtype=np.float32)[:, None] * inverse[None, :].astype(np.float32)
    cosine, sine = np.cos(angles.astype(np.float64)), np.sin(angles.astype(np.float64))
    rest = np.zeros((length, HEAD - ROT))
    none = np.zeros((length, half))
    one_head = (
        np.concatenate([cosine, cosine, rest + 1.0], -1),
        np.concatenate([-sine, none, rest], -1),
        np.concatenate([none, sine, rest], -1),
    )
    return tuple(jnp.asarray(np.tile(t, (1, width // HEAD)).astype(np.float32)) for t in one_head)


def swap_sp(value):
    return lax.all_to_all(value, "sp", split_axis=0, concat_axis=0, tiled=True)


def in_line(blocks, mine):
    count, rows = len(blocks), blocks[0].shape[0]
    total = jnp.zeros((count * rows, blocks[0].shape[1]), blocks[0].dtype)
    for step, block in enumerate(blocks):
        total = lax.dynamic_update_slice(total, block, (lax.rem(mine - step + count, count) * rows, 0))
    return total


def per_device(
    tokens, cotangent, first_gain, first_shift, joint_weight, joint_bias, out_weight, second_gain, second_shift,
    gate_weight, up_weight, down_weight,
):
    n_sp = lax.axis_size("sp")
    n_z = lax.axis_size("fsdp")
    n_all = n_sp * n_z
    plane = Plane(n_sp)
    half = plane.half
    me = lax.axis_index("sp")
    span = tokens.shape[1]
    length = n_sp * span
    width = D // n_sp
    depth = joint_weight.shape[0]
    ff_rows = down_weight.shape[0]
    unit = max(16, 128 // n_z)
    ff_pad = -(-ff_rows // unit) * unit
    ff = n_z * ff_pad

    order = jnp.asarray(plane.table)[me]
    place = jnp.asarray(np.argsort(plane.table, axis=1).astype(np.int32))[me]
    groups = 2 if width % 256 == 0 else 1
    group = width // groups
    my_z = lax.axis_index("fsdp")

    small = jnp.concatenate([first_gain, first_shift, second_gain, second_shift, joint_bias])
    small = jnp.broadcast_to(small[None], (n_all, small.shape[0]))
    small_all = lax.all_to_all(small, ("fsdp", "sp"), split_axis=0, concat_axis=0, tiled=True)
    small = small_all.astype(f32)
    n_gain = first_gain.shape[0]
    gain_one, shift_one, gain_two, shift_two = (
        small[:, i * n_gain : (i + 1) * n_gain].reshape(1, D) for i in range(4)
    )
    bias_all = small[:, 4 * n_gain :].reshape(3, n_sp, width)
    bias = lax.dynamic_index_in_dim(bias_all, me, axis=1, keepdims=False)
    bias = bias.reshape(3, groups, group).transpose(1, 0, 2).reshape(1, 3 * width)

    ring = [(i, (i + 1) % n_z) for i in range(n_z)]
    joint_block = swap_sp(cut_joint(joint_weight, n_sp, groups)).reshape(n_sp * depth, 3 * width)
    out_blocks = [out_weight]
    for _ in range(n_z - 1):
        out_blocks.append(lax.ppermute(out_blocks[-1], "fsdp", ring))
    out_rows = in_line(out_blocks, my_z)
    joint_blocks = [held(joint_block, out_blocks[1:])]
    for _ in range(n_z - 1):
        joint_blocks.append(lax.ppermute(joint_blocks[-1], "fsdp", ring))
    joint_mine = in_line(joint_blocks, my_z)

    gate_up_cols, cot = cut_feed(gate_weight, up_weight, cotangent.reshape(span, D), n_sp, n_z, ff_pad)
    down_rows = jnp.pad(down_weight, ((0, ff_pad - ff_rows), (0, 0)))
    x = tokens.reshape(span, D)
    normed = None

    def norm_next(normed, block, t, deps=()):
        return norm_block(block, gain_one, shift_one, t, n_sp, normed, deps)

    partner, one, twos = plane.gather_first(x)
    normed = norm_next(None, x, 0)
    normed = norm_next(normed, partner, half)
    one = held(one, (normed, joint_blocks[1:3], gate_up_cols, cot))
    one_other, two_others, threes = plane.gather_second(one, twos)
    normed = norm_next(normed, one, 1)
    for n, two in enumerate(twos):
        normed = norm_next(normed, two, 2 + 2 * n)
    normed = norm_next(normed, one_other, half + 1)
    for n, two in enumerate(two_others):
        normed = norm_next(normed, two, half + 2 + 2 * n)
    threes = [held(three, (normed, joint_mine, bias)) if n == 0 else three for n, three in enumerate(threes)]
    for n, three in enumerate(threes):
        normed = norm_next(normed, three, 3 + 2 * n)
    for n, three in enumerate(plane.gather_third(threes)):
        normed = norm_next(normed, three, half + 3 + 2 * n)
    tables = rotary_columns(length, group)
    heads = joint_projection(order, normed, joint_mine, bias, tables, span, groups)

    out_full = lax.all_gather(held(out_rows, threes), "sp", axis=0, tiled=True)
    down = lax.all_gather(held(down_rows, threes), "fsdp", axis=0, tiled=True)
    gate_up_blocks = [held(swap_sp(held(gate_up_cols, threes)).reshape(n_sp * depth, 2 * ff), heads[0])]
    gate_up_blocks.append(lax.ppermute(gate_up_blocks[0], "fsdp", ring))
    cot = held(cot, gate_up_blocks[0])
    cot_partner, cot_one, cot_twos = plane.gather_first(cot)
    results = [attend(*heads[:3])]
    cot_one = held(cot_one, results[0][1])
    gate_up_blocks[1] = held(gate_up_blocks[1], results[0][1])
    gate_up_blocks.append(lax.ppermute(gate_up_blocks[1], "fsdp", ring))
    cot_one_other, cot_two_others, cot_threes = plane.gather_second(cot_one, cot_twos)
    for g in range(1, groups):
        results.append(attend(*heads[3 * g : 3 * g + 3], (cot_partner, cot_one, cot_twos, gate_up_blocks[1])))
    gate_up_blocks[2] = held(gate_up_blocks[2], results[-1][1])
    for _ in range(3, n_z):
        gate_up_blocks.append(lax.ppermute(gate_up_blocks[-1], "fsdp", ring))
    cot_three_others = plane.gather_third(cot_threes)
    cot_blocks, cot_partners = [cot, cot_one], [cot_partner, cot_one_other]
    for pieces in zip(cot_twos, cot_threes):
        cot_blocks += pieces
    for pieces in zip(cot_two_others, cot_three_others):
        cot_partners += pieces
    gate_up = in_line(gate_up_blocks, my_z)
    results[-1] = (held(results[-1][0], cot_threes), results[-1][1])
    attended = [swap_sp(o).reshape(n_sp, span, group) for o, _ in results]
    middle, normed_two, normed_again, attended_all = middle_of(
        attended, out_full, depth, x, gain_two, shift_two, (gate_up, down)
    )

    feed = None

    def feed_next(feed, pair, t, deps=()):
        return feed_block(pair, (cot_blocks[t], cot_partners[t]), gate_up, down, t, half, feed, deps)

    partner = plane.send(normed_two, plane.core)
    one = plane.send(normed_two, plane.first)
    feed = feed_next(None, (normed_two, partner), 0)
    one = held(one, feed[0])
    one_other = plane.send(one, plane.core)
    again = held(normed_again, one)
    for n, perm in enumerate(plane.later):
        two = plane.send(again, perm)
        if n == 0:
            feed = feed_next(feed, (one, one_other), 1, again)
        two = held(two, feed[0])
        one = held(one, (two, one_other))
        three = plane.send(one, perm)
        feed = feed_next(feed, (two, plane.send(two, plane.core)), 2 + 2 * n)
        three = held(three, feed[0])
        feed = feed_next(feed, (three, plane.send(three, plane.core)), 3 + 2 * n)
    hidden, gate_up_grad, two_all, cot_all = feed

    two_product = product_of([gate_up_grad], gate_up, NT, span)
    out_product = product_of([hidden], down, NN, span)
    two_far, two_theirs = plane.reduce_sums(two_product, (), True)
    further, nearer = plane.legs(two_far)
    down_sum = dot(hidden, held(cot_all, two_far), TN).astype(bf16)
    two_one, two_last = plane.legs_next(two_product, further, two_theirs, down_sum)
    gate_up_sum = dot(held(two_all, two_one), gate_up_grad, TN).astype(bf16)
    down_part = lax.psum_scatter(held(down_sum, two_one), "fsdp", scatter_dimension=0, tiled=True)
    two_grad = plane.legs_own(two_product, nearer, two_theirs, two_last, gate_up_sum)
    gate_up_part = lax.psum_scatter(held(gate_up_sum, two_grad), "fsdp", scatter_dimension=0, tiled=True)
    middle_grad, two_sums, branch_grad, *parts = norm_back(
        two_grad, middle, gain_two, cot, out_full, depth, n_sp, groups
    )
    dos = [swap_sp(part).reshape(n_sp * span, group) for part in parts]
    out_sum = dot(attended_all, branch_grad, TN).astype(bf16).reshape(n_sp, n_z * depth, D)

    out_sums, out_theirs = plane.reduce_sums(out_product, branch_grad)
    out_got = plane.reduce_leg(out_sums)
    rows = attend_back(place, *heads[:3], dos[0], *results[0], tables, span, out_sums)
    joint_rows = [rows]
    joint_sums = [dot(normed, rows, TN).astype(bf16)]
    joint_parts = [lax.psum_scatter(joint_sums[0], "fsdp", scatter_dimension=0, tiled=True)]
    out_one, out_last = plane.reduce_next(out_product, out_got, out_theirs)
    out_weight_part = parts_of(out_sum, order)
    weight_sums, weight_theirs = plane.reduce_sums(out_weight_part)
    weight_got = plane.reduce_leg(weight_sums)
    gate_up_own = swap_sp(gate_up_part)
    for g in range(1, groups):
        deps = (joint_sums, out_one, weight_sums, weight_theirs)
        rows = attend_back(place, *heads[3 * g : 3 * g + 3], dos[g], *results[g], tables, span, deps)
        joint_rows.append(rows)
    _, weight_last = plane.reduce_next(out_weight_part, weight_got, weight_theirs)

    normed_product = product_of(joint_rows, joint_mine, NT, span)
    normed_far, normed_theirs = plane.reduce_sums(normed_product, (out_last, weight_got, joint_parts, down_part, gate_up_own), True)
    further, nearer = plane.legs(normed_far)
    last_normed = held(normed, (normed_far, joint_sums))
    for g in range(1, groups):
        joint_sums.append(dot(last_normed, joint_rows[g], TN).astype(bf16))
        joint_parts.append(lax.psum_scatter(joint_sums[g], "fsdp", scatter_dimension=0, tiled=True))
    normed_one, normed_last = plane.legs_next(
        normed_product, further, normed_theirs, joint_sums
    )
    output = (middle + plane.reduce_own(out_product, out_got, out_theirs, out_last, f32)).astype(bf16)
    out_own = plane.reduce_own(out_weight_part, weight_got, weight_theirs, weight_last)
    out_grad = lax.psum_scatter(held(out_own, joint_parts), "fsdp", scatter_dimension=0, tiled=True).astype(f32)
    down_grad = down_part[:ff_rows].astype(f32)
    gate_grad, up_grad = join_feed(gate_up_own.reshape(n_sp, depth, 2 * ff), n_z, ff_rows, ff_pad)
    bias_sum = jnp.stack([jnp.sum(r.astype(f32), axis=0).reshape(3, group) for r in joint_rows], 1)
    bias_sum = bias_sum.reshape(3, 1, width)
    bias_sum = lax.dynamic_update_slice(jnp.zeros((3, n_sp, width), f32), bias_sum, (0, me, 0))
    joint_own = jnp.concatenate(joint_parts, axis=1)
    joint_own = swap_sp(joint_own).reshape(n_sp, depth, 3 * width)
    fill = (output, out_own, gate_grad, up_grad, bias_sum)
    normed_grad = plane.legs_own(normed_product, nearer, normed_theirs, normed_last, fill)
    joint_grad = join_joint(held(joint_own, normed_grad), groups)
    tokens_grad, one_sums = norm_back(normed_grad, x, gain_one, middle_grad, deps=joint_grad)
    tokens_grad = tokens_grad.reshape(tokens.shape)

    sums = [one_sums[0], one_sums[1], two_sums[0], two_sums[1]]
    sums = jnp.concatenate([s.reshape(n_all, n_gain) for s in sums] + [bias_sum.reshape(n_all, -1)], axis=1)
    sums = jnp.sum(lax.all_to_all(sums, ("fsdp", "sp"), split_axis=0, concat_axis=0, tiled=True), axis=0)
    gain_one_grad, shift_one_grad, gain_two_grad, shift_two_grad = (
        sums[i * n_gain : (i + 1) * n_gain] for i in range(4)
    )
    return (
        output.reshape(tokens.shape),
        tokens_grad,
        gain_one_grad,
        shift_one_grad,
        joint_grad,
        sums[4 * n_gain :],
        out_grad,
        gain_two_grad,
        shift_two_grad,
        gate_grad,
        up_grad,
        down_grad,
    )


def solution(mesh):
    rows = P("fsdp", "sp", None)
    vector = P(("fsdp", "sp"))
    matrix = P(("fsdp", "sp"), None)
    return jax.shard_map(
        per_device,
        mesh=mesh,
        in_specs=(rows, rows, vector, vector, matrix, vector, matrix, vector, vector, matrix, matrix, matrix),
        out_specs=(rows, rows, vector, vector, matrix, vector, matrix, vector, vector, matrix, matrix, matrix),
        check_vma=False,
    )
```

```python
import functools
import math

import jax
import jax.numpy as jnp
import numpy as np
from jax import lax
from jax.experimental import pallas as pl
from jax.experimental.pallas import tpu as pltpu
from jax.sharding import PartitionSpec as P

D = 2048
HEADS = 32
HEAD = 64
ROT = 16

epsilon = 1e-05
masked_value = -1e30
f32 = jnp.float32
bf16 = jnp.bfloat16
LOG2E_SCALE = math.log2(math.e) * HEAD**-0.5
NN = (((1,), (0,)), ((), ()))
NT = (((1,), (1,)), ((), ()))
TN = (((0,), (0,)), ((), ()))


def dot(a, b, dims):
    return lax.dot_general(a, b, dims, preferred_element_type=f32)


def params(mib=56):
    return pltpu.CompilerParams(vmem_limit_bytes=mib * 2**20)


class Plane:
    def __init__(self, count):
        outer = count // 4
        self.count = count
        self.outer = outer

        def spot(o, i, c):
            return ((o % outer) * 2 + i) * 2 + c

        def split(s):
            return s // 4, (s // 2) % 2, s % 2

        self.core = [(s, s ^ 1) for s in range(count)]
        first = []
        later = [[] for _ in range(outer - 1)]
        for s in range(count):
            o, i, c = split(s)
            swapped = outer == 2 and c == 1
            first.append((s, spot(o + 1, i, c) if swapped else spot(o, 1 - i, c)))
            for k in range(1, outer):
                later[k - 1].append((s, spot(o, 1 - i, c) if swapped else spot(o + k, i, c)))
        self.first = first
        self.later = later
        here = list(range(count))

        def moved(table, perm):
            out = [None] * count
            for a, b in perm:
                out[b] = table[a]
            return out

        blocks = [here, moved(here, first)]
        for perm in later:
            blocks += [moved(blocks[0], perm), moved(blocks[1], perm)]
        blocks += [moved(b, self.core) for b in blocks]
        self.table = np.array(blocks, np.int32).T
        self.half = 2 * outer
        self.far = list(reversed(range(2, self.half, 2)))

    @staticmethod
    def send(value, perm):
        return lax.ppermute(value, "sp", perm)

    @staticmethod
    def back(value, perm):
        return lax.ppermute(value, "sp", [(b, a) for a, b in perm])

    def gather_first(self, value):
        return (
            self.send(value, self.core),
            self.send(value, self.first),
            [self.send(value, perm) for perm in self.later],
        )

    def gather_second(self, one, twos):
        return (
            self.send(one, self.core),
            [self.send(two, self.core) for two in twos],
            [self.send(one, perm) for perm in self.later],
        )

    def gather_third(self, threes):
        return [self.send(three, self.core) for three in threes]


    def reduce_sums(self, product, deps=(), apart=False):
        far = [product(self.half + start, self.half + start + 2, (), bf16, deps) for start in self.far]
        near = product(self.half, self.half + 2, (), bf16, far)
        theirs = [self.send(value, self.core) for value in far]
        more = (True,) if apart else ()
        sums = [product(start, start + 2, ((value, 0),), bf16, near, *more) for start, value in zip(self.far, theirs)]
        return sums, self.send(near, self.core)

    def reduce_leg(self, sums):
        return [self.back(value, self.later[start // 2 - 1]) for start, value in zip(self.far, sums)]

    def reduce_next(self, product, got, theirs, deps=()):
        one = product(1, 2, tuple((t, 1) for t in [theirs] + got), bf16, deps)
        return one, self.back(one, self.first)

    def reduce_own(self, product, got, theirs, last, dtype=bf16, deps=()):
        return product(0, 1, tuple((t, 0) for t in [theirs] + got + [last]), dtype, deps)[0]


    def legs(self, sums):
        perms = [self.later[start // 2 - 1] for start in self.far]
        further = [self.back(pair[1], perm) for pair, perm in zip(sums, perms)]
        nearer = [self.back(held(pair[0], further), perm) for pair, perm in zip(sums, perms)]
        return further, nearer

    def legs_next(self, product, further, theirs, deps=()):
        one = product(1, 2, ((theirs, 1), *((t, 0) for t in further)), bf16, deps)
        return one, self.back(one, self.first)

    def legs_own(self, product, nearer, theirs, last, deps=()):
        return product(0, 1, ((theirs, 0), *((t, 0) for t in [*nearer, last])), bf16, deps)[0]


def launch(
    kernel, operands, in_specs, outs, out_specs, *, grid, name, cost, scratch=(), deps=(), aliases=None, prefetch=0, mib=60
):
    deps = jax.tree.leaves(deps)
    count = len(operands)

    def body(*refs):
        kernel(*refs[:count], *refs[count + len(deps) :])

    flops, moved, transcendentals = cost
    return pl.pallas_call(
        body,
        grid_spec=pltpu.PrefetchScalarGridSpec(
            num_scalar_prefetch=prefetch,
            grid=grid,
            in_specs=list(in_specs) + [pl.BlockSpec(memory_space=pl.ANY)] * len(deps),
            out_specs=list(out_specs),
            scratch_shapes=list(scratch),
        ),
        out_shape=list(outs),
        input_output_aliases=aliases or {},
        compiler_params=pltpu.CompilerParams(vmem_limit_bytes=mib * 2**20),
        cost_estimate=pl.CostEstimate(flops=int(flops), bytes_accessed=int(moved), transcendentals=int(transcendentals)),
        name=name,
    )(*operands, *deps)


ANYWHERE = pl.BlockSpec(memory_space=pl.ANY)


def held(value, deps):
    return launch(
        lambda *refs: None, [value], [ANYWHERE], [shape_of(value.shape, value.dtype)], [ANYWHERE],
        grid=(1,), aliases={0: 0}, deps=deps, cost=(0, 0, 0), name="held",
    )[0]


def whole(shape):
    return pl.BlockSpec(shape, lambda *_: (0,) * len(shape))


def shape_of(shape, dtype):
    return jax.ShapeDtypeStruct(shape, dtype)


def product_kernel(terms, dims, pieces, *refs):
    outs = refs[-pieces:]
    each, rows, width = outs[0].shape
    count = each * pieces
    total = dot(refs[0][...], refs[terms][...], dims)
    for t in range(1, terms):
        total += dot(refs[t][...], refs[terms + t][...], dims)
    for ref in refs[2 * terms : -pieces]:
        total += ref[...].astype(f32).reshape(count * rows, width)
    total = total.reshape(pieces, each, rows, width)
    for n, out_ref in enumerate(outs):
        out_ref[...] = total[n].astype(out_ref.dtype)


def product_of(lefts, right, dims, span):
    tile = 512
    depth = sum(left.shape[1] for left in lefts)

    def right_at(at, left):
        if dims is NT:
            return pl.BlockSpec((tile, left.shape[1]), lambda i: (i, at))
        return pl.BlockSpec((left.shape[1], tile), lambda i: (at, i))

    def product(start, stop, addends, dtype, deps=(), apart=False):
        count = stop - start
        pieces = count if apart else 1
        assert start % count == 0 and all(at % count == 0 for _, at in addends)

        def columns(at):
            return pl.BlockSpec((count, span, tile), lambda i: (at // count, 0, i))

        values = launch(
            functools.partial(product_kernel, len(lefts), dims, pieces),
            [*lefts, *[right] * len(lefts), *(value for value, _ in addends)],
            [pl.BlockSpec((count * span, a.shape[1]), lambda i: (start // count, 0)) for a in lefts]
            + [right_at(t, left) for t, left in enumerate(lefts)]
            + [columns(at) for _, at in addends],
            [shape_of((count // pieces, span, D), dtype)] * pieces,
            [pl.BlockSpec((count // pieces, span, tile), lambda i: (0, 0, i))] * pieces,
            grid=(D // tile,),
            deps=deps,
            mib=60,
            cost=(2 * count * span * D * depth, 2 * depth * (D + count * span) + 4 * count * span * D, 0),
            name="block_product",
        )
        return values if apart else values[0]

    return product


def part_kernel(table_ref, sum_ref, *refs):
    total = sum_ref[...].astype(f32)
    for ref in refs[:-1]:
        total += ref[...].astype(f32)
    refs[-1][...] = total.astype(refs[-1].dtype)


def parts_of(sums, order):
    rows = sums.shape[1]

    def part(start, stop, addends, dtype, deps=()):
        def block(at):
            return pl.BlockSpec((1, rows, D), lambda b, t: (at + b, 0, 0))

        return launch(
            part_kernel,
            [order, sums, *(value for value, _ in addends)],
            [pl.BlockSpec((1, rows, D), lambda b, t: (t[start + b], 0, 0))] + [block(at) for _, at in addends],
            [shape_of((stop - start, rows, D), dtype)],
            [block(0)],
            grid=(stop - start,),
            prefetch=1,
            deps=deps,
            cost=((stop - start) * rows * D, (stop - start) * rows * D * 4, 0),
            name="part",
        )[0]

    return part


def norm_kernel(x_ref, gain_ref, shift_ref, *rest):
    out_ref = rest[-1]
    values = x_ref[...].astype(f32)
    center = values - jnp.mean(values, axis=-1, keepdims=True)
    spread = jnp.mean(center * center, axis=-1, keepdims=True)
    out_ref[...] = (center * lax.rsqrt(spread + epsilon) * gain_ref[...] + shift_ref[...]).astype(bf16)


def norm_block(x, gain, shift, at, blocks, buffer, deps=()):
    rows = x.shape[0]
    tile = min(256, rows)
    steps = rows // tile
    row = pl.BlockSpec((1, D), lambda i: (0, 0))
    held = [] if buffer is None else [buffer]
    return launch(
        norm_kernel,
        [x, gain, shift, *held],
        [pl.BlockSpec((tile, D), lambda i: (i, 0)), row, row, *[ANYWHERE] * len(held)],
        [shape_of((blocks * rows, D), bf16)],
        [pl.BlockSpec((tile, D), lambda i: (at * steps + i, 0))],
        grid=(steps,),
        aliases={3: 0} if held else {},
        deps=deps,
        mib=60,
        cost=(rows * D * 12, rows * D * 4, rows),
        name="first_norm",
    )[0]


def cut_joint_kernel(n_sp, groups, group, in_ref, out_ref):
    for j in range(n_sp):
        for g in range(groups):
            for m in range(3):
                to = (g * 3 + m) * group
                start = m * D + (j * groups + g) * group
                out_ref[j, :, to : to + group] = in_ref[:, start : start + group]


def cut_joint(weight, n_sp, groups):
    depth = weight.shape[0]
    width = D // n_sp
    return launch(
        functools.partial(cut_joint_kernel, n_sp, groups, width // groups),
        [weight], [whole(weight.shape)], [shape_of((n_sp, depth, 3 * width), bf16)], [whole((n_sp, depth, 3 * width))],
        grid=(1,), cost=(0, weight.size * 4, 0), name="cut_joint",
    )[0]


def join_joint_kernel(n_sp, groups, group, in_ref, out_ref):
    for j in range(n_sp):
        for g in range(groups):
            for m in range(3):
                start = m * D + (j * groups + g) * group
                to = (g * 3 + m) * group
                out_ref[:, start : start + group] = in_ref[j, :, to : to + group].astype(f32)


def join_joint(value, groups):
    n_sp, depth, width = value.shape
    return launch(
        functools.partial(join_joint_kernel, n_sp, groups, width // 3 // groups),
        [value], [whole(value.shape)], [shape_of((depth, 3 * D), f32)], [whole((depth, 3 * D))],
        grid=(1,), cost=(0, depth * D * 18, 0), name="join_joint",
    )[0]


def cut_feed_kernel(n_sp, n_z, size, padded, gate_ref, up_ref, beside_ref, out_ref, copy_ref):
    copy_ref[...] = beside_ref[...]
    out_ref[...] = jnp.zeros_like(out_ref)
    for j in range(n_sp):
        for p, ref in enumerate((gate_ref, up_ref)):
            for z in range(n_z):
                start = (z * n_sp + j) * size
                to = (p * n_z + z) * padded
                out_ref[j, :, to : to + size] = ref[:, start : start + size]


def cut_feed(gate_weight, up_weight, beside, n_sp, n_z, padded):
    depth, total = gate_weight.shape
    size = total // (n_sp * n_z)
    shape = (n_sp, depth, 2 * n_z * padded)
    return launch(
        functools.partial(cut_feed_kernel, n_sp, n_z, size, padded),
        [gate_weight, up_weight, beside],
        [whole(gate_weight.shape)] * 2 + [whole(beside.shape)],
        [shape_of(shape, bf16), shape_of(beside.shape, beside.dtype)],
        [whole(shape), whole(beside.shape)],
        grid=(1,), cost=(0, gate_weight.size * 8, 0), name="cut_feed",
    )


def join_feed_kernel(n_sp, n_z, size, padded, in_ref, gate_ref, up_ref):
    for p, ref in enumerate((gate_ref, up_ref)):
        for z in range(n_z):
            for j in range(n_sp):
                start = (z * n_sp + j) * size
                to = (p * n_z + z) * padded
                ref[:, start : start + size] = in_ref[j, :, to : to + size].astype(f32)


def join_feed(value, n_z, size, padded):
    n_sp, depth, _ = value.shape
    shape = (depth, n_sp * n_z * size)
    return launch(
        functools.partial(join_feed_kernel, n_sp, n_z, size, padded),
        [value], [whole(value.shape)], [shape_of(shape, f32)] * 2, [whole(shape)] * 2,
        grid=(1,), cost=(0, value.size * 6, 0), name="join_feed",
    )


def norm_back_kernel(depth, n_parts, *refs):
    grad_ref, x_ref, gain_ref, beside_ref = refs[:4]
    weights = refs[4 : 4 + n_parts]
    outs = refs[4 + n_parts :]
    result_ref, sums_ref = outs[0], outs[1]
    values = x_ref[...].astype(f32)
    center = values - jnp.mean(values, axis=-1, keepdims=True)
    spread = jnp.mean(center * center, axis=-1, keepdims=True)
    inverse = lax.rsqrt(spread + epsilon)
    xhat = center * inverse
    grad = grad_ref[...].astype(f32)
    scaled = grad * gain_ref[...]
    level = jnp.mean(scaled, axis=-1, keepdims=True)
    along = jnp.mean(scaled * xhat, axis=-1, keepdims=True)
    result = beside_ref[...].astype(f32) + inverse * (scaled - level - xhat * along)
    result_ref[...] = result

    @pl.when(pl.program_id(0) == 0)
    def _():
        sums_ref[...] = jnp.zeros_like(sums_ref)

    sums_ref[0:1] += jnp.sum(grad * xhat, axis=0, keepdims=True)
    sums_ref[1:2] += jnp.sum(grad, axis=0, keepdims=True)
    if n_parts:
        branch = result.astype(bf16)
        outs[2][...] = branch
        parts = outs[3:]
        full = dot(branch, weights[0][...], NT).astype(bf16)
        for place, g, j, columns in head_pieces(parts[0].shape[0], depth, len(parts)):
            parts[g][j, :, columns] = full[:, place]


def norm_back(grad, x, gain, beside, weight=None, depth=0, n_sp=0, groups=0, deps=()):
    rows = x.shape[0]
    tile = min(256, rows)
    row = pl.BlockSpec((1, D), lambda i: (0, 0))
    block = pl.BlockSpec((tile, D), lambda i: (i, 0))
    outs = [shape_of((rows, D), f32), shape_of((8, D), f32)]
    out_specs = [block, whole((8, D))]
    extra, specs = [], []
    if weight is not None:
        group = D // n_sp // groups
        extra, specs = [weight], [whole((D, D))]
        outs += [shape_of((rows, D), bf16)] + [shape_of((n_sp, rows, group), bf16)] * groups
        out_specs += [block] + [pl.BlockSpec((n_sp, tile, group), lambda i: (0, i, 0))] * groups
    return launch(
        functools.partial(norm_back_kernel, depth, len(extra)),
        [grad, x, gain, beside, *extra],
        [block, block, row, block, *specs],
        outs,
        out_specs,
        grid=(rows // tile,),
        cost=(rows * D * (20 + 2 * D * len(extra)), rows * D * 16 + 2 * D * D * len(extra), rows),
        deps=deps,
        name="norm_back",
    )


def head_pieces(n_sp, depth, groups):
    group = D // n_sp // groups
    n_z = D // n_sp // depth
    for z in range(n_z):
        for s in range(n_sp):
            j, rest = divmod((z * n_sp + s) * depth, groups * group)
            g, column = divmod(rest, group)
            yield slice((s * n_z + z) * depth, (s * n_z + z + 1) * depth), g, j, slice(column, column + depth)


def middle_kernel(groups, n_sp, depth, *refs):
    parts, (out_w, x_ref, gain_ref, shift_ref) = refs[:groups], refs[groups : groups + 4]
    middle_ref, normed_ref, again_ref, attended_ref = refs[groups + 4 :]
    for to, g, j, columns in head_pieces(n_sp, depth, groups):
        attended_ref[:, to] = parts[g][j, :, columns]
    values = x_ref[...].astype(f32) + dot(attended_ref[...], out_w[...], NN)
    middle_ref[...] = values
    center = values - jnp.mean(values, axis=-1, keepdims=True)
    spread = jnp.mean(center * center, axis=-1, keepdims=True)
    normed = (center * lax.rsqrt(spread + epsilon) * gain_ref[...] + shift_ref[...]).astype(bf16)
    normed_ref[...] = normed
    again_ref[...] = normed


def middle_of(parts, out_w, depth, x, gain, shift, deps=()):
    n_sp, rows, group = parts[0].shape
    tile = min(256, rows)
    row = pl.BlockSpec((1, D), lambda i: (0, 0))
    block = pl.BlockSpec((tile, D), lambda i: (i, 0))
    return launch(
        functools.partial(middle_kernel, len(parts), n_sp, depth),
        [*parts, out_w, x, gain, shift],
        [pl.BlockSpec((n_sp, tile, group), lambda i: (0, i, 0))] * len(parts)
        + [pl.BlockSpec((D, D), lambda i: (0, 0)), block, row, row],
        [shape_of((rows, D), f32)] + [shape_of((rows, D), bf16)] * 3,
        [block] * 4,
        grid=(rows // tile,),
        deps=deps,
        cost=(2 * rows * D * D, 2 * D * D + rows * D * 12, rows),
        name="middle",
    )


def turn(values, cosine, sine_up, sine_down):
    width = values.shape[1]
    half = ROT // 2
    return (
        values * cosine
        + pltpu.roll(values, width - half, 1) * sine_up
        + pltpu.roll(values, half, 1) * sine_down
    )


def joint_kernel(width, table_ref, x_ref, w_ref, bias_ref, cos_ref, up_ref, down_ref, *outs):
    rows = x_ref.shape[0]
    tile = min(256, rows)
    for start in range(0, rows, tile):
        at = slice(start, start + tile)
        projected = dot(x_ref[at], w_ref[...], NN) + bias_ref[...]
        tables = (cos_ref[at], up_ref[at], down_ref[at])
        for g in range(len(outs) // 3):
            part = projected[:, 3 * g * width : 3 * (g + 1) * width]
            outs[3 * g][at] = turn(part[:, :width], *tables).astype(bf16)
            outs[3 * g + 1][at] = turn(part[:, width : 2 * width], *tables).astype(bf16)
            outs[3 * g + 2][at] = part[:, 2 * width :].astype(bf16)


def joint_projection(table, normed, weight, bias, tables, span, groups):
    length = normed.shape[0]
    total = weight.shape[1]
    width = total // 3 // groups
    placed = pl.BlockSpec((span, width), lambda b, t: (t[b], 0))
    return pl.pallas_call(
        functools.partial(joint_kernel, width),
        grid_spec=pltpu.PrefetchScalarGridSpec(
            num_scalar_prefetch=1,
            grid=(length // span,),
            in_specs=[
                pl.BlockSpec((span, D), lambda b, t: (b, 0)),
                pl.BlockSpec((D, total), lambda b, t: (0, 0)),
                pl.BlockSpec((1, total), lambda b, t: (0, 0)),
                placed,
                placed,
                placed,
            ],
            out_specs=[placed] * (3 * groups),
        ),
        out_shape=[jax.ShapeDtypeStruct((length, width), bf16)] * (3 * groups),
        compiler_params=params(),
        cost_estimate=pl.CostEstimate(
            flops=2 * length * D * total, bytes_accessed=length * (D + total) * 2, transcendentals=0
        ),
        name="joint_projection",
    )(table, normed, weight, bias, *tables)


def attend_kernel(heads, bq, bk, q_ref, k_ref, v_ref, o_ref, lse_ref, qm, vt, acc, m_s, l_s):
    i = pl.program_id(0)
    length, width = k_ref.shape
    lane = lax.broadcasted_iota(jnp.int32, (1, width), 1) // HEAD

    @pl.when(i == 0)
    def _():
        def flip(b, carry):
            rows = pl.ds(pl.multiple_of(b * bk, bk), bk)
            vt[:, rows] = jnp.transpose(v_ref[rows, :])
            return carry

        lax.fori_loop(0, length // bk, flip, 0)

    q = q_ref[...]
    for h in range(heads):
        qm[h] = jnp.where(lane == h, q, jnp.zeros_like(q))
    acc[...] = jnp.zeros_like(acc)
    m_s[...] = jnp.full_like(m_s, masked_value)
    l_s[...] = jnp.zeros_like(l_s)

    def body(j, masked, start=0):
        at = slice(start, bq)
        rows = pl.ds(pl.multiple_of(j * bk, bk), bk)
        k = k_ref[rows, :]
        scores = [dot(k, qm[h, at], NT) for h in range(heads)]
        if masked:
            key_at = lax.broadcasted_iota(jnp.int32, scores[0].shape, 0) + j * bk
            query_at = lax.broadcasted_iota(jnp.int32, scores[0].shape, 1) + (i * bq + start)
            scores = [jnp.where(key_at <= query_at, s, masked_value) for s in scores]
        m0 = m_s[:, at]
        l0 = l_s[:, at]
        m1 = jnp.maximum(m0, jnp.concatenate([jnp.max(s, axis=0, keepdims=True) for s in scores] + [m0[heads:]], 0))
        m_s[:, at] = m1
        kept = jnp.exp2((m0 - m1) * LOG2E_SCALE)
        base = m1 * LOG2E_SCALE
        raised = [jnp.exp2(scores[h] * LOG2E_SCALE - base[h : h + 1]) for h in range(heads)]
        l_s[:, at] = l0 * kept + jnp.concatenate([jnp.sum(p, axis=0, keepdims=True) for p in raised] + [l0[heads:]], 0)
        for h in range(heads):
            part = slice(h * HEAD, (h + 1) * HEAD)
            acc[part, at] = acc[part, at] * kept[h : h + 1] + dot(vt[part, rows], raised[h].astype(bf16), NN)

    whole = (i * bq) // bk
    lax.fori_loop(0, whole, lambda j, c: (body(j, False), c)[1], 0)
    for d in range(max(1, bq // bk)):
        body(whole + d, True, d * bk)
    for h in range(heads):
        part = slice(h * HEAD, (h + 1) * HEAD)
        acc[part, :] = acc[part, :] * (1.0 / l_s[h : h + 1])
    o_ref[...] = jnp.transpose(acc[...].astype(bf16))
    lse_ref[...] = m_s[...] * LOG2E_SCALE + jnp.log2(l_s[...])


def attend(q, k, v, deps=()):
    length, width = q.shape
    heads = width // HEAD
    bq, bk = min(1024, length), min(512, length)
    full = pl.BlockSpec((length, width), lambda i: (0, 0))
    return launch(
        functools.partial(attend_kernel, heads, bq, bk),
        [q, k, v],
        [pl.BlockSpec((bq, width), lambda i: (i, 0)), full, full],
        [shape_of((length, width), bf16), shape_of((8, length), f32)],
        [pl.BlockSpec((bq, width), lambda i: (i, 0)), pl.BlockSpec((8, bq), lambda i: (0, i))],
        grid=(length // bq,),
        scratch=[
            pltpu.VMEM((heads, bq, width), bf16),
            pltpu.VMEM((width, length), bf16),
            pltpu.VMEM((width, bq), f32),
            pltpu.VMEM((8, bq), f32),
            pltpu.VMEM((8, bq), f32),
        ],
        deps=deps,
        cost=(8 * length * length * width, length * width * 8, length * length * heads // 2),
        name="attend",
    )


def attend_back_kernel(
    heads, bq, bk, place_ref, q_ref, k_ref, v_ref, do_ref, o_ref, lse_ref, cos_ref, up_ref, down_ref, out_ref,
    dq_acc, dk_acc, dv_acc, delta,
):
    j = pl.program_id(0)
    length, width = q_ref.shape
    lane = lax.broadcasted_iota(jnp.int32, (1, width), 1) // HEAD

    @pl.when(j == 0)
    def _():
        dq_acc[...] = jnp.zeros_like(dq_acc)
        pick = (
            lax.broadcasted_iota(jnp.int32, (8, width), 0) == lax.broadcasted_iota(jnp.int32, (8, width), 1) // HEAD
        ).astype(f32)

        def sums(b, carry):
            rows = pl.ds(pl.multiple_of(b * bq, bq), bq)
            both = do_ref[rows, :].astype(f32) * o_ref[rows, :].astype(f32)
            delta[:, rows] = lax.dot_general(
                pick, both, NT, precision=lax.Precision.HIGHEST, preferred_element_type=f32
            )
            return carry

        lax.fori_loop(0, length // bq, sums, 0)

    key_rows = pl.ds(pl.multiple_of(j * bk, bk), bk)
    k = k_ref[key_rows, :]
    v = v_ref[key_rows, :]
    kt = jnp.transpose(k)
    dk_acc[...] = jnp.zeros_like(dk_acc)
    dv_acc[...] = jnp.zeros_like(dv_acc)

    def body(i, masked):
        rows = pl.ds(pl.multiple_of(i * bq, bq), bq)
        q = q_ref[rows, :]
        do = do_ref[rows, :]
        probs, grads, queries, results = [], [], [], []
        for h in range(heads):
            qh = jnp.where(lane == h, q, jnp.zeros_like(q))
            doh = jnp.where(lane == h, do, jnp.zeros_like(do))
            s = dot(k, qh, NT)
            p = jnp.exp2(s * LOG2E_SCALE - lse_ref[h : h + 1, rows])
            if masked:
                key_at = lax.broadcasted_iota(jnp.int32, s.shape, 0) + j * bk
                query_at = lax.broadcasted_iota(jnp.int32, s.shape, 1) + i * bq
                p = jnp.where(key_at <= query_at, p, 0.0)
            dp = dot(v, doh, NT)
            ds = p * (dp - delta[h : h + 1, rows])
            probs.append(p.astype(bf16))
            grads.append(ds.astype(bf16))
            queries.append(qh)
            results.append(doh)
        dv_acc[...] += dot(jnp.concatenate(probs, 1), jnp.concatenate(results, 0), NN)
        dk_acc[...] += dot(jnp.concatenate(grads, 1), jnp.concatenate(queries, 0), NN)
        for h in range(heads):
            part = slice(h * HEAD, (h + 1) * HEAD)
            dq_acc[part, rows] += dot(kt[part], grads[h], NN)

    first = (j * bk) // bq
    near = max(1, bk // bq)
    for d in range(near):
        body(first + d, True)
    lax.fori_loop(first + near, length // bq, lambda i, c: (body(i, False), c)[1], 0)
    scale = HEAD**-0.5
    tables = (cos_ref[...], -up_ref[...], -down_ref[...])
    dq = (jnp.transpose(dq_acc[:, key_rows]) * scale).astype(bf16).astype(f32)
    dk = (dk_acc[...] * scale).astype(bf16).astype(f32)
    out_ref[:, :width] = turn(dq, *tables).astype(bf16)
    out_ref[:, width : 2 * width] = turn(dk, *tables).astype(bf16)
    out_ref[:, 2 * width :] = dv_acc[...].astype(bf16)


def attend_back(place, q, k, v, do, o, lse, tables, span, deps=()):
    length, width = q.shape
    heads = width // HEAD
    bq = min(512, length)
    bk = span
    full = pl.BlockSpec((length, width), lambda i, t: (0, 0))
    block = pl.BlockSpec((bk, width), lambda i, t: (i, 0))
    return launch(
        functools.partial(attend_back_kernel, heads, bq, bk),
        [place, q, k, v, do, o, lse, *tables],
        [full] * 5 + [pl.BlockSpec((8, length), lambda i, t: (0, 0))] + [block] * 3,
        [shape_of((length, 3 * width), bf16)],
        [pl.BlockSpec((bk, 3 * width), lambda i, t: (t[i], 0))],
        grid=(length // bk,),
        prefetch=1,
        scratch=[
            pltpu.VMEM((width, length), f32),
            pltpu.VMEM((bk, width), f32),
            pltpu.VMEM((bk, width), f32),
            pltpu.VMEM((8, length), f32),
        ],
        deps=deps,
        cost=(12 * length * length * width, length * width * 16, length * length * heads // 2),
        name="attend_back",
    )[0]


def feed_kernel(ff, x0, x1, c0, c1, wgu_ref, wd_ref, *rest):
    hidden_ref, grad_ref, x_ref, c_ref = rest[-4:]
    which = pl.program_id(0)

    @pl.when(which == 0)
    def _():
        x_ref[...] = x0[...]
        c_ref[...] = c0[...]

    @pl.when(which == 1)
    def _():
        x_ref[...] = x1[...]
        c_ref[...] = c1[...]

    both = dot(x_ref[...], wgu_ref[...], NN)
    hidden_grad = dot(c_ref[...], wd_ref[...], NT)
    gate = both[:, :ff]
    up = both[:, ff:]
    open_ = jax.nn.sigmoid(gate)
    swished = gate * open_
    hidden_ref[...] = (swished * up).astype(bf16)
    grad_ref[:, :ff] = (hidden_grad * up * open_ * (1.0 + gate * (1.0 - open_))).astype(bf16)
    grad_ref[:, ff:] = (hidden_grad * swished).astype(bf16)


def feed_block(pair, cot_pair, gate_up, down, at, half, buffers, deps=()):
    rows = pair[0].shape[0]
    ff = down.shape[0]
    tile = min(256, rows)
    steps = rows // tile
    length = 2 * half * rows
    early = pl.BlockSpec((tile, D), lambda p, i: (jnp.where(p == 0, i, steps - 1), 0))
    late = pl.BlockSpec((tile, D), lambda p, i: (jnp.where(p == 0, 0, i), 0))
    operands = [pair[0], pair[1], cot_pair[0], cot_pair[1], gate_up, down]
    specs = [
        early,
        late,
        early,
        late,
        pl.BlockSpec((D, 2 * ff), lambda p, i: (0, 0)),
        pl.BlockSpec((ff, D), lambda p, i: (0, 0)),
    ]
    aliases = {}
    if buffers is not None:
        aliases = {len(operands) + n: n for n in range(4)}
        operands += list(buffers)
        specs += [pl.BlockSpec(memory_space=pl.ANY)] * 4

    def place(p, i):
        return ((p * half + at) * steps + i, 0)

    return launch(
        functools.partial(feed_kernel, ff),
        operands,
        specs,
        [
            shape_of((length, ff), bf16),
            shape_of((length, 2 * ff), bf16),
            shape_of((length, D), bf16),
            shape_of((length, D), bf16),
        ],
        [
            pl.BlockSpec((tile, ff), place),
            pl.BlockSpec((tile, 2 * ff), place),
            pl.BlockSpec((tile, D), place),
            pl.BlockSpec((tile, D), place),
        ],
        grid=(2, steps),
        aliases=aliases,
        deps=deps,
        cost=(12 * rows * D * ff, 6 * D * ff + rows * D * 16, 2 * rows * ff),
        name="feed_forward",
    )


def rotary_columns(length, width):
    half = ROT // 2
    indices = np.arange(half, dtype=np.float32)
    inverse = np.float32(1.0) / np.float32(10000.0) ** (indices * np.float32(2.0 / ROT))
    angles = np.arange(length, dtype=np.float32)[:, None] * inverse[None, :].astype(np.float32)
    cosine, sine = np.cos(angles.astype(np.float64)), np.sin(angles.astype(np.float64))
    rest = np.zeros((length, HEAD - ROT))
    none = np.zeros((length, half))
    one_head = (
        np.concatenate([cosine, cosine, rest + 1.0], -1),
        np.concatenate([-sine, none, rest], -1),
        np.concatenate([none, sine, rest], -1),
    )
    return tuple(jnp.asarray(np.tile(t, (1, width // HEAD)).astype(np.float32)) for t in one_head)


def swap_sp(value):
    return lax.all_to_all(value, "sp", split_axis=0, concat_axis=0, tiled=True)


def in_line(blocks, mine):
    count, rows = len(blocks), blocks[0].shape[0]
    total = jnp.zeros((count * rows, blocks[0].shape[1]), blocks[0].dtype)
    for step, block in enumerate(blocks):
        total = lax.dynamic_update_slice(total, block, (lax.rem(mine - step + count, count) * rows, 0))
    return total


def per_device(
    tokens, cotangent, first_gain, first_shift, joint_weight, joint_bias, out_weight, second_gain, second_shift,
    gate_weight, up_weight, down_weight,
):
    n_sp = lax.axis_size("sp")
    n_z = lax.axis_size("fsdp")
    n_all = n_sp * n_z
    plane = Plane(n_sp)
    half = plane.half
    me = lax.axis_index("sp")
    span = tokens.shape[1]
    length = n_sp * span
    width = D // n_sp
    depth = joint_weight.shape[0]
    ff_rows = down_weight.shape[0]
    unit = max(16, 128 // n_z)
    ff_pad = -(-ff_rows // unit) * unit
    ff = n_z * ff_pad

    order = jnp.asarray(plane.table)[me]
    place = jnp.asarray(np.argsort(plane.table, axis=1).astype(np.int32))[me]
    groups = 2 if width % 256 == 0 else 1
    group = width // groups
    my_z = lax.axis_index("fsdp")

    small = jnp.concatenate([first_gain, first_shift, second_gain, second_shift, joint_bias])
    small = jnp.broadcast_to(small[None], (n_all, small.shape[0]))
    small_all = lax.all_to_all(small, ("fsdp", "sp"), split_axis=0, concat_axis=0, tiled=True)
    small = small_all.astype(f32)
    n_gain = first_gain.shape[0]
    gain_one, shift_one, gain_two, shift_two = (
        small[:, i * n_gain : (i + 1) * n_gain].reshape(1, D) for i in range(4)
    )
    bias_all = small[:, 4 * n_gain :].reshape(3, n_sp, width)
    bias = lax.dynamic_index_in_dim(bias_all, me, axis=1, keepdims=False)
    bias = bias.reshape(3, groups, group).transpose(1, 0, 2).reshape(1, 3 * width)

    ring = [(i, (i + 1) % n_z) for i in range(n_z)]
    joint_block = swap_sp(cut_joint(joint_weight, n_sp, groups)).reshape(n_sp * depth, 3 * width)
    out_blocks = [out_weight]
    for _ in range(n_z - 1):
        out_blocks.append(lax.ppermute(out_blocks[-1], "fsdp", ring))
    out_rows = in_line(out_blocks, my_z)
    joint_blocks = [held(joint_block, out_blocks[1:])]
    for _ in range(n_z - 1):
        joint_blocks.append(lax.ppermute(joint_blocks[-1], "fsdp", ring))
    joint_mine = in_line(joint_blocks, my_z)

    gate_up_cols, cot = cut_feed(gate_weight, up_weight, cotangent.reshape(span, D), n_sp, n_z, ff_pad)
    down_rows = jnp.pad(down_weight, ((0, ff_pad - ff_rows), (0, 0)))
    x = tokens.reshape(span, D)
    normed = None

    def norm_next(normed, block, t, deps=()):
        return norm_block(block, gain_one, shift_one, t, n_sp, normed, deps)

    partner, one, twos = plane.gather_first(x)
    normed = norm_next(None, x, 0)
    normed = norm_next(normed, partner, half)
    one = held(one, (normed, joint_blocks[1:3], gate_up_cols, cot))
    one_other, two_others, threes = plane.gather_second(one, twos)
    normed = norm_next(normed, one, 1)
    for n, two in enumerate(twos):
        normed = norm_next(normed, two, 2 + 2 * n)
    normed = norm_next(normed, one_other, half + 1)
    for n, two in enumerate(two_others):
        normed = norm_next(normed, two, half + 2 + 2 * n)
    threes = [held(three, (normed, joint_mine, bias)) if n == 0 else three for n, three in enumerate(threes)]
    for n, three in enumerate(threes):
        normed = norm_next(normed, three, 3 + 2 * n)
    for n, three in enumerate(plane.gather_third(threes)):
        normed = norm_next(normed, three, half + 3 + 2 * n)
    tables = rotary_columns(length, group)
    heads = joint_projection(order, normed, joint_mine, bias, tables, span, groups)

    out_full = lax.all_gather(held(out_rows, threes), "sp", axis=0, tiled=True)
    down = lax.all_gather(held(down_rows, threes), "fsdp", axis=0, tiled=True)
    gate_up_blocks = [held(swap_sp(held(gate_up_cols, threes)).reshape(n_sp * depth, 2 * ff), heads[0])]
    gate_up_blocks.append(lax.ppermute(gate_up_blocks[0], "fsdp", ring))
    cot = held(cot, gate_up_blocks[0])
    cot_partner, cot_one, cot_twos = plane.gather_first(cot)
    results = [attend(*heads[:3])]
    cot_one = held(cot_one, results[0][1])
    gate_up_blocks[1] = held(gate_up_blocks[1], results[0][1])
    gate_up_blocks.append(lax.ppermute(gate_up_blocks[1], "fsdp", ring))
    cot_one_other, cot_two_others, cot_threes = plane.gather_second(cot_one, cot_twos)
    for g in range(1, groups):
        results.append(attend(*heads[3 * g : 3 * g + 3], (cot_partner, cot_one, cot_twos, gate_up_blocks[1])))
    gate_up_blocks[2] = held(gate_up_blocks[2], results[-1][1])
    for _ in range(3, n_z):
        gate_up_blocks.append(lax.ppermute(gate_up_blocks[-1], "fsdp", ring))
    cot_three_others = plane.gather_third(cot_threes)
    cot_blocks, cot_partners = [cot, cot_one], [cot_partner, cot_one_other]
    for pieces in zip(cot_twos, cot_threes):
        cot_blocks += pieces
    for pieces in zip(cot_two_others, cot_three_others):
        cot_partners += pieces
    gate_up = in_line(gate_up_blocks, my_z)
    results[-1] = (held(results[-1][0], cot_threes), results[-1][1])
    attended = [swap_sp(o).reshape(n_sp, span, group) for o, _ in results]
    middle, normed_two, normed_again, attended_all = middle_of(
        attended, out_full, depth, x, gain_two, shift_two, (gate_up, down)
    )

    feed = None

    def feed_next(feed, pair, t, deps=()):
        return feed_block(pair, (cot_blocks[t], cot_partners[t]), gate_up, down, t, half, feed, deps)

    partner = plane.send(normed_two, plane.core)
    one = plane.send(normed_two, plane.first)
    feed = feed_next(None, (normed_two, partner), 0)
    one = held(one, feed[0])
    one_other = plane.send(one, plane.core)
    again = held(normed_again, one)
    for n, perm in enumerate(plane.later):
        two = plane.send(again, perm)
        if n == 0:
            feed = feed_next(feed, (one, one_other), 1, again)
        two = held(two, feed[0])
        one = held(one, (two, one_other))
        three = plane.send(one, perm)
        feed = feed_next(feed, (two, plane.send(two, plane.core)), 2 + 2 * n)
        three = held(three, feed[0])
        feed = feed_next(feed, (three, plane.send(three, plane.core)), 3 + 2 * n)
    hidden, gate_up_grad, two_all, cot_all = feed

    two_product = product_of([gate_up_grad], gate_up, NT, span)
    out_product = product_of([hidden], down, NN, span)
    two_far, two_theirs = plane.reduce_sums(two_product, (), True)
    further, nearer = plane.legs(two_far)
    down_sum = dot(hidden, held(cot_all, two_far), TN).astype(bf16)
    two_one, two_last = plane.legs_next(two_product, further, two_theirs, down_sum)
    gate_up_sum = dot(held(two_all, two_one), gate_up_grad, TN).astype(bf16)
    down_part = lax.psum_scatter(held(down_sum, two_one), "fsdp", scatter_dimension=0, tiled=True)
    two_grad = plane.legs_own(two_product, nearer, two_theirs, two_last, gate_up_sum)
    gate_up_part = lax.psum_scatter(held(gate_up_sum, two_grad), "fsdp", scatter_dimension=0, tiled=True)
    middle_grad, two_sums, branch_grad, *parts = norm_back(
        two_grad, middle, gain_two, cot, out_full, depth, n_sp, groups
    )
    dos = [swap_sp(part).reshape(n_sp * span, group) for part in parts]
    out_sum = dot(attended_all, branch_grad, TN).astype(bf16).reshape(n_sp, n_z * depth, D)

    out_sums, out_theirs = plane.reduce_sums(out_product, branch_grad)
    out_got = plane.reduce_leg(out_sums)
    rows = attend_back(place, *heads[:3], dos[0], *results[0], tables, span, out_sums)
    joint_rows = [rows]
    joint_sums = [dot(normed, rows, TN).astype(bf16)]
    joint_parts = [lax.psum_scatter(joint_sums[0], "fsdp", scatter_dimension=0, tiled=True)]
    out_one, out_last = plane.reduce_next(out_product, out_got, out_theirs)
    out_weight_part = parts_of(out_sum, order)
    weight_sums, weight_theirs = plane.reduce_sums(out_weight_part)
    weight_got = plane.reduce_leg(weight_sums)
    gate_up_own = swap_sp(gate_up_part)
    for g in range(1, groups):
        deps = (joint_sums, out_one, weight_sums, weight_theirs)
        rows = attend_back(place, *heads[3 * g : 3 * g + 3], dos[g], *results[g], tables, span, deps)
        joint_rows.append(rows)
    _, weight_last = plane.reduce_next(out_weight_part, weight_got, weight_theirs)

    normed_product = product_of(joint_rows, joint_mine, NT, span)
    normed_far, normed_theirs = plane.reduce_sums(normed_product, (out_last, weight_got, joint_parts, down_part, gate_up_own), True)
    further, nearer = plane.legs(normed_far)
    last_normed = held(normed, (normed_far, joint_sums))
    for g in range(1, groups):
        joint_sums.append(dot(last_normed, joint_rows[g], TN).astype(bf16))
        joint_parts.append(lax.psum_scatter(joint_sums[g], "fsdp", scatter_dimension=0, tiled=True))
    normed_one, normed_last = plane.legs_next(
        normed_product, further, normed_theirs, joint_sums
    )
    output = (middle + plane.reduce_own(out_product, out_got, out_theirs, out_last, f32)).astype(bf16)
    out_own = plane.reduce_own(out_weight_part, weight_got, weight_theirs, weight_last)
    out_grad = lax.psum_scatter(held(out_own, joint_parts), "fsdp", scatter_dimension=0, tiled=True).astype(f32)
    down_grad = down_part[:ff_rows].astype(f32)
    gate_grad, up_grad = join_feed(gate_up_own.reshape(n_sp, depth, 2 * ff), n_z, ff_rows, ff_pad)
    bias_sum = jnp.stack([jnp.sum(r.astype(f32), axis=0).reshape(3, group) for r in joint_rows], 1)
    bias_sum = bias_sum.reshape(3, 1, width)
    bias_sum = lax.dynamic_update_slice(jnp.zeros((3, n_sp, width), f32), bias_sum, (0, me, 0))
    joint_own = jnp.concatenate(joint_parts, axis=1)
    joint_own = swap_sp(joint_own).reshape(n_sp, depth, 3 * width)
    fill = (output, out_own, gate_grad, up_grad, bias_sum)
    normed_grad = plane.legs_own(normed_product, nearer, normed_theirs, normed_last, fill)
    joint_grad = join_joint(held(joint_own, normed_grad), groups)
    tokens_grad, one_sums = norm_back(normed_grad, x, gain_one, middle_grad, deps=joint_grad)
    tokens_grad = tokens_grad.reshape(tokens.shape)

    sums = [one_sums[0], one_sums[1], two_sums[0], two_sums[1]]
    sums = jnp.concatenate([s.reshape(n_all, n_gain) for s in sums] + [bias_sum.reshape(n_all, -1)], axis=1)
    sums = jnp.sum(lax.all_to_all(sums, ("fsdp", "sp"), split_axis=0, concat_axis=0, tiled=True), axis=0)
    gain_one_grad, shift_one_grad, gain_two_grad, shift_two_grad = (
        sums[i * n_gain : (i + 1) * n_gain] for i in range(4)
    )
    return (
        output.reshape(tokens.shape),
        tokens_grad,
        gain_one_grad,
        shift_one_grad,
        joint_grad,
        sums[4 * n_gain :],
        out_grad,
        gain_two_grad,
        shift_two_grad,
        gate_grad,
        up_grad,
        down_grad,
    )


def solution(mesh):
    rows = P("fsdp", "sp", None)
    vector = P(("fsdp", "sp"))
    matrix = P(("fsdp", "sp"), None)
    return jax.shard_map(
        per_device,
        mesh=mesh,
        in_specs=(rows, rows, vector, vector, matrix, vector, matrix, vector, vector, matrix, matrix, matrix),
        out_specs=(rows, rows, vector, vector, matrix, vector, matrix, vector, vector, matrix, matrix, matrix),
        check_vma=False,
    )
```
